32 devices in a mesh: spec: 4 (over y, x), tile: 8 (over z, core).
Axes of the slice: x: 2, y: 2, z: 4, core: 2. Of those that a mesh axis runs over, the one named last changes fastest.
Arguments:
- action: bfloat16 [128, 3072, 256], P('tile', 'spec'), may hold values from 0.099609375 to 2
- east_current: float32 [128, 256], P('tile'), may hold values from -0.4 to 0.4
- north_current: float32 [128, 256], P('tile'), may hold values from -0.4 to 0.4
- sea_mask: int32 [128, 256], P('tile'), may hold values from 0 to 1, as said below
- pattern: int32 [48, 24], replicated, may hold values from 0 to 47, as said below
- table: bfloat16 [48, 64, 64], replicated, may hold values from -0.15625 to 0.15625
Outputs:
- updated: bfloat16 [128, 3072, 256], P('tile', 'spec')
The draws below stay inside these ranges and needn't reach their ends.
Inputs may be any that keep to these rules, and one draw needn't show every extreme that they name: `sea_mask`: each tile of 16 latitude rows (all 256 longitudes) holds at most 2048 sea points, and in every draw some tile holds exactly 2048. `pattern`: each row names 24 different direction blocks.
All inputs are finite; a program needn't handle non-finite values.
Results may differ from the reference program's by a relative error of at most 0.0043.
Values may be sent and summed in bfloat16 or wider, within the bound.
No kernel may reach another device: no remote copies, remote signals or barrier semaphores. Data moves between devices by JAX's collectives and lax.ppermute only.
A program may use at most 128 MiB of HBM per device.

```python
import math
import jax
import jax.numpy as jnp
from jax import lax

NF = 64
ND = 48
K = 3072
R = 24
SUB = 2
ROWS = 16
LON = 256
LAT = 128
SEA_TILE = 2048


def draw_sea_mask(key, part):
    tile_count = LAT // ROWS
    tile_cells = ROWS * LON
    first_key, second_key, third_key = jax.random.split(key, 3)
    counts = jax.random.randint(first_key, (tile_count,), SEA_TILE // 2, SEA_TILE + 1)
    fullest = jax.random.randint(second_key, (), 0, tile_count)
    counts = jnp.where(jnp.arange(tile_count) == fullest, SEA_TILE, counts)
    tile_keys = jax.random.split(third_key, tile_count)
    ranks = jax.vmap(lambda tile_key: jax.random.permutation(tile_key, tile_cells))(tile_keys)
    sea_cells = (ranks < counts[:, None]).astype(jnp.int32)
    return sea_cells.reshape(LAT, LON)


def draw_pattern(key, part):
    row_keys = jax.random.split(jax.random.fold_in(key, 7), ND)
    chosen = jax.vmap(lambda row_key: jax.random.permutation(row_key, ND)[:R])(row_keys)
    return chosen.astype(jnp.int32)


def level_of(stream_key, dims, shards, low, high):
    loudness = 1.0
    for axis_at, blocks in shards:
        draws = jax.random.uniform(jax.random.fold_in(jax.random.fold_in(stream_key, 6), axis_at), (blocks,), jnp.float32, low / len(shards), high / len(shards))
        loudness = loudness * jnp.repeat(jnp.exp(draws), dims[axis_at] // blocks).reshape((-1,) + (1,) * (len(dims) - 1 - axis_at))
    return loudness


def gaussian(key, dims, deviation, reach, kind=jnp.bfloat16):
    drawn = deviation * jax.random.normal(key, dims, jnp.float32)
    return jnp.clip(drawn, min=-reach, max=reach).astype(kind)


def setup_inputs(seed: int = 0) -> dict:
    splits = jax.random.split(jax.random.key(seed), 7)
    action = jnp.clip(jnp.exp(math.log(2.0) - 2.9996462 * jax.random.uniform(splits[0], (LAT, K, LON), jnp.float32) ** level_of(splits[0], (LAT, K, LON), ((0, 8), (1, 4)), -0.2, 0.2)), 0.099609375, 2.0).astype(jnp.bfloat16)
    east_current = jnp.clip(jax.random.uniform(splits[1], (LAT, LON), jnp.float32, -0.4, 0.4) * level_of(splits[1], (LAT, LON), ((0, 8),), -0.4, 0.0), -0.4, 0.4)
    north_current = jnp.clip(jax.random.uniform(splits[2], (LAT, LON), jnp.float32, -0.4, 0.4) * level_of(splits[2], (LAT, LON), ((0, 8),), -0.4, 0.0), -0.4, 0.4)
    sea_mask = draw_sea_mask(jax.random.fold_in(splits[6], 71), 0)
    pattern = draw_pattern(jax.random.fold_in(splits[6], 71), 0)
    table = gaussian(splits[5], (ND, NF, NF), (R * NF) ** -0.5, 0.15625)
    return {"action": action, "east_current": east_current, "north_current": north_current, "sea_mask": sea_mask, "pattern": pattern, "table": table}


courant_scale = 0.45


def upwind(padded, courant_east, courant_north):
    center = padded[1:-1]
    south_row = padded[:-2]
    north_row = padded[2:]
    zero_column = jnp.zeros_like(center[:, :, :1])
    west_cell = jnp.concatenate([zero_column, center[:, :, :-1]], axis=2)
    east_cell = jnp.concatenate([center[:, :, 1:], zero_column], axis=2)
    return (center
            - jnp.maximum(courant_east, 0.0) * (center - west_cell)
            - jnp.minimum(courant_east, 0.0) * (east_cell - center)
            - jnp.maximum(courant_north, 0.0) * (center - south_row)
            - jnp.minimum(courant_north, 0.0) * (north_row - center))


def reference(action, east_current, north_current, sea_mask, pattern, table):
    speed = jnp.exp(-2.0 * jnp.arange(NF, dtype=jnp.float32) / (NF - 1))

    def propagate(direction):
        block = lax.dynamic_slice_in_dim(action, direction * NF, NF, 1).astype(jnp.float32)
        theta = 2.0 * jnp.pi * direction.astype(jnp.float32) / ND
        courant_east = courant_scale * (speed[None, :, None] * jnp.cos(theta) + east_current[:, None, :])
        courant_north = courant_scale * (speed[None, :, None] * jnp.sin(theta) + north_current[:, None, :])
        for substep in range(SUB):
            padded = jnp.pad(block, ((1, 1), (0, 0), (0, 0)))
            block = upwind(padded, courant_east, courant_north)
        return jnp.transpose(block.astype(jnp.bfloat16), (1, 0, 2))

    moved = lax.map(propagate, jnp.arange(ND, dtype=jnp.int32))
    cell_count = LAT * LON
    flat = moved.reshape(ND, NF, cell_count)
    offsets = (pattern - jnp.arange(ND, dtype=jnp.int32)[:, None]) % ND
    weights = table[offsets].astype(jnp.float32)
    mask_flat = sea_mask.reshape(cell_count)
    block_cells = math.gcd(cell_count, 512)

    def source(start):
        piece = lax.dynamic_slice_in_dim(flat, start, block_cells, 2)
        gathered = piece[pattern].astype(jnp.float32)
        coupled = jnp.einsum('rjab,rjbc->rac', weights, gathered)
        own_action = piece.astype(jnp.float32)
        sea_part = lax.dynamic_slice_in_dim(mask_flat, start, block_cells, 0).astype(jnp.float32)
        return (own_action + sea_part[None, None, :] * own_action * coupled).astype(jnp.bfloat16)

    starts = jnp.arange(cell_count // block_cells, dtype=jnp.int32) * block_cells
    blocks_out = lax.map(source, starts)
    result = jnp.moveaxis(blocks_out, 0, 2).reshape(ND * NF, LAT, LON)
    return jnp.transpose(result, (1, 0, 2))
```

```python
import functools

import jax
import jax.numpy as jnp
from jax import lax
from jax.experimental import pallas as pl
from jax.experimental.pallas import tpu as pltpu
from jax.sharding import PartitionSpec as P

NF = 64
ND = 48
SEA = 2048
WINDOW = 512
STEP = 256
SUBK = 16
courant_scale = 0.45
VMEM_LIMIT = 48 * 1024 * 1024


def split_directions(count, sizes):
    if sum(sizes) == count:
        return sizes
    return (1,) * count


def offsets_of(sizes):
    return [sum(sizes[:i]) for i in range(len(sizes))]


def propagate_kernel(rows, peers, share, meta, act, low, high, ae_ref, an_ref, be_ref, bn_ref, slot_t, *rest):
    moved = rest[-(peers + 3)]
    outs = rest[-(peers + 2):-2]
    onehot, packed = rest[-2:]
    lon = act.shape[2]
    depth = act.shape[1]

    @pl.when(pl.program_id(0) == 0)
    def build():
        lanes = lax.broadcasted_iota(jnp.int32, (lon, WINDOW), 1)
        for r in range(rows):
            hit = (slot_t[:, r:r + 1] - meta[3 + r]) == lanes
            onehot[r] = jnp.where(hit, 1.0, 0.0).astype(jnp.bfloat16)

    lane = lax.broadcasted_iota(jnp.int32, (SUBK, lon), 1)
    first = lane == 0
    last = lane == lon - 1

    def group(i, carry):
        ks = pl.ds(pl.multiple_of(i * SUBK, SUBK), SUBK)
        ae = jnp.concatenate([ae_ref[ks, :]] * (lon // 128), axis=1)
        an = jnp.concatenate([an_ref[ks, :]] * (lon // 128), axis=1)

        def load(r):
            if r < 0:
                block = low[r + 2, ks, :]
            elif r < rows:
                block = act[r, ks, :]
            else:
                block = high[r - rows, ks, :]
            return block.astype(jnp.float32)

        def advance(center, south, north, ce, cn):
            west = jnp.where(first, 0.0, pltpu.roll(center, 1, 1))
            east = jnp.where(last, 0.0, pltpu.roll(center, lon - 1, 1))
            along = jnp.where(ce > 0.0, west, east)
            across = jnp.where(cn > 0.0, south, north)
            return center - jnp.abs(ce) * (center - along) - jnp.abs(cn) * (center - across)

        below, here = load(-2), load(-1)
        once = {}
        courant = {}
        for r in range(-1, rows + 1):
            above = load(r + 1)
            ce = ae + be_ref[r + 1:r + 2, :]
            cn = an + bn_ref[r + 1:r + 2, :]
            value = advance(here, below, above, ce, cn)
            if r == -1:
                value = jnp.where(meta[1] > 0, value, 0.0)
            if r == rows:
                value = jnp.where(meta[2] > 0, value, 0.0)
            once[r] = value
            courant[r] = (ce, cn)
            if r >= 1:
                twice = advance(once[r - 1], once[r - 2], once[r], *courant[r - 1])
                moved[r - 1, ks, :] = twice.astype(jnp.bfloat16)
            below, here = here, above
        return carry

    lax.fori_loop(0, depth // SUBK, group, 0)

    packed[...] = jnp.zeros_like(packed)
    for r in range(rows):
        window = pl.ds(pl.multiple_of(meta[3 + r], STEP), WINDOW)
        part = jnp.dot(moved[r], onehot[r], preferred_element_type=jnp.float32)
        packed[:, window] += part.astype(jnp.bfloat16)
    me = meta[0]
    for k in range(peers):
        start = pl.multiple_of((me ^ k) * share, 128)
        outs[k][...] = packed[:, pl.ds(start, share)]


def propagate(meta, action, low, high, ae, an, be, bn, slot_t, moved, begin, count, peers):
    rows, comps, lon = action.shape
    share = SEA // peers
    here = lambda s, m: (0, begin + s, 0)
    local = lambda s, m: (0, s, 0)
    flat = lambda s, m: (begin + s, 0)
    whole = lambda s, m: (0, 0)
    in_specs = [
        pl.BlockSpec((rows, NF, lon), here),
        pl.BlockSpec((2, NF, lon), local),
        pl.BlockSpec((2, NF, lon), local),
        pl.BlockSpec((NF, 128), flat),
        pl.BlockSpec((NF, 128), flat),
        pl.BlockSpec((rows + 2, lon), whole),
        pl.BlockSpec((rows + 2, lon), whole),
        pl.BlockSpec((lon, rows), whole),
    ]
    args = [meta, action, low, high, ae, an, be, bn, slot_t]
    aliases = {}
    if moved is not None:
        in_specs.append(pl.BlockSpec(memory_space=pl.ANY))
        aliases = {len(args): 0}
        args.append(moved)
    cells = count * NF * rows * lon
    return pl.pallas_call(
        functools.partial(propagate_kernel, rows, peers, share),
        grid_spec=pltpu.PrefetchScalarGridSpec(
            num_scalar_prefetch=1,
            grid=(count,),
            in_specs=in_specs,
            out_specs=[pl.BlockSpec((rows, NF, lon), here)]
            + [pl.BlockSpec((NF, share), lambda s, m: (s, 0))] * peers,
            scratch_shapes=[
                pltpu.VMEM((rows, lon, WINDOW), jnp.bfloat16),
                pltpu.VMEM((NF, SEA), jnp.bfloat16),
            ],
        ),
        out_shape=[jax.ShapeDtypeStruct(action.shape, jnp.bfloat16)]
        + [jax.ShapeDtypeStruct((count * NF, share), jnp.bfloat16)] * peers,
        input_output_aliases=aliases,
        compiler_params=pltpu.CompilerParams(vmem_limit_bytes=VMEM_LIMIT),
        cost_estimate=pl.CostEstimate(
            flops=cells * 2 * WINDOW, bytes_accessed=cells * 6, transcendentals=0
        ),
        name="propagate",
    )(*args)


def couple_kernel(peers, dirs, begin, size, spots, meta, sel, tt, *rest):
    pieces = rest[:len(spots)]
    outs = rest[len(spots):len(spots) + peers]
    x, w, y, in_sem, out_sem = rest[len(spots) + peers:]
    me = meta[0]
    copies = []
    for i, (k, first) in enumerate(spots):
        depth = pieces[i].shape[0]
        start = pl.multiple_of(((me ^ k) * dirs + first) * NF, NF)
        copies.append(pltpu.make_async_copy(pieces[i], x.at[pl.ds(start, depth), :], in_sem.at[i]))
        copies[-1].start()
    for copy in copies:
        copy.wait()

    def peer(p, carry):
        for d in range(size):
            r = p * dirs + begin + d
            turn = lax.rem(ND - r, ND)
            lanes = pl.ds(pl.multiple_of((turn // 2) * 128, 128), ND * NF)
            keep = jnp.broadcast_to(sel[pl.ds(r, 1), :], (16, ND * NF)).astype(jnp.bfloat16)
            for q in range(NF // 16):
                w[pl.ds(d * NF + q * 16, 16), :] = tt[turn % 2, pl.ds(q * 16, 16), lanes] * keep
        coupled = jnp.dot(w[...], x[...], preferred_element_type=jnp.float32)
        own = x[pl.ds(pl.multiple_of((p * dirs + begin) * NF, NF), size * NF), :].astype(jnp.float32)
        y[p] = (own + own * coupled).astype(jnp.bfloat16)
        return carry

    lax.fori_loop(0, peers, peer, 0)
    copies = []
    for k in range(peers):
        copies.append(pltpu.make_async_copy(y.at[me ^ k], outs[k], out_sem.at[k]))
        copies[-1].start()
    for copy in copies:
        copy.wait()


def couple(meta, sel, tt, pieces, spots, begin, size, peers, dirs):
    share = SEA // peers
    return pl.pallas_call(
        functools.partial(couple_kernel, peers, dirs, begin, size, spots),
        in_specs=[
            pl.BlockSpec(memory_space=pltpu.SMEM),
            pl.BlockSpec(memory_space=pltpu.VMEM),
            pl.BlockSpec(memory_space=pltpu.VMEM),
        ]
        + [pl.BlockSpec(memory_space=pl.ANY)] * len(pieces),
        out_specs=[pl.BlockSpec(memory_space=pl.ANY)] * peers,
        out_shape=[jax.ShapeDtypeStruct((size * NF, share), jnp.bfloat16)] * peers,
        scratch_shapes=[
            pltpu.VMEM((ND * NF, share), jnp.bfloat16),
            pltpu.VMEM((size * NF, ND * NF), jnp.bfloat16),
            pltpu.VMEM((peers, size * NF, share), jnp.bfloat16),
            pltpu.SemaphoreType.DMA((len(pieces),)),
            pltpu.SemaphoreType.DMA((peers,)),
        ],
        compiler_params=pltpu.CompilerParams(vmem_limit_bytes=VMEM_LIMIT),
        cost_estimate=pl.CostEstimate(
            flops=2 * peers * size * NF * ND * NF * share,
            bytes_accessed=2 * (ND * NF + peers * size * NF) * share,
            transcendentals=0,
        ),
        name="couple",
    )(meta, sel, tt, *pieces)


def finish_kernel(peers, share, group, meta, slot, moved, *rest):
    pieces = rest[:peers]
    out, renewed, sem = rest[peers:]
    me = meta[0]

    @pl.when(pl.program_id(0) == 0)
    def fetch():
        copies = []
        for k in range(peers):
            start = pl.multiple_of((me ^ k) * share, 128)
            copies.append(pltpu.make_async_copy(pieces[k], renewed.at[:, pl.ds(start, share)], sem.at[k]))
            copies[-1].start()
        for copy in copies:
            copy.wait()

    lon = moved.shape[2]
    spots = lax.broadcasted_iota(jnp.int32, (WINDOW, lon), 0)
    for i in range(group):
        r = pl.program_id(0) * group + i
        base = pl.multiple_of(meta[3 + r], STEP)
        cells = slot[pl.ds(r, 1), :]
        hit = (cells - base) == spots
        onehot = jnp.where(hit, 1.0, 0.0).astype(jnp.bfloat16)
        spread = jnp.dot(renewed[:, pl.ds(base, WINDOW)], onehot, preferred_element_type=jnp.float32)
        out[i] = jnp.where(cells >= 0, spread, moved[i].astype(jnp.float32)).astype(jnp.bfloat16)


def finish(meta, slot, moved, pieces, which, size, peers):
    rows, comps, lon = moved.shape
    share = SEA // peers
    group = 4
    block = pl.BlockSpec((group, size * NF, lon), lambda s, m: (s, which, 0))
    return pl.pallas_call(
        functools.partial(finish_kernel, peers, share, group),
        grid_spec=pltpu.PrefetchScalarGridSpec(
            num_scalar_prefetch=1,
            grid=(rows // group,),
            in_specs=[pl.BlockSpec((rows, lon), lambda s, m: (0, 0)), block]
            + [pl.BlockSpec(memory_space=pl.ANY)] * peers,
            out_specs=block,
            scratch_shapes=[
                pltpu.VMEM((size * NF, SEA), jnp.bfloat16),
                pltpu.SemaphoreType.DMA((peers,)),
            ],
        ),
        out_shape=jax.ShapeDtypeStruct(moved.shape, jnp.bfloat16),
        input_output_aliases={2: 0},
        compiler_params=pltpu.CompilerParams(vmem_limit_bytes=VMEM_LIMIT),
        cost_estimate=pl.CostEstimate(
            flops=2 * rows * size * NF * lon * WINDOW,
            bytes_accessed=4 * rows * size * NF * lon,
            transcendentals=0,
        ),
        name="finish",
    )(meta, slot, moved, *pieces)


def pass_on(array, axis, up):
    count = lax.axis_size(axis)
    if up:
        return lax.ppermute(array, axis, [(i, i + 1) for i in range(count - 1)])
    return lax.ppermute(array, axis, [(i + 1, i) for i in range(count - 1)])


def local(action, east_current, north_current, sea_mask, pattern, table):
    rows, comps, lon = action.shape
    peers = lax.axis_size("spec")
    me = lax.axis_index("spec")
    tile = lax.axis_index("tile")
    tiles = lax.axis_size("tile")
    dirs = comps // NF
    parts_out = split_directions(dirs, (1, 2, 3, 6))
    parts_back = split_directions(dirs, (3, 3, 3, 3))

    currents = jnp.stack([east_current, north_current]) * courant_scale
    low_current = pass_on(currents[:, rows - 1:, :], "tile", True)
    high_current = pass_on(currents[:, :1, :], "tile", False)
    halos = []
    for begin, count in zip(offsets_of(parts_out), parts_out):
        part = slice(begin * NF, (begin + count) * NF)
        halos.append((
            pass_on(action[rows - 2:, part, :], "tile", True),
            pass_on(action[:2, part, :], "tile", False),
        ))
    wide = jnp.concatenate([low_current, currents, high_current], axis=1)
    be, bn = wide[0], wide[1]

    components = me * comps + jnp.arange(comps, dtype=jnp.int32)
    direction = (components // NF).astype(jnp.float32)
    frequency = (components % NF).astype(jnp.float32)
    speed = courant_scale * jnp.exp(-2.0 * frequency / (NF - 1))
    theta = 2.0 * jnp.pi * direction / ND
    ae = jnp.broadcast_to((speed * jnp.cos(theta))[:, None], (comps, 128))
    an = jnp.broadcast_to((speed * jnp.sin(theta))[:, None], (comps, 128))

    sea = sea_mask > 0
    before = jnp.dot(
        sea.astype(jnp.bfloat16),
        jnp.triu(jnp.ones((lon, lon), jnp.bfloat16), 1),
        preferred_element_type=jnp.float32,
    )
    totals = jnp.sum(sea.astype(jnp.float32), axis=1)
    starts = jnp.sum(
        jnp.where(jnp.tril(jnp.ones((rows, rows), jnp.bool_), -1), totals[None, :], 0.0), axis=1
    )
    slot = jnp.where(sea, (before + starts[:, None]).astype(jnp.int32), -1)
    bases = jnp.minimum(starts.astype(jnp.int32) // STEP * STEP, SEA - WINDOW)
    meta = jnp.concatenate([
        jnp.stack([me, (tile > 0).astype(jnp.int32), (tile < tiles - 1).astype(jnp.int32)]),
        bases,
    ]).astype(jnp.int32)
    slot_t = slot.T

    chosen = jnp.any(pattern[:, :, None] == jnp.arange(ND, dtype=jnp.int32), axis=1)
    sel = jnp.repeat(chosen.astype(jnp.float32), NF, axis=1)
    flat = jnp.transpose(table, (1, 0, 2)).reshape(NF, ND * NF)
    twofold = jnp.concatenate([flat, flat], axis=1)
    tt = jnp.stack([twofold, jnp.roll(twofold, -NF, axis=1)])

    moved = None
    pieces, spots = [], []
    for j, (begin, count) in enumerate(zip(offsets_of(parts_out), parts_out)):
        low, high = halos[j]
        moved, *packed = propagate(
            meta, action, low, high, ae, an, be, bn, slot_t, moved, begin, count, peers
        )
        for k in range(peers):
            piece = packed[k]
            if k:
                piece = lax.ppermute(piece, "spec", [(i, i ^ k) for i in range(peers)])
            pieces.append(piece)
            spots.append((k, begin))

    result = moved
    for g, (begin, size) in enumerate(zip(offsets_of(parts_back), parts_back)):
        renewed = couple(meta, sel, tt, pieces, tuple(spots), begin, size, peers, dirs)
        back = [renewed[0]] + [
            lax.ppermute(renewed[k], "spec", [(i, i ^ k) for i in range(peers)])
            for k in range(1, peers)
        ]
        result = finish(meta, slot, result, back, begin // size, size, peers)
    return result


def solution(mesh):
    return jax.shard_map(
        local,
        mesh=mesh,
        in_specs=(
            P("tile", "spec", None),
            P("tile", None),
            P("tile", None),
            P("tile", None),
            P(),
            P(),
        ),
        out_specs=P("tile", "spec", None),
        check_vma=False,
    )
```

```python
import functools

import jax
import jax.numpy as jnp
from jax import lax
from jax.experimental import pallas as pl
from jax.experimental.pallas import tpu as pltpu
from jax.sharding import PartitionSpec as P

NF = 64
ND = 48
SEA = 2048
WINDOW = 512
STEP = 256
SUBK = 16
courant_scale = 0.45
VMEM_LIMIT = 24 * 1024 * 1024


def split_directions(count, sizes):
    if sum(sizes) == count:
        return sizes
    return (1,) * count


def offsets_of(sizes):
    return [sum(sizes[:i]) for i in range(len(sizes))]


def setup_kernel(rows, bases, slot, slot_t, pattern, table, onehot, spread, sel, tt):
    lon = slot.shape[1]
    lanes = lax.broadcasted_iota(jnp.int32, (lon, WINDOW), 1)
    depths = lax.broadcasted_iota(jnp.int32, (WINDOW, lon), 0)
    for r in range(rows):
        base = bases[r]
        onehot[r] = jnp.where(slot_t[:, r:r + 1] - base == lanes, 1.0, 0.0).astype(jnp.bfloat16)
        spread[r] = jnp.where(slot[r:r + 1, :] - base == depths, 1.0, 0.0).astype(jnp.bfloat16)
    columns = [jnp.broadcast_to(pattern[:, j:j + 1], (ND, 128)) for j in range(pattern.shape[1])]
    which = lax.broadcasted_iota(jnp.int32, (ND, 128), 1) // NF
    for t in range(ND * NF // 128):
        target = which + t * (128 // NF)
        hit = columns[0] == target
        for column in columns[1:]:
            hit = hit | (column == target)
        sel[:, t * 128:(t + 1) * 128] = jnp.where(hit, 1.0, 0.0)
    for odd in range(2):
        for t in range(ND // 2):
            pair = jnp.concatenate(
                [table[2 * t + odd].astype(jnp.float32), table[(2 * t + odd + 1) % ND].astype(jnp.float32)],
                axis=1,
            ).astype(jnp.bfloat16)
            tt[odd, :, t * 128:(t + 1) * 128] = pair
            tt[odd, :, ND * NF + t * 128:ND * NF + (t + 1) * 128] = pair


def setup(bases, slot, slot_t, pattern, table):
    rows, lon = slot.shape
    vmem = pl.BlockSpec(memory_space=pltpu.VMEM)
    return pl.pallas_call(
        functools.partial(setup_kernel, rows),
        in_specs=[pl.BlockSpec(memory_space=pltpu.SMEM)] + [vmem] * 4,
        out_specs=[vmem] * 4,
        out_shape=[
            jax.ShapeDtypeStruct((rows, lon, WINDOW), jnp.bfloat16),
            jax.ShapeDtypeStruct((rows, WINDOW, lon), jnp.bfloat16),
            jax.ShapeDtypeStruct((ND, ND * NF), jnp.float32),
            jax.ShapeDtypeStruct((2, NF, 2 * ND * NF), jnp.bfloat16),
        ],
        compiler_params=pltpu.CompilerParams(vmem_limit_bytes=VMEM_LIMIT),
        cost_estimate=pl.CostEstimate(
            flops=8 * 2 ** 20, bytes_accessed=12 * 2 ** 20, transcendentals=0
        ),
        name="setup",
    )(bases, slot, slot_t, pattern, table)


def propagate_kernel(rows, peers, share, meta, act, low, high, ae_ref, an_ref, be_ref, bn_ref, onehot, *rest):
    moved = rest[-(peers + 2)]
    outs = rest[-(peers + 1):-1]
    packed = rest[-1]
    lon = act.shape[2]
    depth = act.shape[1]
    halves = lon // 128
    lane = lax.broadcasted_iota(jnp.int32, (SUBK, 128), 1)
    first = lane == 0
    last = lane == 127

    def group(i, carry):
        ks = pl.ds(pl.multiple_of(i * SUBK, SUBK), SUBK)
        ae = ae_ref[ks, :]
        an = an_ref[ks, :]

        def load(r):
            if r < 0:
                block = low[r + 2, ks, :]
            elif r < rows:
                block = act[r, ks, :]
            else:
                block = high[r - rows, ks, :]
            block = block.astype(jnp.float32)
            return [block[:, h * 128:(h + 1) * 128] for h in range(halves)]

        def parts(r):
            found = []
            for h in range(halves):
                ce = ae + be_ref[r + 1:r + 2, h * 128:(h + 1) * 128]
                cn = an + bn_ref[r + 1:r + 2, h * 128:(h + 1) * 128]
                found.append((ce > 0.0, jnp.abs(ce), cn > 0.0, jnp.abs(cn)))
            return found

        def advance(center, south, north, courant):
            right = [pltpu.roll(c, 1, 1) for c in center]
            left = [pltpu.roll(c, 127, 1) for c in center]
            result = []
            for h in range(halves):
                eastward, ce, northward, cn = courant[h]
                west = jnp.where(first, right[h - 1] if h else 0.0, right[h])
                east = jnp.where(last, left[h + 1] if h < halves - 1 else 0.0, left[h])
                along = jnp.where(eastward, west, east)
                across = jnp.where(northward, south[h], north[h])
                c = center[h]
                result.append(c - ce * (c - along) - cn * (c - across))
            return result

        below, here = load(-2), load(-1)
        once = {}
        courant = {}
        for r in range(-1, rows + 1):
            above = load(r + 1)
            courant[r] = parts(r)
            value = advance(here, below, above, courant[r])
            if r == -1:
                value = [jnp.where(meta[1] > 0, v, 0.0) for v in value]
            if r == rows:
                value = [jnp.where(meta[2] > 0, v, 0.0) for v in value]
            once[r] = value
            if r >= 1:
                twice = advance(once[r - 1], once[r - 2], once[r], courant[r - 1])
                for h in range(halves):
                    moved[r - 1, ks, h * 128:(h + 1) * 128] = twice[h].astype(jnp.bfloat16)
            below, here = here, above
        return carry

    lax.fori_loop(0, depth // SUBK, group, 0)

    packed[...] = jnp.zeros_like(packed)
    for r in range(rows):
        window = pl.ds(pl.multiple_of(meta[3 + r], STEP), WINDOW)
        part = jnp.dot(moved[r], onehot[r], preferred_element_type=jnp.float32)
        packed[:, window] += part.astype(jnp.bfloat16)
    me = meta[0]
    for k in range(peers):
        start = pl.multiple_of((me ^ k) * share, 128)
        outs[k][...] = packed[:, pl.ds(start, share)]


def propagate(meta, action, low, high, ae, an, be, bn, onehot, moved, begin, count, peers):
    rows, comps, lon = action.shape
    share = SEA // peers
    which = begin // count
    depth = count * NF
    here = lambda s, m: (0, which, 0)
    vmem = pl.BlockSpec(memory_space=pltpu.VMEM)
    in_specs = [
        pl.BlockSpec((rows, depth, lon), here),
        pl.BlockSpec((2, depth, lon), here),
        pl.BlockSpec((2, depth, lon), here),
        pl.BlockSpec((depth, 128), lambda s, m: (which, 0)),
        pl.BlockSpec((depth, 128), lambda s, m: (which, 0)),
        vmem,
        vmem,
        vmem,
    ]
    args = [meta, action, low, high, ae, an, be, bn, onehot]
    aliases = {}
    if moved is not None:
        in_specs.append(pl.BlockSpec(memory_space=pl.ANY))
        aliases = {len(args): 0}
        args.append(moved)
    cells = depth * rows * lon
    return pl.pallas_call(
        functools.partial(propagate_kernel, rows, peers, share),
        grid_spec=pltpu.PrefetchScalarGridSpec(
            num_scalar_prefetch=1,
            grid=(1,),
            in_specs=in_specs,
            out_specs=[pl.BlockSpec((rows, depth, lon), here)] + [vmem] * peers,
            scratch_shapes=[pltpu.VMEM((depth, SEA), jnp.bfloat16)],
        ),
        out_shape=[jax.ShapeDtypeStruct(action.shape, jnp.bfloat16)]
        + [jax.ShapeDtypeStruct((depth, share), jnp.bfloat16)] * peers,
        input_output_aliases=aliases,
        compiler_params=pltpu.CompilerParams(vmem_limit_bytes=VMEM_LIMIT),
        cost_estimate=pl.CostEstimate(
            flops=cells * 2 * WINDOW, bytes_accessed=cells * 6, transcendentals=0
        ),
        name="propagate",
    )(*args)


def couple_kernel(peers, dirs, begin, size, spots, meta, sel, tt, *rest):
    pieces = rest[:len(spots)]
    outs = rest[len(spots):len(spots) + peers]
    x, w, y, in_sem, out_sem = rest[len(spots) + peers:]
    me = meta[0]
    copies = []
    for i, (k, first) in enumerate(spots):
        depth = pieces[i].shape[0]
        start = pl.multiple_of(((me ^ k) * dirs + first) * NF, NF)
        copies.append(pltpu.make_async_copy(pieces[i], x.at[pl.ds(start, depth), :], in_sem.at[i]))
        copies[-1].start()

    def strip(i, carry):
        r = i // size * dirs + begin + i % size
        turn = lax.rem(ND - r, ND)
        lanes = pl.ds(pl.multiple_of((turn // 2) * 128, 128), ND * NF)
        keep = jnp.broadcast_to(sel[pl.ds(r, 1), :], (16, ND * NF)).astype(jnp.bfloat16)
        for q in range(NF // 16):
            w[pl.ds(pl.multiple_of(i * NF + q * 16, 16), 16), :] = tt[turn % 2, pl.ds(q * 16, 16), lanes] * keep
        return carry

    lax.fori_loop(0, peers * size, strip, 0)
    for copy in copies:
        copy.wait()
    coupled = jnp.dot(w[...], x[...], preferred_element_type=jnp.float32)
    for p in range(peers):
        own = x[(p * dirs + begin) * NF:(p * dirs + begin + size) * NF, :].astype(jnp.float32)
        y[p] = (own + own * coupled[p * size * NF:(p + 1) * size * NF]).astype(jnp.bfloat16)
    copies = []
    for k in range(peers):
        copies.append(pltpu.make_async_copy(y.at[me ^ k], outs[k], out_sem.at[k]))
        copies[-1].start()
    for copy in copies:
        copy.wait()


def couple(meta, sel, tt, pieces, spots, begin, size, peers, dirs):
    share = SEA // peers
    return pl.pallas_call(
        functools.partial(couple_kernel, peers, dirs, begin, size, spots),
        in_specs=[
            pl.BlockSpec(memory_space=pltpu.SMEM),
            pl.BlockSpec(memory_space=pltpu.VMEM),
            pl.BlockSpec(memory_space=pltpu.VMEM),
        ]
        + [pl.BlockSpec(memory_space=pl.ANY)] * len(pieces),
        out_specs=[pl.BlockSpec(memory_space=pl.ANY)] * peers,
        out_shape=[jax.ShapeDtypeStruct((size * NF, share), jnp.bfloat16)] * peers,
        scratch_shapes=[
            pltpu.VMEM((ND * NF, share), jnp.bfloat16),
            pltpu.VMEM((peers * size * NF, ND * NF), jnp.bfloat16),
            pltpu.VMEM((peers, size * NF, share), jnp.bfloat16),
            pltpu.SemaphoreType.DMA((len(pieces),)),
            pltpu.SemaphoreType.DMA((peers,)),
        ],
        compiler_params=pltpu.CompilerParams(vmem_limit_bytes=VMEM_LIMIT),
        cost_estimate=pl.CostEstimate(
            flops=2 * peers * size * NF * ND * NF * share,
            bytes_accessed=2 * (ND * NF + peers * size * NF) * share,
            transcendentals=0,
        ),
        name="couple",
    )(meta, sel, tt, *pieces)


def finish_kernel(peers, share, group, meta, slot, spread, moved, *rest):
    pieces = rest[:peers]
    out, renewed, sem = rest[peers:]
    me = meta[0]

    @pl.when(pl.program_id(0) == 0)
    def fetch():
        copies = []
        for k in range(peers):
            start = pl.multiple_of((me ^ k) * share, 128)
            copies.append(pltpu.make_async_copy(pieces[k], renewed.at[:, pl.ds(start, share)], sem.at[k]))
            copies[-1].start()
        for copy in copies:
            copy.wait()

    for i in range(group):
        r = pl.program_id(0) * group + i
        base = pl.multiple_of(meta[3 + r], STEP)
        cells = slot[pl.ds(r, 1), :]
        new = jnp.dot(renewed[:, pl.ds(base, WINDOW)], spread[r], preferred_element_type=jnp.float32)
        out[i] = jnp.where(cells >= 0, new, moved[i].astype(jnp.float32)).astype(jnp.bfloat16)


def finish(meta, slot, spread, moved, pieces, which, size, peers):
    rows, comps, lon = moved.shape
    share = SEA // peers
    group = 4
    block = pl.BlockSpec((group, size * NF, lon), lambda s, m: (s, which, 0))
    return pl.pallas_call(
        functools.partial(finish_kernel, peers, share, group),
        grid_spec=pltpu.PrefetchScalarGridSpec(
            num_scalar_prefetch=1,
            grid=(rows // group,),
            in_specs=[pl.BlockSpec(memory_space=pltpu.VMEM)] * 2 + [block]
            + [pl.BlockSpec(memory_space=pl.ANY)] * peers,
            out_specs=block,
            scratch_shapes=[
                pltpu.VMEM((size * NF, SEA), jnp.bfloat16),
                pltpu.SemaphoreType.DMA((peers,)),
            ],
        ),
        out_shape=jax.ShapeDtypeStruct(moved.shape, jnp.bfloat16),
        input_output_aliases={3: 0},
        compiler_params=pltpu.CompilerParams(vmem_limit_bytes=VMEM_LIMIT),
        cost_estimate=pl.CostEstimate(
            flops=2 * rows * size * NF * lon * WINDOW,
            bytes_accessed=4 * rows * size * NF * lon,
            transcendentals=0,
        ),
        name="finish",
    )(meta, slot, spread, moved, *pieces)


def pass_on(array, axis, up):
    count = lax.axis_size(axis)
    if up:
        return lax.ppermute(array, axis, [(i, i + 1) for i in range(count - 1)])
    return lax.ppermute(array, axis, [(i + 1, i) for i in range(count - 1)])


def local(action, east_current, north_current, sea_mask, pattern, table):
    rows, comps, lon = action.shape
    peers = lax.axis_size("spec")
    me = lax.axis_index("spec")
    tile = lax.axis_index("tile")
    tiles = lax.axis_size("tile")
    dirs = comps // NF
    parts_out = split_directions(dirs, (3, 3, 3, 3))
    parts_back = split_directions(dirs, (3, 3, 3, 3))

    def edge(row):
        pair = jnp.concatenate([east_current[row:row + 1], north_current[row:row + 1]])
        coarse = lax.reduce_precision(pair, 8, 7)
        fine = pair - coarse
        tail = jnp.concatenate([coarse, fine, jnp.zeros((12, lon), jnp.float32)])
        return jnp.broadcast_to(tail.astype(jnp.bfloat16), (2, 16, lon))

    low = pass_on(jnp.concatenate([action[rows - 2:], edge(rows - 1)], axis=1), "tile", True)
    high = pass_on(jnp.concatenate([action[:2], edge(0)], axis=1), "tile", False)
    low_current = low[0, comps:comps + 4].astype(jnp.float32)
    high_current = high[0, comps:comps + 4].astype(jnp.float32)
    be, bn = [
        courant_scale
        * jnp.concatenate([
            low_current[i:i + 1] + low_current[i + 2:i + 3],
            own,
            high_current[i:i + 1] + high_current[i + 2:i + 3],
        ])
        for i, own in enumerate((east_current, north_current))
    ]

    components = me * comps + jnp.arange(comps, dtype=jnp.int32)
    direction = (components // NF).astype(jnp.float32)
    frequency = (components % NF).astype(jnp.float32)
    speed = courant_scale * jnp.exp(-2.0 * frequency / (NF - 1))
    theta = 2.0 * jnp.pi * direction / ND
    ae = jnp.broadcast_to((speed * jnp.cos(theta))[:, None], (comps, 128))
    an = jnp.broadcast_to((speed * jnp.sin(theta))[:, None], (comps, 128))

    sea = sea_mask > 0
    before = jnp.dot(
        sea.astype(jnp.bfloat16),
        jnp.triu(jnp.ones((lon, lon), jnp.bfloat16), 1),
        preferred_element_type=jnp.float32,
    )
    totals = jnp.sum(sea.astype(jnp.float32), axis=1)
    starts = jnp.sum(
        jnp.where(jnp.tril(jnp.ones((rows, rows), jnp.bool_), -1), totals[None, :], 0.0), axis=1
    )
    slot = jnp.where(sea, (before + starts[:, None]).astype(jnp.int32), -1)
    bases = jnp.minimum(starts.astype(jnp.int32) // STEP * STEP, SEA - WINDOW)
    meta = jnp.concatenate([
        jnp.stack([me, (tile > 0).astype(jnp.int32), (tile < tiles - 1).astype(jnp.int32)]),
        bases,
    ]).astype(jnp.int32)
    slot_t = slot.T

    onehot, spread, sel, tt = setup(bases, slot, slot_t, pattern, table)

    moved = None
    pieces, spots = [], []
    for begin, count in zip(offsets_of(parts_out), parts_out):
        moved, *packed = propagate(
            meta, action, low, high, ae, an, be, bn, onehot, moved, begin, count, peers
        )
        for k in range(peers):
            piece = packed[k]
            if k:
                piece = lax.ppermute(piece, "spec", [(i, i ^ k) for i in range(peers)])
            pieces.append(piece)
            spots.append((k, begin))

    result = moved
    for g, (begin, size) in enumerate(zip(offsets_of(parts_back), parts_back)):
        renewed = couple(meta, sel, tt, pieces, tuple(spots), begin, size, peers, dirs)
        back = [renewed[0]] + [
            lax.ppermute(renewed[k], "spec", [(i, i ^ k) for i in range(peers)])
            for k in range(1, peers)
        ]
        result = finish(meta, slot, spread, result, back, begin // size, size, peers)
    return result


def solution(mesh):
    return jax.shard_map(
        local,
        mesh=mesh,
        in_specs=(
            P("tile", "spec", None),
            P("tile", None),
            P("tile", None),
            P("tile", None),
            P(),
            P(),
        ),
        out_specs=P("tile", "spec", None),
        check_vma=False,
    )
```

```python
import functools

import jax
import jax.numpy as jnp
from jax import lax
from jax.experimental import pallas as pl
from jax.experimental.pallas import tpu as pltpu
from jax.sharding import PartitionSpec as P

NF = 64
ND = 48
SEA = 2048
WINDOW = 512
STEP = 256
SUBK = 16
courant_scale = 0.45
VMEM_LIMIT = 24 * 1024 * 1024


def split_directions(count, sizes):
    if sum(sizes) == count:
        return sizes
    return (1,) * count


def offsets_of(sizes):
    return [sum(sizes[:i]) for i in range(len(sizes))]


def cost(us):
    return pl.CostEstimate(
        flops=int(us * 1.15e9), bytes_accessed=int(us * 3e6), transcendentals=0
    )


def params():
    return pltpu.CompilerParams(vmem_limit_bytes=VMEM_LIMIT)


def edge_kernel(depth, act, east, north, up_a, up_b, down_a, down_b, sem):
    rows, comps, lon = act.shape
    targets = ((rows - 2, rows - 1, up_a, up_b), (0, 0, down_a, down_b))
    for first, row, near, far in targets:
        pair = jnp.concatenate([east[row:row + 1, :], north[row:row + 1, :]], axis=0)
        coarse = pair.astype(jnp.bfloat16).astype(jnp.float32)
        tail = jnp.concatenate([coarse, pair - coarse, jnp.zeros((12, lon), jnp.float32)], axis=0)
        near[0, depth:, :] = tail.astype(jnp.bfloat16)
        near[1, depth:, :] = jnp.zeros((16, lon), jnp.bfloat16)
    copies = []
    for i, (first, row, near, far) in enumerate(targets):
        copies.append(pltpu.make_async_copy(
            act.at[first:first + 2, :depth, :], near.at[:, :depth, :], sem.at[2 * i]))
        copies.append(pltpu.make_async_copy(
            act.at[first:first + 2, depth:, :], far, sem.at[2 * i + 1]))
    for copy in copies:
        copy.start()
    for copy in copies:
        copy.wait()


def edges(action, east, north, depth):
    rows, comps, lon = action.shape
    vmem = pl.BlockSpec(memory_space=pltpu.VMEM)
    near = jax.ShapeDtypeStruct((2, depth + 16, lon), jnp.bfloat16)
    far = jax.ShapeDtypeStruct((2, comps - depth, lon), jnp.bfloat16)
    return pl.pallas_call(
        functools.partial(edge_kernel, depth),
        in_specs=[pl.BlockSpec(memory_space=pl.ANY), vmem, vmem],
        out_specs=[vmem] * 4,
        out_shape=[near, far, near, far],
        scratch_shapes=[pltpu.SemaphoreType.DMA((4,))],
        compiler_params=params(),
        cost_estimate=cost(2),
        name="edges",
    )(action, east, north)


def mark_kernel(rows, bases, slot_t, onehot):
    lanes = lax.broadcasted_iota(jnp.int32, onehot.shape[1:], 1)
    for r in range(rows):
        onehot[r] = jnp.where(slot_t[:, r:r + 1] - bases[r] == lanes, 1.0, 0.0).astype(jnp.bfloat16)


def mark(bases, slot_t):
    lon, rows = slot_t.shape
    vmem = pl.BlockSpec(memory_space=pltpu.VMEM)
    return pl.pallas_call(
        functools.partial(mark_kernel, rows),
        in_specs=[pl.BlockSpec(memory_space=pltpu.SMEM), vmem],
        out_specs=vmem,
        out_shape=jax.ShapeDtypeStruct((rows, lon, WINDOW), jnp.bfloat16),
        compiler_params=params(),
        cost_estimate=cost(2),
        name="mark",
    )(bases, slot_t)


def setup_kernel(rows, bases, slot, pattern, table, after, spread, sel, tt):
    lon = slot.shape[1]
    depths = lax.broadcasted_iota(jnp.int32, (WINDOW, lon), 0)
    for r in range(rows):
        spread[r] = jnp.where(slot[r:r + 1, :] - bases[r] == depths, 1.0, 0.0).astype(jnp.bfloat16)
    columns = [jnp.broadcast_to(pattern[:, j:j + 1], (ND, 128)) for j in range(pattern.shape[1])]
    which = lax.broadcasted_iota(jnp.int32, (ND, 128), 1) // NF
    for t in range(ND * NF // 128):
        target = which + t * (128 // NF)
        hit = columns[0] == target
        for column in columns[1:]:
            hit = hit | (column == target)
        sel[:, t * 128:(t + 1) * 128] = jnp.where(hit, 1.0, 0.0)
    for odd in range(2):
        for t in range(ND // 2):
            pair = jnp.concatenate(
                [table[2 * t + odd].astype(jnp.float32), table[(2 * t + odd + 1) % ND].astype(jnp.float32)],
                axis=1,
            ).astype(jnp.bfloat16)
            tt[odd, :, t * 128:(t + 1) * 128] = pair
            tt[odd, :, ND * NF + t * 128:ND * NF + (t + 1) * 128] = pair


def setup(bases, slot, pattern, table, after):
    rows, lon = slot.shape
    vmem = pl.BlockSpec(memory_space=pltpu.VMEM)
    return pl.pallas_call(
        functools.partial(setup_kernel, rows),
        in_specs=[pl.BlockSpec(memory_space=pltpu.SMEM)] + [vmem] * 3 + [pl.BlockSpec(memory_space=pl.ANY)],
        out_specs=[vmem] * 3,
        out_shape=[
            jax.ShapeDtypeStruct((rows, WINDOW, lon), jnp.bfloat16),
            jax.ShapeDtypeStruct((ND, ND * NF), jnp.float32),
            jax.ShapeDtypeStruct((2, NF, 2 * ND * NF), jnp.bfloat16),
        ],
        compiler_params=params(),
        cost_estimate=cost(4),
        name="setup",
    )(bases, slot, pattern, table, after)


def weave_kernel(peers, dirs, begin, size, sel, tt, after, w):
    def strip(i, carry):
        r = i // size * dirs + begin + i % size
        turn = lax.rem(ND - r, ND)
        lanes = pl.ds(pl.multiple_of((turn // 2) * 128, 128), ND * NF)
        keep = jnp.broadcast_to(sel[pl.ds(r, 1), :], (16, ND * NF)).astype(jnp.bfloat16)
        for q in range(NF // 16):
            w[pl.ds(pl.multiple_of(i * NF + q * 16, 16), 16), :] = tt[turn % 2, pl.ds(q * 16, 16), lanes] * keep
        return carry

    lax.fori_loop(0, peers * size, strip, 0)


def weave(sel, tt, after, begin, size, peers, dirs):
    vmem = pl.BlockSpec(memory_space=pltpu.VMEM)
    return pl.pallas_call(
        functools.partial(weave_kernel, peers, dirs, begin, size),
        in_specs=[vmem, vmem, pl.BlockSpec(memory_space=pl.ANY)],
        out_specs=vmem,
        out_shape=jax.ShapeDtypeStruct((peers * size * NF, ND * NF), jnp.bfloat16),
        compiler_params=params(),
        cost_estimate=cost(3),
        name="weave",
    )(sel, tt, after)


def propagate_kernel(rows, peers, share, begin, aliased, meta, act, low, high, low_tail, high_tail,
                     ae_ref, an_ref, east, north, onehot, *rest):
    if aliased:
        rest = rest[1:]
    moved_out = rest[0]
    outs = rest[1:peers + 1]
    block, moved, once, be_ref, bn_ref, packed, in_sem, out_sem = rest[peers + 1:]
    lon = act.shape[2]
    depth = low.shape[1]
    count = depth // NF
    halves = lon // 128
    lane = lax.broadcasted_iota(jnp.int32, (SUBK, 128), 1)
    first = lane == 0
    last = lane == 127

    def bring(i):
        part = pl.ds(pl.multiple_of(i * NF, NF), NF)
        far = pl.ds(pl.multiple_of(begin + i * NF, NF), NF)
        return pltpu.make_async_copy(act.at[:, far, :], block.at[:, part, :], in_sem.at[i])

    def leave(i):
        part = pl.ds(pl.multiple_of(i * NF, NF), NF)
        far = pl.ds(pl.multiple_of(begin + i * NF, NF), NF)
        return pltpu.make_async_copy(moved.at[:, part, :], moved_out.at[:, far, :], out_sem.at[i])

    for i in range(count):
        bring(i).start()
    for n, (own, b_ref) in enumerate(((east, be_ref), (north, bn_ref))):
        for at, tail in ((0, low_tail), (rows + 1, high_tail)):
            ends = tail[0].astype(jnp.float32)
            b_ref[at:at + 1, :] = courant_scale * (ends[n:n + 1, :] + ends[n + 2:n + 3, :])
        b_ref[1:rows + 1, :] = courant_scale * own[...]

    def advance(center, south, north_of, ks, r):
        ae = ae_ref[ks, :]
        an = an_ref[ks, :]
        right = [pltpu.roll(c, 1, 1) for c in center]
        left = [pltpu.roll(c, 127, 1) for c in center]
        result = []
        for h in range(halves):
            ce = ae + be_ref[r + 1:r + 2, h * 128:(h + 1) * 128]
            cn = an + bn_ref[r + 1:r + 2, h * 128:(h + 1) * 128]
            west = jnp.where(first, right[h - 1] if h else 0.0, right[h])
            east_of = jnp.where(last, left[h + 1] if h < halves - 1 else 0.0, left[h])
            along = jnp.where(ce > 0.0, west, east_of)
            across = jnp.where(cn > 0.0, south[h], north_of[h])
            c = center[h]
            result.append(c - jnp.abs(ce) * (c - along) - jnp.abs(cn) * (c - across))
        return result

    def group(g, carry):
        ks = pl.ds(pl.multiple_of(g * SUBK, SUBK), SUBK)

        def halved(value):
            return [value[:, h * 128:(h + 1) * 128] for h in range(halves)]

        def load(r):
            if r < 0:
                value = low[r + 2, ks, :]
            elif r < rows:
                value = block[r, ks, :]
            else:
                value = high[r - rows, ks, :]
            return halved(value.astype(jnp.float32))

        below, here = load(-2), load(-1)
        for r in range(-1, rows + 1):
            above = load(r + 1)
            value = advance(here, below, above, ks, r)
            if r == -1:
                value = [jnp.where(meta[1] > 0, v, 0.0) for v in value]
            if r == rows:
                value = [jnp.where(meta[2] > 0, v, 0.0) for v in value]
            for h in range(halves):
                once[r + 1, :, h * 128:(h + 1) * 128] = value[h]
            below, here = here, above
        below, here = halved(once[0]), halved(once[1])
        for r in range(rows):
            above = halved(once[r + 2])
            value = advance(here, below, above, ks, r)
            for h in range(halves):
                moved[r, ks, h * 128:(h + 1) * 128] = value[h].astype(jnp.bfloat16)
            below, here = here, above
        return carry

    def piece(i, carry):
        bring(i).wait()
        lax.fori_loop(i * (NF // SUBK), (i + 1) * (NF // SUBK), group, 0)
        leave(i).start()
        return carry

    lax.fori_loop(0, count, piece, 0)

    packed[...] = jnp.zeros_like(packed)
    for r in range(rows):
        window = pl.ds(pl.multiple_of(meta[3 + r], STEP), WINDOW)
        part = jnp.dot(moved[r], onehot[r], preferred_element_type=jnp.float32)
        packed[:, window] += part.astype(jnp.bfloat16)
    me = meta[0]
    for k in range(peers):
        start = pl.multiple_of((me ^ k) * share, 128)
        outs[k][...] = packed[:, pl.ds(start, share)]
    for i in range(count):
        leave(i).wait()


def propagate(meta, action, low, high, at, tails, ae, an, east, north, onehot, moved, begin, count, peers):
    rows, comps, lon = action.shape
    share = SEA // peers
    which = begin // count
    depth = count * NF
    vmem = pl.BlockSpec(memory_space=pltpu.VMEM)
    hbm = pl.BlockSpec(memory_space=pl.ANY)
    halo = pl.BlockSpec((2, depth, lon), lambda s, m: (0, at, 0))
    tail = pl.BlockSpec((2, 16, lon), lambda s, m: (0, tails[0].shape[1] // 16 - 1, 0))
    part = pl.BlockSpec((depth, 128), lambda s, m: (which, 0))
    in_specs = [hbm, halo, halo, tail, tail, part, part, vmem, vmem, vmem]
    args = [meta, action, low, high, *tails, ae, an, east, north, onehot]
    aliases = {}
    if moved is not None:
        in_specs.append(hbm)
        aliases = {len(args): 0}
        args.append(moved)
    return pl.pallas_call(
        functools.partial(propagate_kernel, rows, peers, share, begin * NF, moved is not None),
        grid_spec=pltpu.PrefetchScalarGridSpec(
            num_scalar_prefetch=1,
            grid=(1,),
            in_specs=in_specs,
            out_specs=[hbm] + [vmem] * peers,
            scratch_shapes=[
                pltpu.VMEM((rows, depth, lon), jnp.bfloat16),
                pltpu.VMEM((rows, depth, lon), jnp.bfloat16),
                pltpu.VMEM((rows + 2, SUBK, lon), jnp.float32),
                pltpu.VMEM((rows + 2, lon), jnp.float32),
                pltpu.VMEM((rows + 2, lon), jnp.float32),
                pltpu.VMEM((depth, SEA), jnp.bfloat16),
                pltpu.SemaphoreType.DMA((count,)),
                pltpu.SemaphoreType.DMA((count,)),
            ],
        ),
        out_shape=[jax.ShapeDtypeStruct(action.shape, jnp.bfloat16)]
        + [jax.ShapeDtypeStruct((depth, share), jnp.bfloat16)] * peers,
        input_output_aliases=aliases,
        compiler_params=params(),
        cost_estimate=cost(2.5 * count),
        name="propagate",
    )(*args)


def couple_kernel(peers, dirs, begin, size, spots, meta, w, *rest):
    pieces = rest[:len(spots)]
    outs = rest[-(peers + 4):-4]
    x, y, in_sem, out_sem = rest[-4:]
    me = meta[0]
    copies = []
    for i, (k, first) in enumerate(spots):
        depth = pieces[i].shape[0]
        start = pl.multiple_of(((me ^ k) * dirs + first) * NF, NF)
        copies.append(pltpu.make_async_copy(pieces[i], x.at[pl.ds(start, depth), :], in_sem.at[i]))
        copies[-1].start()
    for copy in copies:
        copy.wait()
    coupled = jnp.dot(w[...], x[...], preferred_element_type=jnp.float32)
    for p in range(peers):
        own = x[(p * dirs + begin) * NF:(p * dirs + begin + size) * NF, :].astype(jnp.float32)
        y[p] = (own + own * coupled[p * size * NF:(p + 1) * size * NF]).astype(jnp.bfloat16)
    copies = []
    for k in range(peers):
        copies.append(pltpu.make_async_copy(y.at[me ^ k], outs[k], out_sem.at[k]))
        copies[-1].start()
    for copy in copies:
        copy.wait()


def couple(meta, w, pieces, after, spots, begin, size, peers, dirs):
    share = SEA // peers
    extra = [] if after is None else [after]
    return pl.pallas_call(
        functools.partial(couple_kernel, peers, dirs, begin, size, spots),
        in_specs=[
            pl.BlockSpec(memory_space=pltpu.SMEM),
            pl.BlockSpec(memory_space=pltpu.VMEM),
        ]
        + [pl.BlockSpec(memory_space=pl.ANY)] * (len(pieces) + len(extra)),
        out_specs=[pl.BlockSpec(memory_space=pl.ANY)] * peers,
        out_shape=[jax.ShapeDtypeStruct((size * NF, share), jnp.bfloat16)] * peers,
        scratch_shapes=[
            pltpu.VMEM((ND * NF, share), jnp.bfloat16),
            pltpu.VMEM((peers, size * NF, share), jnp.bfloat16),
            pltpu.SemaphoreType.DMA((len(pieces),)),
            pltpu.SemaphoreType.DMA((peers,)),
        ],
        compiler_params=params(),
        cost_estimate=cost(5),
        name="couple",
    )(meta, w, *pieces, *extra)


def finish_kernel(peers, share, group, meta, slot, spread, moved, *rest):
    pieces = rest[:peers]
    out, renewed, sem = rest[peers:]
    me = meta[0]

    @pl.when(pl.program_id(0) == 0)
    def fetch():
        copies = []
        for k in range(peers):
            start = pl.multiple_of((me ^ k) * share, 128)
            copies.append(pltpu.make_async_copy(pieces[k], renewed.at[:, pl.ds(start, share)], sem.at[k]))
            copies[-1].start()
        for copy in copies:
            copy.wait()

    for i in range(group):
        r = pl.program_id(0) * group + i
        base = pl.multiple_of(meta[3 + r], STEP)
        cells = slot[pl.ds(r, 1), :]
        new = jnp.dot(renewed[:, pl.ds(base, WINDOW)], spread[r], preferred_element_type=jnp.float32)
        out[i] = jnp.where(cells >= 0, new, moved[i].astype(jnp.float32)).astype(jnp.bfloat16)


def finish(meta, slot, spread, moved, pieces, which, size, peers):
    rows, comps, lon = moved.shape
    share = SEA // peers
    group = 4
    block = pl.BlockSpec((group, size * NF, lon), lambda s, m: (s, which, 0))
    return pl.pallas_call(
        functools.partial(finish_kernel, peers, share, group),
        grid_spec=pltpu.PrefetchScalarGridSpec(
            num_scalar_prefetch=1,
            grid=(rows // group,),
            in_specs=[pl.BlockSpec(memory_space=pltpu.VMEM)] * 2 + [block]
            + [pl.BlockSpec(memory_space=pl.ANY)] * peers,
            out_specs=block,
            scratch_shapes=[
                pltpu.VMEM((size * NF, SEA), jnp.bfloat16),
                pltpu.SemaphoreType.DMA((peers,)),
            ],
        ),
        out_shape=jax.ShapeDtypeStruct(moved.shape, jnp.bfloat16),
        input_output_aliases={3: 0},
        compiler_params=params(),
        cost_estimate=cost(5),
        name="finish",
    )(meta, slot, spread, moved, *pieces)


def pass_on(array, axis, up):
    count = lax.axis_size(axis)
    if up:
        return lax.ppermute(array, axis, [(i, i + 1) for i in range(count - 1)])
    return lax.ppermute(array, axis, [(i + 1, i) for i in range(count - 1)])


def local(action, east_current, north_current, sea_mask, pattern, table):
    rows, comps, lon = action.shape
    peers = lax.axis_size("spec")
    me = lax.axis_index("spec")
    tile = lax.axis_index("tile")
    tiles = lax.axis_size("tile")
    dirs = comps // NF
    parts_out = split_directions(dirs, (3, 3, 3, 3))
    parts_back = split_directions(dirs, (3, 3, 3, 3))

    ahead = parts_out[0] * NF
    up_near, up_far, down_near, down_far = edges(action, east_current, north_current, ahead)
    low_near = pass_on(up_near, "tile", True)
    high_near = pass_on(down_near, "tile", False)
    low_far = pass_on(up_far, "tile", True)
    high_far = pass_on(down_far, "tile", False)

    components = me * comps + jnp.arange(comps, dtype=jnp.int32)
    direction = (components // NF).astype(jnp.float32)
    frequency = (components % NF).astype(jnp.float32)
    speed = courant_scale * jnp.exp(-2.0 * frequency / (NF - 1))
    theta = 2.0 * jnp.pi * direction / ND
    ae = jnp.broadcast_to((speed * jnp.cos(theta))[:, None], (comps, 128))
    an = jnp.broadcast_to((speed * jnp.sin(theta))[:, None], (comps, 128))

    sea = sea_mask > 0
    before = jnp.dot(
        sea.astype(jnp.bfloat16),
        jnp.triu(jnp.ones((lon, lon), jnp.bfloat16), 1),
        preferred_element_type=jnp.float32,
    )
    totals = jnp.sum(sea.astype(jnp.float32), axis=1)
    starts = jnp.sum(
        jnp.where(jnp.tril(jnp.ones((rows, rows), jnp.bool_), -1), totals[None, :], 0.0), axis=1
    )
    slot = jnp.where(sea, (before + starts[:, None]).astype(jnp.int32), -1)
    bases = jnp.minimum(starts.astype(jnp.int32) // STEP * STEP, SEA - WINDOW)
    meta = jnp.concatenate([
        jnp.stack([me, (tile > 0).astype(jnp.int32), (tile < tiles - 1).astype(jnp.int32)]),
        bases,
    ]).astype(jnp.int32)
    slot_t = slot.T

    onehot = mark(bases, slot_t)

    moved = None
    pieces, spots = [], []
    for j, (begin, count) in enumerate(zip(offsets_of(parts_out), parts_out)):
        low, high = (low_far, high_far) if j else (low_near, high_near)
        at = (begin - parts_out[0]) // count if j else 0
        moved, *packed = propagate(
            meta, action, low, high, at, (low_near, high_near), ae, an,
            east_current, north_current, onehot, moved, begin, count, peers,
        )
        for k in range(peers):
            piece = packed[k]
            if k:
                piece = lax.ppermute(piece, "spec", [(i, i ^ k) for i in range(peers)])
            pieces.append(piece)
            spots.append((k, begin))

    spread, sel, tt = setup(bases, slot, pattern, table, packed[0])
    woven = [
        weave(sel, tt, packed[0], begin, size, peers, dirs)
        for begin, size in zip(offsets_of(parts_back), parts_back)
    ]
    result = moved
    renewed = [None]
    for g, (begin, size) in enumerate(zip(offsets_of(parts_back), parts_back)):
        renewed = couple(meta, woven[g], pieces, renewed[0], tuple(spots), begin, size, peers, dirs)
        back = [renewed[0]] + [
            lax.ppermute(renewed[k], "spec", [(i, i ^ k) for i in range(peers)])
            for k in range(1, peers)
        ]
        result = finish(meta, slot, spread, result, back, begin // size, size, peers)
    return result


def solution(mesh):
    return jax.shard_map(
        local,
        mesh=mesh,
        in_specs=(
            P("tile", "spec", None),
            P("tile", None),
            P("tile", None),
            P("tile", None),
            P(),
            P(),
        ),
        out_specs=P("tile", "spec", None),
        check_vma=False,
    )
```

```python
import functools

import jax
import jax.numpy as jnp
from jax import lax
from jax.experimental import pallas as pl
from jax.experimental.pallas import tpu as pltpu
from jax.sharding import PartitionSpec as P

NF = 64
ND = 48
SEA = 2048
WINDOW = 512
STEP = 256
SUBK = 16
courant_scale = 0.45
VMEM_LIMIT = 24 * 1024 * 1024


def split_directions(count, sizes):
    if sum(sizes) == count:
        return sizes
    return (1,) * count


def offsets_of(sizes):
    return [sum(sizes[:i]) for i in range(len(sizes))]


def cost(us):
    return pl.CostEstimate(
        flops=int(us * 1.15e9), bytes_accessed=int(us * 3e6), transcendentals=0
    )


def params():
    return pltpu.CompilerParams(vmem_limit_bytes=VMEM_LIMIT)


def edge_kernel(depth, parity, act, east, north, across_near, across_far, beyond_near, beyond_far, ends, sem):
    rows, comps, lon = act.shape
    even = parity[0] == 0
    targets = ((across_near, across_far), (beyond_near, beyond_far))
    copies = []
    for i, (near, far) in enumerate(targets):
        top = even if i == 0 else jnp.logical_not(even)
        first = jnp.where(top, rows - 2, 0)
        copies.append(pltpu.make_async_copy(
            act.at[pl.ds(first, 2), :depth, :], near.at[:, :depth, :], sem.at[2 * i]))
        copies.append(pltpu.make_async_copy(
            act.at[pl.ds(first, 2), depth:, :], far, sem.at[2 * i + 1]))
    for n, current in enumerate((east, north)):
        copies.append(pltpu.make_async_copy(current, ends.at[n], sem.at[4 + n]))
    for copy in reversed(copies):
        copy.start()
    for copy in reversed(copies):
        copy.wait()
    for i, (near, far) in enumerate(targets):
        top = even if i == 0 else jnp.logical_not(even)
        pair = [jnp.where(top, ends[n, rows - 1:rows, :], ends[n, 0:1, :]) for n in range(2)]
        pair = jnp.concatenate(pair, axis=0)
        coarse = pair.astype(jnp.bfloat16).astype(jnp.float32)
        tail = jnp.concatenate([coarse, pair - coarse, jnp.zeros((12, lon), jnp.float32)], axis=0)
        near[0, depth:, :] = tail.astype(jnp.bfloat16)
        near[1, depth:, :] = jnp.zeros((16, lon), jnp.bfloat16)


def edges(parity, action, east, north, depth):
    rows, comps, lon = action.shape
    vmem = pl.BlockSpec(memory_space=pltpu.VMEM)
    hbm = pl.BlockSpec(memory_space=pltpu.HBM)
    near = jax.ShapeDtypeStruct((2, depth + 16, lon), jnp.bfloat16)
    far = jax.ShapeDtypeStruct((2, comps - depth, lon), jnp.bfloat16)
    return pl.pallas_call(
        functools.partial(edge_kernel, depth),
        in_specs=[pl.BlockSpec(memory_space=pltpu.SMEM), hbm, hbm, hbm],
        out_specs=[vmem] * 4,
        out_shape=[near, far, near, far],
        scratch_shapes=[pltpu.VMEM((2, rows, lon), jnp.float32), pltpu.SemaphoreType.DMA((6,))],
        compiler_params=params(),
        cost_estimate=cost(2),
        name="edges",
    )(parity, action, east, north)


def mark_kernel(rows, bases, slot_t, onehot):
    lanes = lax.broadcasted_iota(jnp.int32, onehot.shape[1:], 1)
    for r in range(rows):
        onehot[r] = jnp.where(slot_t[:, r:r + 1] - bases[r] == lanes, 1.0, 0.0).astype(jnp.bfloat16)


def mark(bases, slot_t):
    lon, rows = slot_t.shape
    vmem = pl.BlockSpec(memory_space=pltpu.VMEM)
    return pl.pallas_call(
        functools.partial(mark_kernel, rows),
        in_specs=[pl.BlockSpec(memory_space=pltpu.SMEM), vmem],
        out_specs=vmem,
        out_shape=jax.ShapeDtypeStruct((rows, lon, WINDOW), jnp.bfloat16),
        compiler_params=params(),
        cost_estimate=cost(2),
        name="mark",
    )(bases, slot_t)


def setup_kernel(rows, bases, slot, pattern, table, after, spread, sel, tt):
    lon = slot.shape[1]
    depths = lax.broadcasted_iota(jnp.int32, (WINDOW, lon), 0)
    for r in range(rows):
        spread[r] = jnp.where(slot[r:r + 1, :] - bases[r] == depths, 1.0, 0.0).astype(jnp.bfloat16)
    columns = [jnp.broadcast_to(pattern[:, j:j + 1], (ND, 128)) for j in range(pattern.shape[1])]
    which = lax.broadcasted_iota(jnp.int32, (ND, 128), 1) // NF
    for t in range(ND * NF // 128):
        target = which + t * (128 // NF)
        hit = columns[0] == target
        for column in columns[1:]:
            hit = hit | (column == target)
        sel[:, t * 128:(t + 1) * 128] = jnp.where(hit, 1.0, 0.0)
    for odd in range(2):
        for t in range(ND // 2):
            pair = jnp.concatenate(
                [table[2 * t + odd].astype(jnp.float32), table[(2 * t + odd + 1) % ND].astype(jnp.float32)],
                axis=1,
            ).astype(jnp.bfloat16)
            tt[odd, :, t * 128:(t + 1) * 128] = pair
            tt[odd, :, ND * NF + t * 128:ND * NF + (t + 1) * 128] = pair


def setup(bases, slot, pattern, table, after):
    rows, lon = slot.shape
    vmem = pl.BlockSpec(memory_space=pltpu.VMEM)
    return pl.pallas_call(
        functools.partial(setup_kernel, rows),
        in_specs=[pl.BlockSpec(memory_space=pltpu.SMEM)] + [vmem] * 3 + [pl.BlockSpec(memory_space=pl.ANY)],
        out_specs=[vmem] * 3,
        out_shape=[
            jax.ShapeDtypeStruct((rows, WINDOW, lon), jnp.bfloat16),
            jax.ShapeDtypeStruct((ND, ND * NF), jnp.float32),
            jax.ShapeDtypeStruct((2, NF, 2 * ND * NF), jnp.bfloat16),
        ],
        compiler_params=params(),
        cost_estimate=cost(4),
        name="setup",
    )(bases, slot, pattern, table, after)


def weave_kernel(peers, dirs, begin, size, sel, tt, after, w):
    def strip(i, carry):
        r = i // size * dirs + begin + i % size
        turn = lax.rem(ND - r, ND)
        lanes = pl.ds(pl.multiple_of((turn // 2) * 128, 128), ND * NF)
        keep = jnp.broadcast_to(sel[pl.ds(r, 1), :], (16, ND * NF)).astype(jnp.bfloat16)
        for q in range(NF // 16):
            w[pl.ds(pl.multiple_of(i * NF + q * 16, 16), 16), :] = tt[turn % 2, pl.ds(q * 16, 16), lanes] * keep
        return carry

    lax.fori_loop(0, peers * size, strip, 0)


def weave(sel, tt, after, begin, size, peers, dirs):
    vmem = pl.BlockSpec(memory_space=pltpu.VMEM)
    return pl.pallas_call(
        functools.partial(weave_kernel, peers, dirs, begin, size),
        in_specs=[vmem, vmem, pl.BlockSpec(memory_space=pl.ANY)],
        out_specs=vmem,
        out_shape=jax.ShapeDtypeStruct((peers * size * NF, ND * NF), jnp.bfloat16),
        compiler_params=params(),
        cost_estimate=cost(3),
        name="weave",
    )(sel, tt, after)


def propagate_kernel(rows, peers, share, begin, extra, meta, act, across, beyond, across_tail, beyond_tail,
                     ae_ref, an_ref, east, north, onehot, *rest):
    rest = rest[extra:]
    even = meta[3 + rows] == 0
    moved_out = rest[0]
    outs = rest[1:peers + 1]
    block, moved, once, be_ref, bn_ref, packed, in_sem, out_sem = rest[peers + 1:]
    lon = act.shape[2]
    depth = across.shape[1]
    count = depth // NF
    halves = lon // 128
    lane = lax.broadcasted_iota(jnp.int32, (SUBK, 128), 1)
    first = lane == 0
    last = lane == 127

    def bring(i):
        part = pl.ds(pl.multiple_of(i * NF, NF), NF)
        far = pl.ds(pl.multiple_of(begin + i * NF, NF), NF)
        return pltpu.make_async_copy(act.at[:, far, :], block.at[:, part, :], in_sem.at[i])

    def leave(i):
        part = pl.ds(pl.multiple_of(i * NF, NF), NF)
        far = pl.ds(pl.multiple_of(begin + i * NF, NF), NF)
        return pltpu.make_async_copy(moved.at[:, part, :], moved_out.at[:, far, :], out_sem.at[i])

    for i in range(count):
        bring(i).start()
    for n, (own, b_ref) in enumerate(((east, be_ref), (north, bn_ref))):
        for at, one, other in ((0, beyond_tail, across_tail), (rows + 1, across_tail, beyond_tail)):
            ends = jnp.where(even, one[0].astype(jnp.float32), other[0].astype(jnp.float32))
            b_ref[at:at + 1, :] = courant_scale * (ends[n:n + 1, :] + ends[n + 2:n + 3, :])
        b_ref[1:rows + 1, :] = courant_scale * own[...]

    def advance(center, south, north_of, ks, r):
        ae = ae_ref[ks, :]
        an = an_ref[ks, :]
        right = [pltpu.roll(c, 1, 1) for c in center]
        left = [pltpu.roll(c, 127, 1) for c in center]
        result = []
        for h in range(halves):
            ce = ae + be_ref[r + 1:r + 2, h * 128:(h + 1) * 128]
            cn = an + bn_ref[r + 1:r + 2, h * 128:(h + 1) * 128]
            west = jnp.where(first, right[h - 1] if h else 0.0, right[h])
            east_of = jnp.where(last, left[h + 1] if h < halves - 1 else 0.0, left[h])
            along = jnp.where(ce > 0.0, west, east_of)
            across = jnp.where(cn > 0.0, south[h], north_of[h])
            c = center[h]
            result.append(c - jnp.abs(ce) * (c - along) - jnp.abs(cn) * (c - across))
        return result

    def group(g, carry):
        ks = pl.ds(pl.multiple_of(g * SUBK, SUBK), SUBK)

        def halved(value):
            return [value[:, h * 128:(h + 1) * 128] for h in range(halves)]

        def load(r):
            if 0 <= r < rows:
                return halved(block[r, ks, :].astype(jnp.float32))
            at = r + 2 if r < 0 else r - rows
            one, other = (beyond, across) if r < 0 else (across, beyond)
            return halved(
                jnp.where(even, one[at, ks, :].astype(jnp.float32), other[at, ks, :].astype(jnp.float32))
            )

        below, here = load(-2), load(-1)
        for r in range(-1, rows + 1):
            above = load(r + 1)
            value = advance(here, below, above, ks, r)
            if r == -1:
                value = [jnp.where(meta[1] > 0, v, 0.0) for v in value]
            if r == rows:
                value = [jnp.where(meta[2] > 0, v, 0.0) for v in value]
            for h in range(halves):
                once[r + 1, :, h * 128:(h + 1) * 128] = value[h]
            below, here = here, above
        below, here = halved(once[0]), halved(once[1])
        for r in range(rows):
            above = halved(once[r + 2])
            value = advance(here, below, above, ks, r)
            for h in range(halves):
                moved[r, ks, h * 128:(h + 1) * 128] = value[h].astype(jnp.bfloat16)
            below, here = here, above
        return carry

    def piece(i, carry):
        bring(i).wait()
        lax.fori_loop(i * (NF // SUBK), (i + 1) * (NF // SUBK), group, 0)
        leave(i).start()
        return carry

    lax.fori_loop(0, count, piece, 0)

    packed[...] = jnp.zeros_like(packed)
    for r in range(rows):
        window = pl.ds(pl.multiple_of(meta[3 + r], STEP), WINDOW)
        part = jnp.dot(moved[r], onehot[r], preferred_element_type=jnp.float32)
        packed[:, window] += part.astype(jnp.bfloat16)
    me = meta[0]
    for k in range(peers):
        start = pl.multiple_of((me ^ k) * share, 128)
        outs[k][...] = packed[:, pl.ds(start, share)]
    for i in range(count):
        leave(i).wait()


def propagate(meta, action, halos, at, tails, ae, an, east, north, onehot, moved, after, begin, count, peers):
    rows, comps, lon = action.shape
    share = SEA // peers
    which = begin // count
    depth = count * NF
    vmem = pl.BlockSpec(memory_space=pltpu.VMEM)
    hbm = pl.BlockSpec(memory_space=pltpu.HBM)
    loose = pl.BlockSpec(memory_space=pl.ANY)
    halo = pl.BlockSpec((2, depth, lon), lambda s, m: (0, at, 0))
    tail = pl.BlockSpec((2, 16, lon), lambda s, m: (0, tails[0].shape[1] // 16 - 1, 0))
    part = pl.BlockSpec((depth, 128), lambda s, m: (which, 0))
    in_specs = [hbm, halo, halo, tail, tail, part, part, vmem, vmem, vmem]
    args = [meta, action, *halos, *tails, ae, an, east, north, onehot]
    aliases = {}
    extra = len(after)
    if moved is not None:
        in_specs.append(hbm)
        aliases = {len(args): 0}
        args.append(moved)
        extra += 1
    in_specs += [loose] * len(after)
    args += after
    return pl.pallas_call(
        functools.partial(propagate_kernel, rows, peers, share, begin * NF, extra),
        grid_spec=pltpu.PrefetchScalarGridSpec(
            num_scalar_prefetch=1,
            grid=(1,),
            in_specs=in_specs,
            out_specs=[hbm] + [vmem] * peers,
            scratch_shapes=[
                pltpu.VMEM((rows, depth, lon), jnp.bfloat16),
                pltpu.VMEM((rows, depth, lon), jnp.bfloat16),
                pltpu.VMEM((rows + 2, SUBK, lon), jnp.float32),
                pltpu.VMEM((rows + 2, lon), jnp.float32),
                pltpu.VMEM((rows + 2, lon), jnp.float32),
                pltpu.VMEM((depth, SEA), jnp.bfloat16),
                pltpu.SemaphoreType.DMA((count,)),
                pltpu.SemaphoreType.DMA((count,)),
            ],
        ),
        out_shape=[jax.ShapeDtypeStruct(action.shape, jnp.bfloat16)]
        + [jax.ShapeDtypeStruct((depth, share), jnp.bfloat16)] * peers,
        input_output_aliases=aliases,
        compiler_params=params(),
        cost_estimate=cost(2.5 * count),
        name="propagate",
    )(*args)


def couple_kernel(peers, dirs, begin, size, spots, meta, w, *rest):
    me = meta[0]
    if spots:
        pieces = rest[:len(spots)]
        outs = rest[len(spots):len(spots) + peers]
        x, y, sem = rest[-3:]
        copies = []
        for i, (k, first) in enumerate(spots):
            depth = pieces[i].shape[0]
            start = pl.multiple_of(((me ^ k) * dirs + first) * NF, NF)
            copies.append(pltpu.make_async_copy(pieces[i], x.at[pl.ds(start, depth), :], sem.at[i]))
            copies[-1].start()
        for copy in copies:
            copy.wait()
    else:
        x = rest[0]
        outs = rest[-(peers + 1):-1]
        y = rest[-1]
    coupled = jnp.dot(w[...], x[...], preferred_element_type=jnp.float32)
    for p in range(peers):
        own = x[(p * dirs + begin) * NF:(p * dirs + begin + size) * NF, :].astype(jnp.float32)
        y[p] = (own + own * coupled[p * size * NF:(p + 1) * size * NF]).astype(jnp.bfloat16)
    for k in range(peers):
        outs[k][...] = y[me ^ k]


def couple(meta, w, x, pieces, after, spots, begin, size, peers, dirs):
    share = SEA // peers
    vmem = pl.BlockSpec(memory_space=pltpu.VMEM)
    loose = pl.BlockSpec(memory_space=pl.ANY)
    outs = [jax.ShapeDtypeStruct((size * NF, share), jnp.bfloat16)] * peers
    scratch = [pltpu.VMEM((peers, size * NF, share), jnp.bfloat16)]
    if x is None:
        in_specs, args = [loose] * len(pieces), pieces
        outs = outs + [jax.ShapeDtypeStruct((ND * NF, share), jnp.bfloat16)]
        scratch.append(pltpu.SemaphoreType.DMA((len(pieces),)))
    else:
        in_specs, args, spots = [vmem, loose], [x, after], ()
    result = pl.pallas_call(
        functools.partial(couple_kernel, peers, dirs, begin, size, spots),
        in_specs=[pl.BlockSpec(memory_space=pltpu.SMEM), vmem] + in_specs,
        out_specs=[vmem] * len(outs),
        out_shape=outs,
        scratch_shapes=scratch,
        compiler_params=params(),
        cost_estimate=cost(6),
        name="couple",
    )(meta, w, *args)
    return result[:peers], result[peers] if x is None else x


def finish_kernel(peers, share, begin, group, meta, slot, spread, moved, *rest):
    pieces = rest[:peers]
    out, renewed, old, new, piece_sem, in_sem, out_sem = rest[peers:]
    rows, lon = slot.shape
    depth = renewed.shape[0]
    me = meta[0]
    copies = []
    for k in range(peers):
        start = pl.multiple_of((me ^ k) * share, 128)
        copies.append(pltpu.make_async_copy(pieces[k], renewed.at[:, pl.ds(start, share)], piece_sem.at[k]))
        copies[-1].start()
    far = slice(begin, begin + depth)
    bring, leave = [], []
    for i in range(rows // group):
        part = slice(i * group, (i + 1) * group)
        bring.append(pltpu.make_async_copy(moved.at[part, far, :], old.at[part], in_sem.at[i]))
        leave.append(pltpu.make_async_copy(new.at[part], out.at[part, far, :], out_sem.at[i]))
        bring[-1].start()
    for copy in copies:
        copy.wait()
    for r in range(rows):
        if r % group == 0:
            bring[r // group].wait()
        base = pl.multiple_of(meta[3 + r], STEP)
        value = jnp.dot(renewed[:, pl.ds(base, WINDOW)], spread[r], preferred_element_type=jnp.float32)
        sea = slot[r:r + 1, :] >= 0
        new[r] = jnp.where(sea, value, old[r].astype(jnp.float32)).astype(jnp.bfloat16)
        if r % group == group - 1:
            leave[r // group].start()
    for copy in leave:
        copy.wait()


def finish(meta, slot, spread, moved, pieces, begin, size, peers):
    rows, comps, lon = moved.shape
    share = SEA // peers
    group = 4
    hbm = pl.BlockSpec(memory_space=pltpu.HBM)
    vmem = pl.BlockSpec(memory_space=pltpu.VMEM)
    return pl.pallas_call(
        functools.partial(finish_kernel, peers, share, begin * NF, group),
        in_specs=[pl.BlockSpec(memory_space=pltpu.SMEM), vmem, vmem, hbm]
        + [pl.BlockSpec(memory_space=pl.ANY)] * peers,
        out_specs=hbm,
        out_shape=jax.ShapeDtypeStruct(moved.shape, jnp.bfloat16),
        scratch_shapes=[
            pltpu.VMEM((size * NF, SEA), jnp.bfloat16),
            pltpu.VMEM((rows, size * NF, lon), jnp.bfloat16),
            pltpu.VMEM((rows, size * NF, lon), jnp.bfloat16),
            pltpu.SemaphoreType.DMA((peers,)),
            pltpu.SemaphoreType.DMA((rows // group,)),
            pltpu.SemaphoreType.DMA((rows // group,)),
        ],
        input_output_aliases={3: 0},
        compiler_params=params(),
        cost_estimate=cost(4),
        name="finish",
    )(meta, slot, spread, moved, *pieces)


def swap(array, first):
    count = lax.axis_size("tile")
    pairs = [(i, i + 1) for i in range(first, count - 1, 2)]
    return lax.ppermute(array, "tile", pairs + [(j, i) for i, j in pairs])


def local(action, east_current, north_current, sea_mask, pattern, table):
    rows, comps, lon = action.shape
    peers = lax.axis_size("spec")
    me = lax.axis_index("spec")
    tile = lax.axis_index("tile")
    tiles = lax.axis_size("tile")
    dirs = comps // NF
    parts_out = split_directions(dirs, (3, 3, 3, 3))
    parts_back = split_directions(dirs, (3, 3, 3, 3))

    ahead = parts_out[0] * NF
    parity = (tile % 2).astype(jnp.int32)
    across_near, across_far, beyond_near, beyond_far = edges(
        parity.reshape(1), action, east_current, north_current, ahead
    )
    near = swap(across_near, 0), swap(beyond_near, 1)
    far = swap(across_far, 0), swap(beyond_far, 1)

    components = me * comps + jnp.arange(comps, dtype=jnp.int32)
    direction = (components // NF).astype(jnp.float32)
    frequency = (components % NF).astype(jnp.float32)
    speed = courant_scale * jnp.exp(-2.0 * frequency / (NF - 1))
    theta = 2.0 * jnp.pi * direction / ND
    ae = jnp.broadcast_to((speed * jnp.cos(theta))[:, None], (comps, 128))
    an = jnp.broadcast_to((speed * jnp.sin(theta))[:, None], (comps, 128))

    sea = sea_mask > 0
    before = jnp.dot(
        sea.astype(jnp.bfloat16),
        jnp.triu(jnp.ones((lon, lon), jnp.bfloat16), 1),
        preferred_element_type=jnp.float32,
    )
    totals = jnp.sum(sea.astype(jnp.float32), axis=1)
    starts = jnp.sum(
        jnp.where(jnp.tril(jnp.ones((rows, rows), jnp.bool_), -1), totals[None, :], 0.0), axis=1
    )
    slot = jnp.where(sea, (before + starts[:, None]).astype(jnp.int32), -1)
    bases = jnp.minimum(starts.astype(jnp.int32) // STEP * STEP, SEA - WINDOW)
    meta = jnp.concatenate([
        jnp.stack([me, (tile > 0).astype(jnp.int32), (tile < tiles - 1).astype(jnp.int32)]),
        bases,
        parity.reshape(1),
    ]).astype(jnp.int32)
    slot_t = slot.T

    onehot = mark(bases, slot_t)

    moved = None
    pieces, spots = [], []
    for j, (begin, count) in enumerate(zip(offsets_of(parts_out), parts_out)):
        after = [pieces[(j - 2) * peers + k] for k in range(1, peers)] if j >= 2 else []
        at = (begin - parts_out[0]) // count if j else 0
        moved, *packed = propagate(
            meta, action, far if j else near, at, near, ae, an,
            east_current, north_current, onehot, moved, after, begin, count, peers,
        )
        for k in range(peers):
            piece = packed[k]
            if k:
                piece = lax.ppermute(piece, "spec", [(i, i ^ k) for i in range(peers)])
            pieces.append(piece)
            spots.append((k, begin))

    spread, sel, tt = setup(bases, slot, pattern, table, packed[0])
    woven = [
        weave(sel, tt, packed[0], begin, size, peers, dirs)
        for begin, size in zip(offsets_of(parts_back), parts_back)
    ]
    result = moved
    renewed, x = [None], None
    for g, (begin, size) in enumerate(zip(offsets_of(parts_back), parts_back)):
        renewed, x = couple(meta, woven[g], x, pieces, renewed[0], tuple(spots), begin, size, peers, dirs)
        back = [renewed[0]] + [
            lax.ppermute(renewed[k], "spec", [(i, i ^ k) for i in range(peers)])
            for k in range(1, peers)
        ]
        result = finish(meta, slot, spread, result, back, begin, size, peers)
    return result


def solution(mesh):
    return jax.shard_map(
        local,
        mesh=mesh,
        in_specs=(
            P("tile", "spec", None),
            P("tile", None),
            P("tile", None),
            P("tile", None),
            P(),
            P(),
        ),
        out_specs=P("tile", "spec", None),
        check_vma=False,
    )
```

```python
import functools

import jax
import jax.numpy as jnp
from jax import lax
from jax.experimental import pallas as pl
from jax.experimental.pallas import tpu as pltpu
from jax.sharding import PartitionSpec as P

NF = 64
ND = 48
SEA = 2048
WINDOW = 512
STEP = 256
SUBK = 16
courant_scale = 0.45
MIB = 1024 * 1024


def split_directions(count, sizes):
    if sum(sizes) == count:
        return sizes
    return (1,) * count


def offsets_of(sizes):
    return [sum(sizes[:i]) for i in range(len(sizes))]


def cost(us):
    return pl.CostEstimate(
        flops=int(us * 1.15e9), bytes_accessed=int(us * 3e6), transcendentals=0
    )


def params(mib=24):
    return pltpu.CompilerParams(vmem_limit_bytes=mib * MIB)


def near_kernel(depth, parity, act, east, north, across, beyond, ends, sem):
    rows, comps, lon = act.shape
    even = parity[0] == 0
    targets = ((even, across), (jnp.logical_not(even), beyond))
    copies = []
    for n, current in enumerate((east, north)):
        copies.append(pltpu.make_async_copy(current, ends.at[n], sem.at[n]))
    for i, (top, near) in enumerate(targets):
        first = jnp.where(top, rows - 2, 0)
        copies.append(pltpu.make_async_copy(
            act.at[pl.ds(first, 2), :depth, :], near.at[:, :depth, :], sem.at[2 + i]))
    for copy in copies:
        copy.start()
    for copy in copies:
        copy.wait()
    for top, near in targets:
        pair = [jnp.where(top, ends[n, rows - 1:rows, :], ends[n, 0:1, :]) for n in range(2)]
        pair = jnp.concatenate(pair, axis=0)
        coarse = pair.astype(jnp.bfloat16).astype(jnp.float32)
        tail = jnp.concatenate([coarse, pair - coarse, jnp.zeros((12, lon), jnp.float32)], axis=0)
        near[0, depth:, :] = tail.astype(jnp.bfloat16)
        near[1, depth:, :] = jnp.zeros((16, lon), jnp.bfloat16)


def near_edges(parity, action, east, north, depth):
    rows, comps, lon = action.shape
    vmem = pl.BlockSpec(memory_space=pltpu.VMEM)
    hbm = pl.BlockSpec(memory_space=pltpu.HBM)
    return pl.pallas_call(
        functools.partial(near_kernel, depth),
        in_specs=[pl.BlockSpec(memory_space=pltpu.SMEM), hbm, hbm, hbm],
        out_specs=[vmem] * 2,
        out_shape=[jax.ShapeDtypeStruct((2, depth + 16, lon), jnp.bfloat16)] * 2,
        scratch_shapes=[pltpu.VMEM((2, rows, lon), jnp.float32), pltpu.SemaphoreType.DMA((4,))],
        compiler_params=params(58),
        cost_estimate=cost(1),
        name="near_edges",
    )(parity, action, east, north)


def far_kernel(depth, parity, act, after, across, beyond, sem):
    rows = act.shape[0]
    even = parity[0] == 0
    copies = []
    for i, (top, far) in enumerate(((even, across), (jnp.logical_not(even), beyond))):
        first = jnp.where(top, rows - 2, 0)
        copies.append(pltpu.make_async_copy(act.at[pl.ds(first, 2), depth:, :], far, sem.at[i]))
        copies[-1].start()
    for copy in copies:
        copy.wait()


def far_edges(parity, action, after, depth):
    rows, comps, lon = action.shape
    vmem = pl.BlockSpec(memory_space=pltpu.VMEM)
    hbm = pl.BlockSpec(memory_space=pltpu.HBM)
    return pl.pallas_call(
        functools.partial(far_kernel, depth),
        in_specs=[pl.BlockSpec(memory_space=pltpu.SMEM), hbm, vmem],
        out_specs=[vmem] * 2,
        out_shape=[jax.ShapeDtypeStruct((2, comps - depth, lon), jnp.bfloat16)] * 2,
        scratch_shapes=[pltpu.SemaphoreType.DMA((2,))],
        compiler_params=params(49),
        cost_estimate=cost(0.5),
        name="far_edges",
    )(parity, action, after)


def mark_kernel(rows, bases, slot_t, onehot, token):
    token[...] = jnp.zeros_like(token)
    lanes = lax.broadcasted_iota(jnp.int32, onehot.shape[1:], 1)
    for r in range(rows):
        onehot[r] = jnp.where(slot_t[:, r:r + 1] - bases[r] == lanes, 1.0, 0.0).astype(jnp.bfloat16)


def mark(bases, slot_t):
    lon, rows = slot_t.shape
    vmem = pl.BlockSpec(memory_space=pltpu.VMEM)
    return pl.pallas_call(
        functools.partial(mark_kernel, rows),
        in_specs=[pl.BlockSpec(memory_space=pltpu.SMEM), vmem],
        out_specs=[vmem] * 2,
        out_shape=[
            jax.ShapeDtypeStruct((rows, lon, WINDOW), jnp.bfloat16),
            jax.ShapeDtypeStruct((8, 128), jnp.float32),
        ],
        compiler_params=params(),
        cost_estimate=cost(0.2),
        name="mark",
    )(bases, slot_t)


def setup_kernel(rows, bases, slot, pattern, table, after, spread, sel, tt):
    lon = slot.shape[1]
    depths = lax.broadcasted_iota(jnp.int32, (WINDOW, lon), 0)
    for r in range(rows):
        spread[r] = jnp.where(slot[r:r + 1, :] - bases[r] == depths, 1.0, 0.0).astype(jnp.bfloat16)
    columns = [jnp.broadcast_to(pattern[:, j:j + 1], (ND, 128)) for j in range(pattern.shape[1])]
    which = lax.broadcasted_iota(jnp.int32, (ND, 128), 1) // NF
    for t in range(ND * NF // 128):
        target = which + t * (128 // NF)
        hit = columns[0] == target
        for column in columns[1:]:
            hit = hit | (column == target)
        sel[:, t * 128:(t + 1) * 128] = jnp.where(hit, 1.0, 0.0)
    for odd in range(2):
        for t in range(ND // 2):
            pair = jnp.concatenate(
                [table[2 * t + odd].astype(jnp.float32), table[(2 * t + odd + 1) % ND].astype(jnp.float32)],
                axis=1,
            ).astype(jnp.bfloat16)
            tt[odd, :, t * 128:(t + 1) * 128] = pair
            tt[odd, :, ND * NF + t * 128:ND * NF + (t + 1) * 128] = pair


def setup(bases, slot, pattern, table, after):
    rows, lon = slot.shape
    vmem = pl.BlockSpec(memory_space=pltpu.VMEM)
    return pl.pallas_call(
        functools.partial(setup_kernel, rows),
        in_specs=[pl.BlockSpec(memory_space=pltpu.SMEM)] + [vmem] * 3 + [pl.BlockSpec(memory_space=pl.ANY)],
        out_specs=[vmem] * 3,
        out_shape=[
            jax.ShapeDtypeStruct((rows, WINDOW, lon), jnp.bfloat16),
            jax.ShapeDtypeStruct((ND, ND * NF), jnp.float32),
            jax.ShapeDtypeStruct((2, NF, 2 * ND * NF), jnp.bfloat16),
        ],
        compiler_params=params(),
        cost_estimate=cost(0.2),
        name="setup",
    )(bases, slot, pattern, table, after)


def weave_kernel(peers, dirs, begin, size, sel, tt, after, w):
    def strip(i, carry):
        r = i // size * dirs + begin + i % size
        turn = lax.rem(ND - r, ND)
        lanes = pl.ds(pl.multiple_of((turn // 2) * 128, 128), ND * NF)
        keep = jnp.broadcast_to(sel[pl.ds(r, 1), :], (16, ND * NF)).astype(jnp.bfloat16)
        for q in range(NF // 16):
            w[pl.ds(pl.multiple_of(i * NF + q * 16, 16), 16), :] = tt[turn % 2, pl.ds(q * 16, 16), lanes] * keep
        return carry

    lax.fori_loop(0, peers * size, strip, 0)


def weave(sel, tt, after, begin, size, peers, dirs):
    vmem = pl.BlockSpec(memory_space=pltpu.VMEM)
    return pl.pallas_call(
        functools.partial(weave_kernel, peers, dirs, begin, size),
        in_specs=[vmem, vmem, pl.BlockSpec(memory_space=pl.ANY)],
        out_specs=vmem,
        out_shape=jax.ShapeDtypeStruct((peers * size * NF, ND * NF), jnp.bfloat16),
        compiler_params=params(),
        cost_estimate=cost(0.1),
        name="weave",
    )(sel, tt, after)


def gather(meta, pieces, spots, dirs, x, sem):
    copies = []
    for i, (k, first) in enumerate(spots):
        depth = pieces[i].shape[0]
        start = pl.multiple_of(((meta[0] ^ k) * dirs + first) * NF, NF)
        copies.append(pltpu.make_async_copy(pieces[i], x.at[pl.ds(start, depth), :], sem.at[i]))
        copies[-1].start()
    return copies


def propagate_kernel(rows, peers, share, begin, dirs, aliased, spots, meta, act, across, beyond, across_tail, beyond_tail,
                     ae_ref, an_ref, east, north, onehot, *rest):
    ready = rest[:len(spots)]
    rest = rest[len(spots) + aliased:]
    even = meta[3 + rows] == 0
    moved_out = rest[0]
    outs = rest[1:peers + 1]
    block, moved, once, be_ref, bn_ref, packed, in_sem, out_sem, x_sem = rest[-9:]
    lon = act.shape[2]
    depth = across.shape[1]
    count = depth // NF
    halves = lon // 128
    lane = lax.broadcasted_iota(jnp.int32, (SUBK, 128), 1)
    first = lane == 0
    last = lane == 127

    def bring(i):
        part = pl.ds(pl.multiple_of(i * NF, NF), NF)
        far = pl.ds(pl.multiple_of(begin + i * NF, NF), NF)
        return pltpu.make_async_copy(act.at[:, far, :], block.at[:, part, :], in_sem.at[i])

    def leave(i):
        part = pl.ds(pl.multiple_of(i * NF, NF), NF)
        far = pl.ds(pl.multiple_of(begin + i * NF, NF), NF)
        return pltpu.make_async_copy(moved.at[:, part, :], moved_out.at[:, far, :], out_sem.at[i])

    for i in range(count):
        bring(i).start()
    gathering = gather(meta, ready, spots, dirs, rest[peers + 1], x_sem)
    for n, (own, b_ref) in enumerate(((east, be_ref), (north, bn_ref))):
        for at, one, other in ((0, beyond_tail, across_tail), (rows + 1, across_tail, beyond_tail)):
            ends = jnp.where(even, one[0].astype(jnp.float32), other[0].astype(jnp.float32))
            b_ref[at:at + 1, :] = courant_scale * (ends[n:n + 1, :] + ends[n + 2:n + 3, :])
        b_ref[1:rows + 1, :] = courant_scale * own[...]

    def advance(center, south, north_of, ks, r):
        ae = ae_ref[ks, :]
        an = an_ref[ks, :]
        right = [pltpu.roll(c, 1, 1) for c in center]
        left = [pltpu.roll(c, 127, 1) for c in center]
        result = []
        for h in range(halves):
            ce = ae + be_ref[r + 1:r + 2, h * 128:(h + 1) * 128]
            cn = an + bn_ref[r + 1:r + 2, h * 128:(h + 1) * 128]
            west = jnp.where(first, right[h - 1] if h else 0.0, right[h])
            east_of = jnp.where(last, left[h + 1] if h < halves - 1 else 0.0, left[h])
            along = jnp.where(ce > 0.0, west, east_of)
            across = jnp.where(cn > 0.0, south[h], north_of[h])
            c = center[h]
            result.append(c - jnp.abs(ce) * (c - along) - jnp.abs(cn) * (c - across))
        return result

    def group(g, carry):
        ks = pl.ds(pl.multiple_of(g * SUBK, SUBK), SUBK)

        def halved(value):
            return [value[:, h * 128:(h + 1) * 128] for h in range(halves)]

        def load(r):
            if 0 <= r < rows:
                return halved(block[r, ks, :].astype(jnp.float32))
            at = r + 2 if r < 0 else r - rows
            one, other = (beyond, across) if r < 0 else (across, beyond)
            return halved(
                jnp.where(even, one[at, ks, :].astype(jnp.float32), other[at, ks, :].astype(jnp.float32))
            )

        below, here = load(-2), load(-1)
        for r in range(-1, rows + 1):
            above = load(r + 1)
            value = advance(here, below, above, ks, r)
            if r == -1:
                value = [jnp.where(meta[1] > 0, v, 0.0) for v in value]
            if r == rows:
                value = [jnp.where(meta[2] > 0, v, 0.0) for v in value]
            for h in range(halves):
                once[r + 1, :, h * 128:(h + 1) * 128] = value[h]
            below, here = here, above
        below, here = halved(once[0]), halved(once[1])
        for r in range(rows):
            above = halved(once[r + 2])
            value = advance(here, below, above, ks, r)
            for h in range(halves):
                moved[r, ks, h * 128:(h + 1) * 128] = value[h].astype(jnp.bfloat16)
            below, here = here, above
        return carry

    def piece(i, carry):
        bring(i).wait()
        lax.fori_loop(i * (NF // SUBK), (i + 1) * (NF // SUBK), group, 0)
        leave(i).start()
        return carry

    lax.fori_loop(0, count, piece, 0)

    packed[...] = jnp.zeros_like(packed)
    for r in range(rows):
        window = pl.ds(pl.multiple_of(meta[3 + r], STEP), WINDOW)
        part = jnp.dot(moved[r], onehot[r], preferred_element_type=jnp.float32)
        packed[:, window] += part.astype(jnp.bfloat16)
    me = meta[0]
    for k in range(peers):
        start = pl.multiple_of((me ^ k) * share, 128)
        outs[k][...] = packed[:, pl.ds(start, share)]
    for i in range(count):
        leave(i).wait()
    for copy in gathering:
        copy.wait()


def propagate(meta, action, halos, at, tails, ae, an, east, north, onehot, moved, x, ready, spots, begin, count, peers):
    rows, comps, lon = action.shape
    share = SEA // peers
    which = begin // count
    depth = count * NF
    vmem = pl.BlockSpec(memory_space=pltpu.VMEM)
    hbm = pl.BlockSpec(memory_space=pltpu.HBM)
    halo = pl.BlockSpec((2, depth, lon), lambda s, m: (0, at, 0))
    tail = pl.BlockSpec((2, 16, lon), lambda s, m: (0, tails[0].shape[1] // 16 - 1, 0))
    part = pl.BlockSpec((depth, 128), lambda s, m: (which, 0))
    in_specs = [hbm, halo, halo, tail, tail, part, part, vmem, vmem, vmem]
    in_specs += [pl.BlockSpec(memory_space=pl.ANY)] * len(ready)
    args = [meta, action, *halos, *tails, ae, an, east, north, onehot, *ready]
    out_specs = [hbm] + [vmem] * peers
    out_shape = [jax.ShapeDtypeStruct(action.shape, jnp.bfloat16)]
    out_shape += [jax.ShapeDtypeStruct((depth, share), jnp.bfloat16)] * peers
    if ready:
        out_specs.append(vmem)
        out_shape.append(jax.ShapeDtypeStruct((ND * NF, share), jnp.bfloat16))
    aliases = {}
    for buffer, spec, out in ((moved, hbm, 0), (x, vmem, peers + 1)):
        if buffer is not None:
            aliases[len(args)] = out
            in_specs.append(spec)
            args.append(buffer)
    result = pl.pallas_call(
        functools.partial(
            propagate_kernel, rows, peers, share, begin * NF, comps // NF, len(aliases), spots
        ),
        grid_spec=pltpu.PrefetchScalarGridSpec(
            num_scalar_prefetch=1,
            grid=(1,),
            in_specs=in_specs,
            out_specs=out_specs,
            scratch_shapes=[
                pltpu.VMEM((rows, depth, lon), jnp.bfloat16),
                pltpu.VMEM((rows, depth, lon), jnp.bfloat16),
                pltpu.VMEM((rows + 2, SUBK, lon), jnp.float32),
                pltpu.VMEM((rows + 2, lon), jnp.float32),
                pltpu.VMEM((rows + 2, lon), jnp.float32),
                pltpu.VMEM((depth, SEA), jnp.bfloat16),
                pltpu.SemaphoreType.DMA((count,)),
                pltpu.SemaphoreType.DMA((count,)),
                pltpu.SemaphoreType.DMA((max(len(ready), 1),)),
            ],
        ),
        out_shape=out_shape,
        input_output_aliases=aliases,
        compiler_params=params(47),
        cost_estimate=cost(2.5 * count),
        name="propagate",
    )(*args)
    return result[0], result[1:peers + 1], result[peers + 1] if ready else None


def collect_kernel(spots, dirs, meta, *rest):
    sem = rest[-1]
    for copy in gather(meta, rest[:len(spots)], spots, dirs, rest[-2], sem):
        copy.wait()


def collect(meta, x, pieces, spots, dirs):
    vmem = pl.BlockSpec(memory_space=pltpu.VMEM)
    return pl.pallas_call(
        functools.partial(collect_kernel, spots, dirs),
        in_specs=[pl.BlockSpec(memory_space=pltpu.SMEM)]
        + [pl.BlockSpec(memory_space=pl.ANY)] * len(pieces)
        + [vmem],
        out_specs=vmem,
        out_shape=jax.ShapeDtypeStruct(x.shape, x.dtype),
        scratch_shapes=[pltpu.SemaphoreType.DMA((len(pieces),))],
        input_output_aliases={1 + len(pieces): 0},
        compiler_params=params(),
        cost_estimate=cost(0.2),
        name="collect",
    )(meta, *pieces, x)


def couple_kernel(peers, dirs, begin, size, spots, meta, w, *rest):
    me = meta[0]
    if spots:
        outs = rest[len(spots) + 1:len(spots) + 1 + peers]
        x, y, sem = rest[-3:]
        for copy in gather(meta, rest[:len(spots)], spots, dirs, x, sem):
            copy.wait()
    else:
        x = rest[0]
        outs = rest[-(peers + 1):-1]
        y = rest[-1]
    coupled = jnp.dot(w[...], x[...], preferred_element_type=jnp.float32)
    for p in range(peers):
        own = x[(p * dirs + begin) * NF:(p * dirs + begin + size) * NF, :].astype(jnp.float32)
        y[p] = (own + own * coupled[p * size * NF:(p + 1) * size * NF]).astype(jnp.bfloat16)
    for k in range(peers):
        outs[k][...] = y[me ^ k]


def couple(meta, w, x, pieces, after, spots, begin, size, peers, dirs):
    share = SEA // peers
    vmem = pl.BlockSpec(memory_space=pltpu.VMEM)
    loose = pl.BlockSpec(memory_space=pl.ANY)
    outs = [jax.ShapeDtypeStruct((size * NF, share), jnp.bfloat16)] * peers
    scratch = [pltpu.VMEM((peers, size * NF, share), jnp.bfloat16)]
    aliases = {}
    if after is None:
        in_specs, args = [loose] * len(pieces) + [vmem], [*pieces, x]
        outs = outs + [jax.ShapeDtypeStruct((ND * NF, share), jnp.bfloat16)]
        scratch.append(pltpu.SemaphoreType.DMA((len(pieces),)))
        aliases = {2 + len(pieces): peers}
    else:
        in_specs, args, spots = [vmem, loose], [x, after], ()
    result = pl.pallas_call(
        functools.partial(couple_kernel, peers, dirs, begin, size, spots),
        in_specs=[pl.BlockSpec(memory_space=pltpu.SMEM), vmem] + in_specs,
        out_specs=[vmem] * len(outs),
        out_shape=outs,
        scratch_shapes=scratch,
        input_output_aliases=aliases,
        compiler_params=params(),
        cost_estimate=cost(size),
        name="couple",
    )(meta, w, *args)
    return result[:peers], result[peers] if after is None else x


def finish_kernel(peers, share, begin, group, meta, slot, spread, moved, *rest):
    pieces = rest[:peers]
    out, renewed, old, new, piece_sem, in_sem, out_sem = rest[peers:]
    rows, lon = slot.shape
    depth = renewed.shape[0]
    me = meta[0]
    copies = []
    for k in range(peers):
        start = pl.multiple_of((me ^ k) * share, 128)
        copies.append(pltpu.make_async_copy(pieces[k], renewed.at[:, pl.ds(start, share)], piece_sem.at[k]))
        copies[-1].start()
    far = slice(begin, begin + depth)
    bring, leave = [], []
    for i in range(rows // group):
        part = slice(i * group, (i + 1) * group)
        bring.append(pltpu.make_async_copy(moved.at[part, far, :], old.at[part], in_sem.at[i]))
        leave.append(pltpu.make_async_copy(new.at[part], out.at[part, far, :], out_sem.at[i]))
        bring[-1].start()
    for copy in copies:
        copy.wait()
    for r in range(rows):
        if r % group == 0:
            bring[r // group].wait()
        base = pl.multiple_of(meta[3 + r], STEP)
        value = jnp.dot(renewed[:, pl.ds(base, WINDOW)], spread[r], preferred_element_type=jnp.float32)
        sea = slot[r:r + 1, :] >= 0
        new[r] = jnp.where(sea, value, old[r].astype(jnp.float32)).astype(jnp.bfloat16)
        if r % group == group - 1:
            leave[r // group].start()
    for copy in leave:
        copy.wait()


def finish(meta, slot, spread, moved, pieces, begin, size, peers):
    rows, comps, lon = moved.shape
    share = SEA // peers
    group = 4
    hbm = pl.BlockSpec(memory_space=pltpu.HBM)
    vmem = pl.BlockSpec(memory_space=pltpu.VMEM)
    return pl.pallas_call(
        functools.partial(finish_kernel, peers, share, begin * NF, group),
        in_specs=[pl.BlockSpec(memory_space=pltpu.SMEM), vmem, vmem, hbm]
        + [pl.BlockSpec(memory_space=pl.ANY)] * peers,
        out_specs=hbm,
        out_shape=jax.ShapeDtypeStruct(moved.shape, jnp.bfloat16),
        scratch_shapes=[
            pltpu.VMEM((size * NF, SEA), jnp.bfloat16),
            pltpu.VMEM((rows, size * NF, lon), jnp.bfloat16),
            pltpu.VMEM((rows, size * NF, lon), jnp.bfloat16),
            pltpu.SemaphoreType.DMA((peers,)),
            pltpu.SemaphoreType.DMA((rows // group,)),
            pltpu.SemaphoreType.DMA((rows // group,)),
        ],
        input_output_aliases={3: 0},
        compiler_params=params(),
        cost_estimate=cost(size),
        name="finish",
    )(meta, slot, spread, moved, *pieces)


def swap(array, first):
    count = lax.axis_size("tile")
    pairs = [(i, i + 1) for i in range(first, count - 1, 2)]
    return lax.ppermute(array, "tile", pairs + [(j, i) for i, j in pairs])


def local(action, east_current, north_current, sea_mask, pattern, table):
    rows, comps, lon = action.shape
    peers = lax.axis_size("spec")
    me = lax.axis_index("spec")
    tile = lax.axis_index("tile")
    tiles = lax.axis_size("tile")
    dirs = comps // NF
    parts_out = split_directions(dirs, (3, 3, 3, 3))
    parts_back = split_directions(dirs, (2, 4, 4, 2))

    ahead = parts_out[0] * NF
    parity = (tile % 2).astype(jnp.int32)
    parity = (tile % 2).astype(jnp.int32)
    across, beyond = near_edges(parity.reshape(1), action, east_current, north_current, ahead)
    near = swap(across, 0), swap(beyond, 1)

    components = me * comps + jnp.arange(comps, dtype=jnp.int32)
    direction = (components // NF).astype(jnp.float32)
    frequency = (components % NF).astype(jnp.float32)
    speed = courant_scale * jnp.exp(-2.0 * frequency / (NF - 1))
    theta = 2.0 * jnp.pi * direction / ND
    ae = jnp.broadcast_to((speed * jnp.cos(theta))[:, None], (comps, 128))
    an = jnp.broadcast_to((speed * jnp.sin(theta))[:, None], (comps, 128))

    sea = sea_mask > 0
    before = jnp.dot(
        sea.astype(jnp.bfloat16),
        jnp.triu(jnp.ones((lon, lon), jnp.bfloat16), 1),
        preferred_element_type=jnp.float32,
    )
    totals = jnp.sum(sea.astype(jnp.float32), axis=1)
    starts = jnp.sum(
        jnp.where(jnp.tril(jnp.ones((rows, rows), jnp.bool_), -1), totals[None, :], 0.0), axis=1
    )
    slot = jnp.where(sea, (before + starts[:, None]).astype(jnp.int32), -1)
    bases = jnp.minimum(starts.astype(jnp.int32) // STEP * STEP, SEA - WINDOW)
    meta = jnp.concatenate([
        jnp.stack([me, (tile > 0).astype(jnp.int32), (tile < tiles - 1).astype(jnp.int32)]),
        bases,
        parity.reshape(1),
    ]).astype(jnp.int32)
    slot_t = slot.T

    onehot, token = mark(bases, slot_t)
    across, beyond = far_edges(parity.reshape(1), action, token, ahead)
    far = swap(across, 0), swap(beyond, 1)

    moved, x = None, None
    pieces, spots = [], []
    for j, (begin, count) in enumerate(zip(offsets_of(parts_out), parts_out)):
        at = (begin - parts_out[0]) // count if j else 0
        ready = (pieces[j - 2], tuple(spots[j - 2])) if j >= 2 else ([], ())
        moved, packed, x = propagate(
            meta, action, far if j else near, at, near, ae, an,
            east_current, north_current, onehot, moved, x, *ready, begin, count, peers,
        )
        pieces.append([packed[0]] + [
            lax.ppermute(packed[k], "spec", [(i, i ^ k) for i in range(peers)])
            for k in range(1, peers)
        ])
        spots.append([(k, begin) for k in range(peers)])

    spread, sel, tt = setup(bases, slot, pattern, table, packed[0])
    woven = [
        weave(sel, tt, packed[0], begin, size, peers, dirs)
        for begin, size in zip(offsets_of(parts_back), parts_back)
    ]
    x = collect(meta, x, pieces[-2], tuple(spots[-2]), dirs)
    result = moved
    renewed = [None]
    for g, (begin, size) in enumerate(zip(offsets_of(parts_back), parts_back)):
        renewed, x = couple(
            meta, woven[g], x, pieces[-1], renewed[0], tuple(spots[-1]), begin, size, peers, dirs
        )
        back = [renewed[0]] + [
            lax.ppermute(renewed[k], "spec", [(i, i ^ k) for i in range(peers)])
            for k in range(1, peers)
        ]
        result = finish(meta, slot, spread, result, back, begin, size, peers)
    return result


def solution(mesh):
    return jax.shard_map(
        local,
        mesh=mesh,
        in_specs=(
            P("tile", "spec", None),
            P("tile", None),
            P("tile", None),
            P("tile", None),
            P(),
            P(),
        ),
        out_specs=P("tile", "spec", None),
        check_vma=False,
    )
```

```python
import functools

import jax
import jax.numpy as jnp
from jax import lax
from jax.experimental import pallas as pl
from jax.experimental.pallas import tpu as pltpu
from jax.sharding import PartitionSpec as P

NF = 64
ND = 48
SEA = 2048
WINDOW = 512
STEP = 256
SUBK = 16
courant_scale = 0.45
MIB = 1024 * 1024


def split_directions(count, sizes):
    if sum(sizes) == count:
        return sizes
    return (1,) * count


def offsets_of(sizes):
    return [sum(sizes[:i]) for i in range(len(sizes))]


def cost(us):
    return pl.CostEstimate(
        flops=int(us * 1.15e9), bytes_accessed=int(us * 3e6), transcendentals=0
    )


def params(mib=14):
    return pltpu.CompilerParams(vmem_limit_bytes=mib * MIB)


def near_kernel(depth, parity, act, east, north, across, beyond, ends, sem):
    rows, comps, lon = act.shape
    even = parity[0] == 0
    targets = ((even, across), (jnp.logical_not(even), beyond))
    copies = []
    for n, current in enumerate((east, north)):
        copies.append(pltpu.make_async_copy(current, ends.at[n], sem.at[n]))
    for i, (top, near) in enumerate(targets):
        first = jnp.where(top, rows - 2, 0)
        copies.append(pltpu.make_async_copy(
            act.at[pl.ds(first, 2), :depth, :], near.at[:, :depth, :], sem.at[2 + i]))
    for copy in copies:
        copy.start()
    for copy in copies:
        copy.wait()
    for top, near in targets:
        pair = [jnp.where(top, ends[n, rows - 1:rows, :], ends[n, 0:1, :]) for n in range(2)]
        pair = jnp.concatenate(pair, axis=0)
        coarse = pair.astype(jnp.bfloat16).astype(jnp.float32)
        tail = jnp.concatenate([coarse, pair - coarse, jnp.zeros((12, lon), jnp.float32)], axis=0)
        near[0, depth:, :] = tail.astype(jnp.bfloat16)
        near[1, depth:, :] = jnp.zeros((16, lon), jnp.bfloat16)


def near_edges(parity, action, east, north, depth):
    rows, comps, lon = action.shape
    vmem = pl.BlockSpec(memory_space=pltpu.VMEM)
    hbm = pl.BlockSpec(memory_space=pltpu.HBM)
    return pl.pallas_call(
        functools.partial(near_kernel, depth),
        in_specs=[pl.BlockSpec(memory_space=pltpu.SMEM), hbm, hbm, hbm],
        out_specs=[vmem] * 2,
        out_shape=[jax.ShapeDtypeStruct((2, depth + 16, lon), jnp.bfloat16)] * 2,
        scratch_shapes=[pltpu.VMEM((2, rows, lon), jnp.float32), pltpu.SemaphoreType.DMA((4,))],
        compiler_params=params(58),
        cost_estimate=cost(1),
        name="near_edges",
    )(parity, action, east, north)


def mark_kernel(rows, ahead, bases, parity, slot_t, act, onehot, held, rest, across, beyond, sem):
    even = parity[0] == 0
    copies = []
    for i, (top, far) in enumerate(((even, across), (jnp.logical_not(even), beyond))):
        first = jnp.where(top, rows - 2, 0)
        copies.append(pltpu.make_async_copy(act.at[pl.ds(first, 2), ahead:, :], far, sem.at[i]))
    for i in range(rows):
        copies.append(pltpu.make_async_copy(act.at[i, :ahead, :], held.at[i], sem.at[2 + i]))
        copies.append(pltpu.make_async_copy(act.at[i, ahead:, :], rest.at[i], sem.at[2 + rows + i]))
    for copy in copies:
        copy.start()
    lanes = lax.broadcasted_iota(jnp.int32, onehot.shape[1:], 1)
    for r in range(rows):
        onehot[r] = jnp.where(slot_t[:, r:r + 1] - bases[r] == lanes, 1.0, 0.0).astype(jnp.bfloat16)
    for copy in copies:
        copy.wait()


def mark(bases, parity, slot_t, action, ahead):
    rows, comps, lon = action.shape
    vmem = pl.BlockSpec(memory_space=pltpu.VMEM)
    smem = pl.BlockSpec(memory_space=pltpu.SMEM)
    far = jax.ShapeDtypeStruct((2, comps - ahead, lon), jnp.bfloat16)
    return pl.pallas_call(
        functools.partial(mark_kernel, rows, ahead),
        in_specs=[smem, smem, vmem, pl.BlockSpec(memory_space=pltpu.HBM)],
        out_specs=[vmem] * 5,
        out_shape=[
            jax.ShapeDtypeStruct((rows, lon, WINDOW), jnp.bfloat16),
            jax.ShapeDtypeStruct((rows, ahead, lon), action.dtype),
            jax.ShapeDtypeStruct((rows, comps - ahead, lon), action.dtype),
            far,
            far,
        ],
        scratch_shapes=[pltpu.SemaphoreType.DMA((2 + 2 * rows,))],
        compiler_params=params(40),
        cost_estimate=cost(0.2),
        name="mark",
    )(bases, parity, slot_t, action)


def setup_kernel(rows, bases, slot, pattern, table, after, spread, sel, tt):
    lon = slot.shape[1]
    depths = lax.broadcasted_iota(jnp.int32, (WINDOW, lon), 0)
    for r in range(rows):
        spread[r] = jnp.where(slot[r:r + 1, :] - bases[r] == depths, 1.0, 0.0).astype(jnp.bfloat16)
    columns = [jnp.broadcast_to(pattern[:, j:j + 1], (ND, 128)) for j in range(pattern.shape[1])]
    which = lax.broadcasted_iota(jnp.int32, (ND, 128), 1) // NF
    for t in range(ND * NF // 128):
        target = which + t * (128 // NF)
        hit = columns[0] == target
        for column in columns[1:]:
            hit = hit | (column == target)
        sel[:, t * 128:(t + 1) * 128] = jnp.where(hit, 1.0, 0.0)
    for odd in range(2):
        for t in range(ND // 2):
            pair = jnp.concatenate(
                [table[2 * t + odd].astype(jnp.float32), table[(2 * t + odd + 1) % ND].astype(jnp.float32)],
                axis=1,
            ).astype(jnp.bfloat16)
            tt[odd, :, t * 128:(t + 1) * 128] = pair
            tt[odd, :, ND * NF + t * 128:ND * NF + (t + 1) * 128] = pair


def setup(bases, slot, pattern, table, after):
    rows, lon = slot.shape
    vmem = pl.BlockSpec(memory_space=pltpu.VMEM)
    return pl.pallas_call(
        functools.partial(setup_kernel, rows),
        in_specs=[pl.BlockSpec(memory_space=pltpu.SMEM)] + [vmem] * 3 + [pl.BlockSpec(memory_space=pl.ANY)],
        out_specs=[vmem] * 3,
        out_shape=[
            jax.ShapeDtypeStruct((rows, WINDOW, lon), jnp.bfloat16),
            jax.ShapeDtypeStruct((ND, ND * NF), jnp.float32),
            jax.ShapeDtypeStruct((2, NF, 2 * ND * NF), jnp.bfloat16),
        ],
        compiler_params=params(),
        cost_estimate=cost(0.2),
        name="setup",
    )(bases, slot, pattern, table, after)


def weave_kernel(peers, dirs, begin, size, sel, tt, after, w):
    def strip(i, carry):
        r = i // size * dirs + begin + i % size
        turn = lax.rem(ND - r, ND)
        lanes = pl.ds(pl.multiple_of((turn // 2) * 128, 128), ND * NF)
        keep = jnp.broadcast_to(sel[pl.ds(r, 1), :], (16, ND * NF)).astype(jnp.bfloat16)
        for q in range(NF // 16):
            w[pl.ds(pl.multiple_of(i * NF + q * 16, 16), 16), :] = tt[turn % 2, pl.ds(q * 16, 16), lanes] * keep
        return carry

    lax.fori_loop(0, peers * size, strip, 0)


def weave(sel, tt, after, begin, size, peers, dirs):
    vmem = pl.BlockSpec(memory_space=pltpu.VMEM)
    return pl.pallas_call(
        functools.partial(weave_kernel, peers, dirs, begin, size),
        in_specs=[vmem, vmem, pl.BlockSpec(memory_space=pl.ANY)],
        out_specs=vmem,
        out_shape=jax.ShapeDtypeStruct((peers * size * NF, ND * NF), jnp.bfloat16),
        compiler_params=params(),
        cost_estimate=cost(0.1),
        name="weave",
    )(sel, tt, after)


def gather(meta, pieces, spots, dirs, x, sem):
    copies = []
    for i, (k, first) in enumerate(spots):
        depth = pieces[i].shape[0]
        start = pl.multiple_of(((meta[0] ^ k) * dirs + first) * NF, NF)
        copies.append(pltpu.make_async_copy(pieces[i], x.at[pl.ds(start, depth), :], sem.at[i]))
        copies[-1].start()
    return copies


def propagate_kernel(peers, share, begin, depth, offset, dirs, aliased, spots, meta, act, across, beyond,
                     across_tail, beyond_tail, ae_ref, an_ref, east, north, onehot, *rest):
    rows, _, lon = act.shape
    ready = rest[:len(spots)]
    rest = rest[len(spots) + aliased:]
    even = meta[3 + rows] == 0
    moved_out = rest[0]
    outs = rest[1:peers + 1]
    moved, once, be_ref, bn_ref, packed, out_sem, x_sem = rest[-7:]
    count = depth // NF
    halves = lon // 128
    lane = lax.broadcasted_iota(jnp.int32, (SUBK, 128), 1)
    first = lane == 0
    last = lane == 127

    def leave(i):
        part = pl.ds(pl.multiple_of(i * NF, NF), NF)
        far = pl.ds(pl.multiple_of(begin + i * NF, NF), NF)
        return pltpu.make_async_copy(moved.at[:, part, :], moved_out.at[:, far, :], out_sem.at[i])

    gathering = gather(meta, ready, spots, dirs, rest[peers + 1], x_sem)
    for n, (own, b_ref) in enumerate(((east, be_ref), (north, bn_ref))):
        for at, one, other in ((0, beyond_tail, across_tail), (rows + 1, across_tail, beyond_tail)):
            tails = [t[0, t.shape[1] - 16:, :].astype(jnp.float32) for t in (one, other)]
            ends = jnp.where(even, tails[0], tails[1])
            b_ref[at:at + 1, :] = courant_scale * (ends[n:n + 1, :] + ends[n + 2:n + 3, :])
        b_ref[1:rows + 1, :] = courant_scale * own[...]

    def advance(center, south, north_of, far, r):
        ae = ae_ref[far, :]
        an = an_ref[far, :]
        right = [pltpu.roll(c, 1, 1) for c in center]
        left = [pltpu.roll(c, 127, 1) for c in center]
        result = []
        for h in range(halves):
            ce = ae + be_ref[r + 1:r + 2, h * 128:(h + 1) * 128]
            cn = an + bn_ref[r + 1:r + 2, h * 128:(h + 1) * 128]
            west = jnp.where(first, right[h - 1] if h else 0.0, right[h])
            east_of = jnp.where(last, left[h + 1] if h < halves - 1 else 0.0, left[h])
            along = jnp.where(ce > 0.0, west, east_of)
            across = jnp.where(cn > 0.0, south[h], north_of[h])
            c = center[h]
            result.append(c - jnp.abs(ce) * (c - along) - jnp.abs(cn) * (c - across))
        return result

    def group(g, carry):
        ks = pl.ds(pl.multiple_of(g * SUBK, SUBK), SUBK)
        far = pl.ds(pl.multiple_of(begin + g * SUBK, SUBK), SUBK)
        edge = pl.ds(pl.multiple_of(offset + g * SUBK, SUBK), SUBK)

        def halved(value):
            return [value[:, h * 128:(h + 1) * 128] for h in range(halves)]

        def load(r):
            if 0 <= r < rows:
                return halved(act[r, edge, :].astype(jnp.float32))
            at = r + 2 if r < 0 else r - rows
            one, other = (beyond, across) if r < 0 else (across, beyond)
            return halved(
                jnp.where(even, one[at, edge, :].astype(jnp.float32), other[at, edge, :].astype(jnp.float32))
            )

        below, here = load(-2), load(-1)
        for r in range(-1, rows + 1):
            above = load(r + 1)
            value = advance(here, below, above, far, r)
            if r == -1:
                value = [jnp.where(meta[1] > 0, v, 0.0) for v in value]
            if r == rows:
                value = [jnp.where(meta[2] > 0, v, 0.0) for v in value]
            for h in range(halves):
                once[r + 1, :, h * 128:(h + 1) * 128] = value[h]
            below, here = here, above
        below, here = halved(once[0]), halved(once[1])
        for r in range(rows):
            above = halved(once[r + 2])
            value = advance(here, below, above, far, r)
            for h in range(halves):
                moved[r, ks, h * 128:(h + 1) * 128] = value[h].astype(jnp.bfloat16)
            below, here = here, above
        return carry

    def piece(i, carry):
        lax.fori_loop(i * (NF // SUBK), (i + 1) * (NF // SUBK), group, 0)
        leave(i).start()
        return carry

    lax.fori_loop(0, count, piece, 0)

    packed[...] = jnp.zeros_like(packed)
    for r in range(rows):
        window = pl.ds(pl.multiple_of(meta[3 + r], STEP), WINDOW)
        part = jnp.dot(moved[r], onehot[r], preferred_element_type=jnp.float32)
        packed[:, window] += part.astype(jnp.bfloat16)
    me = meta[0]
    for k in range(peers):
        start = pl.multiple_of((me ^ k) * share, 128)
        outs[k][...] = packed[:, pl.ds(start, share)]
    for i in range(count):
        leave(i).wait()
    for copy in gathering:
        copy.wait()


def propagate(meta, held, halos, offset, tails, ae, an, east, north, onehot, moved, x, ready, spots, begin, count, peers):
    rows, _, lon = held.shape
    comps = ae.shape[0]
    share = SEA // peers
    depth = count * NF
    vmem = pl.BlockSpec(memory_space=pltpu.VMEM)
    hbm = pl.BlockSpec(memory_space=pltpu.HBM)
    in_specs = [pl.BlockSpec(memory_space=pltpu.SMEM)] + [vmem] * 10
    in_specs += [pl.BlockSpec(memory_space=pl.ANY)] * len(ready)
    args = [meta, held, *halos, *tails, ae, an, east, north, onehot, *ready]
    out_specs = [hbm] + [vmem] * peers
    out_shape = [jax.ShapeDtypeStruct((rows, comps, lon), jnp.bfloat16)]
    out_shape += [jax.ShapeDtypeStruct((depth, share), jnp.bfloat16)] * peers
    if ready:
        out_specs.append(vmem)
        out_shape.append(jax.ShapeDtypeStruct((ND * NF, share), jnp.bfloat16))
    aliases = {}
    for buffer, spec, out in ((moved, hbm, 0), (x, vmem, peers + 1)):
        if buffer is not None:
            aliases[len(args)] = out
            in_specs.append(spec)
            args.append(buffer)
    result = pl.pallas_call(
        functools.partial(
            propagate_kernel, peers, share, begin * NF, depth, offset * NF, comps // NF, len(aliases), spots
        ),
        in_specs=in_specs,
        out_specs=out_specs,
        scratch_shapes=[
            pltpu.VMEM((rows, depth, lon), jnp.bfloat16),
            pltpu.VMEM((rows + 2, SUBK, lon), jnp.float32),
            pltpu.VMEM((rows + 2, lon), jnp.float32),
            pltpu.VMEM((rows + 2, lon), jnp.float32),
            pltpu.VMEM((depth, SEA), jnp.bfloat16),
            pltpu.SemaphoreType.DMA((count,)),
            pltpu.SemaphoreType.DMA((max(len(ready), 1),)),
        ],
        out_shape=out_shape,
        input_output_aliases=aliases,
        compiler_params=params(),
        cost_estimate=cost(2.2 * count),
        name="propagate",
    )(*args)
    return result[0], result[1:peers + 1], result[peers + 1] if ready else None


def collect_kernel(spots, dirs, meta, *rest):
    sem = rest[-1]
    for copy in gather(meta, rest[:len(spots)], spots, dirs, rest[-2], sem):
        copy.wait()


def collect(meta, x, pieces, spots, dirs):
    vmem = pl.BlockSpec(memory_space=pltpu.VMEM)
    return pl.pallas_call(
        functools.partial(collect_kernel, spots, dirs),
        in_specs=[pl.BlockSpec(memory_space=pltpu.SMEM)]
        + [pl.BlockSpec(memory_space=pl.ANY)] * len(pieces)
        + [vmem],
        out_specs=vmem,
        out_shape=jax.ShapeDtypeStruct(x.shape, x.dtype),
        scratch_shapes=[pltpu.SemaphoreType.DMA((len(pieces),))],
        input_output_aliases={1 + len(pieces): 0},
        compiler_params=params(),
        cost_estimate=cost(0.2),
        name="collect",
    )(meta, *pieces, x)


def couple_kernel(peers, dirs, begin, size, spots, meta, w, *rest):
    me = meta[0]
    if spots:
        outs = rest[len(spots) + 1:len(spots) + 1 + peers]
        x, y, sem = rest[-3:]
        for copy in gather(meta, rest[:len(spots)], spots, dirs, x, sem):
            copy.wait()
    else:
        x = rest[0]
        outs = rest[-(peers + 1):-1]
        y = rest[-1]
    coupled = jnp.dot(w[...], x[...], preferred_element_type=jnp.float32)
    for p in range(peers):
        own = x[(p * dirs + begin) * NF:(p * dirs + begin + size) * NF, :].astype(jnp.float32)
        y[p] = (own + own * coupled[p * size * NF:(p + 1) * size * NF]).astype(jnp.bfloat16)
    for k in range(peers):
        outs[k][...] = y[me ^ k]


def couple(meta, w, x, pieces, after, spots, begin, size, peers, dirs):
    share = SEA // peers
    vmem = pl.BlockSpec(memory_space=pltpu.VMEM)
    loose = pl.BlockSpec(memory_space=pl.ANY)
    outs = [jax.ShapeDtypeStruct((size * NF, share), jnp.bfloat16)] * peers
    scratch = [pltpu.VMEM((peers, size * NF, share), jnp.bfloat16)]
    aliases = {}
    if after is None:
        in_specs, args = [loose] * len(pieces) + [vmem], [*pieces, x]
        outs = outs + [jax.ShapeDtypeStruct((ND * NF, share), jnp.bfloat16)]
        scratch.append(pltpu.SemaphoreType.DMA((len(pieces),)))
        aliases = {2 + len(pieces): peers}
    else:
        in_specs, args, spots = [vmem] + [loose] * len(after), [x, *after], ()
    result = pl.pallas_call(
        functools.partial(couple_kernel, peers, dirs, begin, size, spots),
        in_specs=[pl.BlockSpec(memory_space=pltpu.SMEM), vmem] + in_specs,
        out_specs=[vmem] * len(outs),
        out_shape=outs,
        scratch_shapes=scratch,
        input_output_aliases=aliases,
        compiler_params=params(),
        cost_estimate=cost(size),
        name="couple",
    )(meta, w, *args)
    return result[:peers], result[peers] if after is None else x


def finish_kernel(peers, share, begin, group, meta, slot, spread, moved, *rest):
    pieces = rest[:peers]
    out, renewed, old, new, piece_sem, in_sem, out_sem = rest[peers:]
    rows, lon = slot.shape
    depth = renewed.shape[0]
    me = meta[0]
    copies = []
    for k in range(peers):
        start = pl.multiple_of((me ^ k) * share, 128)
        copies.append(pltpu.make_async_copy(pieces[k], renewed.at[:, pl.ds(start, share)], piece_sem.at[k]))
        copies[-1].start()
    far = slice(begin, begin + depth)
    bring, leave = [], []
    for i in range(rows // group):
        part = slice(i * group, (i + 1) * group)
        bring.append(pltpu.make_async_copy(moved.at[part, far, :], old.at[part], in_sem.at[i]))
        leave.append(pltpu.make_async_copy(new.at[part], out.at[part, far, :], out_sem.at[i]))
        bring[-1].start()
    for copy in copies:
        copy.wait()
    for r in range(rows):
        if r % group == 0:
            bring[r // group].wait()
        base = pl.multiple_of(meta[3 + r], STEP)
        value = jnp.dot(renewed[:, pl.ds(base, WINDOW)], spread[r], preferred_element_type=jnp.float32)
        sea = slot[r:r + 1, :] >= 0
        new[r] = jnp.where(sea, value, old[r].astype(jnp.float32)).astype(jnp.bfloat16)
        if r % group == group - 1:
            leave[r // group].start()
    for copy in leave:
        copy.wait()


def finish(meta, slot, spread, moved, pieces, begin, size, peers):
    rows, comps, lon = moved.shape
    share = SEA // peers
    group = 4
    hbm = pl.BlockSpec(memory_space=pltpu.HBM)
    vmem = pl.BlockSpec(memory_space=pltpu.VMEM)
    return pl.pallas_call(
        functools.partial(finish_kernel, peers, share, begin * NF, group),
        in_specs=[pl.BlockSpec(memory_space=pltpu.SMEM), vmem, vmem, hbm]
        + [pl.BlockSpec(memory_space=pl.ANY)] * peers,
        out_specs=hbm,
        out_shape=jax.ShapeDtypeStruct(moved.shape, jnp.bfloat16),
        scratch_shapes=[
            pltpu.VMEM((size * NF, SEA), jnp.bfloat16),
            pltpu.VMEM((rows, size * NF, lon), jnp.bfloat16),
            pltpu.VMEM((rows, size * NF, lon), jnp.bfloat16),
            pltpu.SemaphoreType.DMA((peers,)),
            pltpu.SemaphoreType.DMA((rows // group,)),
            pltpu.SemaphoreType.DMA((rows // group,)),
        ],
        input_output_aliases={3: 0},
        compiler_params=params(),
        cost_estimate=cost(size),
        name="finish",
    )(meta, slot, spread, moved, *pieces)


def swap(array, first):
    count = lax.axis_size("tile")
    pairs = [(i, i + 1) for i in range(first, count - 1, 2)]
    return lax.ppermute(array, "tile", pairs + [(j, i) for i, j in pairs])


def local(action, east_current, north_current, sea_mask, pattern, table):
    rows, comps, lon = action.shape
    peers = lax.axis_size("spec")
    me = lax.axis_index("spec")
    tile = lax.axis_index("tile")
    tiles = lax.axis_size("tile")
    dirs = comps // NF
    parts_out = split_directions(dirs, (3, 3, 3, 3))
    parts_back = split_directions(dirs, (2, 4, 4, 2))

    ahead = parts_out[0] * NF
    parity = (tile % 2).astype(jnp.int32)
    parity = (tile % 2).astype(jnp.int32)
    across, beyond = near_edges(parity.reshape(1), action, east_current, north_current, ahead)
    near = swap(across, 0), swap(beyond, 1)

    components = me * comps + jnp.arange(comps, dtype=jnp.int32)
    direction = (components // NF).astype(jnp.float32)
    frequency = (components % NF).astype(jnp.float32)
    speed = courant_scale * jnp.exp(-2.0 * frequency / (NF - 1))
    theta = 2.0 * jnp.pi * direction / ND
    ae = jnp.broadcast_to((speed * jnp.cos(theta))[:, None], (comps, 128))
    an = jnp.broadcast_to((speed * jnp.sin(theta))[:, None], (comps, 128))

    sea = sea_mask > 0
    before = jnp.dot(
        sea.astype(jnp.bfloat16),
        jnp.triu(jnp.ones((lon, lon), jnp.bfloat16), 1),
        preferred_element_type=jnp.float32,
    )
    totals = jnp.sum(sea.astype(jnp.float32), axis=1)
    starts = jnp.sum(
        jnp.where(jnp.tril(jnp.ones((rows, rows), jnp.bool_), -1), totals[None, :], 0.0), axis=1
    )
    slot = jnp.where(sea, (before + starts[:, None]).astype(jnp.int32), -1)
    bases = jnp.minimum(starts.astype(jnp.int32) // STEP * STEP, SEA - WINDOW)
    meta = jnp.concatenate([
        jnp.stack([me, (tile > 0).astype(jnp.int32), (tile < tiles - 1).astype(jnp.int32)]),
        bases,
        parity.reshape(1),
    ]).astype(jnp.int32)
    slot_t = slot.T

    onehot, held, remaining, across, beyond = mark(bases, parity.reshape(1), slot_t, action, ahead)
    far = swap(across, 0), swap(beyond, 1)

    moved, x = None, None
    pieces, spots = [], []
    for j, (begin, count) in enumerate(zip(offsets_of(parts_out), parts_out)):
        offset = begin - parts_out[0] if j else 0
        ready = (pieces[j - 2], tuple(spots[j - 2])) if j >= 2 else ([], ())
        moved, packed, x = propagate(
            meta, remaining if j else held, far if j else near, offset, near, ae, an,
            east_current, north_current, onehot, moved, x, *ready, begin, count, peers,
        )
        pieces.append([packed[0]] + [
            lax.ppermute(packed[k], "spec", [(i, i ^ k) for i in range(peers)])
            for k in range(1, peers)
        ])
        spots.append([(k, begin) for k in range(peers)])

    spread, sel, tt = setup(bases, slot, pattern, table, packed[0])
    woven = [
        weave(sel, tt, packed[0], begin, size, peers, dirs)
        for begin, size in zip(offsets_of(parts_back), parts_back)
    ]
    x = collect(meta, x, pieces[-2], tuple(spots[-2]), dirs)
    result = moved
    backs = []
    for g, (begin, size) in enumerate(zip(offsets_of(parts_back), parts_back)):
        after = backs[g - 2][1:] if g >= 2 else renewed[:1] if g else None
        renewed, x = couple(
            meta, woven[g], x, pieces[-1], after, tuple(spots[-1]), begin, size, peers, dirs
        )
        back = [renewed[0]] + [
            lax.ppermute(renewed[k], "spec", [(i, i ^ k) for i in range(peers)])
            for k in range(1, peers)
        ]
        backs.append(back)
        result = finish(meta, slot, spread, result, back, begin, size, peers)
    return result


def solution(mesh):
    return jax.shard_map(
        local,
        mesh=mesh,
        in_specs=(
            P("tile", "spec", None),
            P("tile", None),
            P("tile", None),
            P("tile", None),
            P(),
            P(),
        ),
        out_specs=P("tile", "spec", None),
        check_vma=False,
    )
```

```python
import functools

import jax
import jax.numpy as jnp
from jax import lax
from jax.experimental import pallas as pl
from jax.experimental.pallas import tpu as pltpu
from jax.sharding import PartitionSpec as P

NF = 64
ND = 48
SEA = 2048
WINDOW = 512
STEP = 256
SUBK = 16
courant_scale = 0.45
MIB = 1024 * 1024


def split_directions(count, sizes):
    if sum(sizes) == count:
        return sizes
    return (1,) * count


def offsets_of(sizes):
    return [sum(sizes[:i]) for i in range(len(sizes))]


def cost(us):
    return pl.CostEstimate(
        flops=int(us * 1.15e9), bytes_accessed=int(us * 3e6), transcendentals=0
    )


def params(mib=16):
    return pltpu.CompilerParams(vmem_limit_bytes=mib * MIB)


def mark_kernel(rows, bases, slot_t, onehot, token):
    token[...] = jnp.zeros_like(token)
    lanes = lax.broadcasted_iota(jnp.int32, onehot.shape[1:], 1)
    for r in range(rows):
        onehot[r] = jnp.where(slot_t[:, r:r + 1] - bases[r] == lanes, 1.0, 0.0).astype(jnp.bfloat16)


def mark(bases, slot_t):
    lon, rows = slot_t.shape
    vmem = pl.BlockSpec(memory_space=pltpu.VMEM)
    return pl.pallas_call(
        functools.partial(mark_kernel, rows),
        in_specs=[pl.BlockSpec(memory_space=pltpu.SMEM), vmem],
        out_specs=[vmem] * 2,
        out_shape=[
            jax.ShapeDtypeStruct((rows, lon, WINDOW), jnp.bfloat16),
            jax.ShapeDtypeStruct((8, 128), jnp.int32),
        ],
        compiler_params=params(),
        cost_estimate=cost(0.2),
        name="mark",
    )(bases, slot_t)


def setup_kernel(rows, bases, slot, pattern, table, after, spread, sel, tt):
    lon = slot.shape[1]
    depths = lax.broadcasted_iota(jnp.int32, (WINDOW, lon), 0)
    for r in range(rows):
        spread[r] = jnp.where(slot[r:r + 1, :] - bases[r] == depths, 1.0, 0.0).astype(jnp.bfloat16)
    columns = [jnp.broadcast_to(pattern[:, j:j + 1], (ND, 128)) for j in range(pattern.shape[1])]
    which = lax.broadcasted_iota(jnp.int32, (ND, 128), 1) // NF
    for t in range(ND * NF // 128):
        target = which + t * (128 // NF)
        hit = columns[0] == target
        for column in columns[1:]:
            hit = hit | (column == target)
        sel[:, t * 128:(t + 1) * 128] = jnp.where(hit, 1.0, 0.0)
    for odd in range(2):
        for t in range(ND // 2):
            pair = jnp.concatenate(
                [table[2 * t + odd].astype(jnp.float32), table[(2 * t + odd + 1) % ND].astype(jnp.float32)],
                axis=1,
            ).astype(jnp.bfloat16)
            tt[odd, :, t * 128:(t + 1) * 128] = pair
            tt[odd, :, ND * NF + t * 128:ND * NF + (t + 1) * 128] = pair


def setup(bases, slot, pattern, table, after):
    rows, lon = slot.shape
    vmem = pl.BlockSpec(memory_space=pltpu.VMEM)
    return pl.pallas_call(
        functools.partial(setup_kernel, rows),
        in_specs=[pl.BlockSpec(memory_space=pltpu.SMEM)] + [vmem] * 3 + [pl.BlockSpec(memory_space=pl.ANY)],
        out_specs=[vmem] * 3,
        out_shape=[
            jax.ShapeDtypeStruct((rows, WINDOW, lon), jnp.bfloat16),
            jax.ShapeDtypeStruct((ND, ND * NF), jnp.float32),
            jax.ShapeDtypeStruct((2, NF, 2 * ND * NF), jnp.bfloat16),
        ],
        compiler_params=params(),
        cost_estimate=cost(0.2),
        name="setup",
    )(bases, slot, pattern, table, after)


def weave_kernel(peers, dirs, begin, size, sel, tt, after, w):
    def strip(i, carry):
        r = i // size * dirs + begin + i % size
        turn = lax.rem(ND - r, ND)
        lanes = pl.ds(pl.multiple_of((turn // 2) * 128, 128), ND * NF)
        keep = jnp.broadcast_to(sel[pl.ds(r, 1), :], (16, ND * NF)).astype(jnp.bfloat16)
        for q in range(NF // 16):
            w[pl.ds(pl.multiple_of(i * NF + q * 16, 16), 16), :] = tt[turn % 2, pl.ds(q * 16, 16), lanes] * keep
        return carry

    lax.fori_loop(0, peers * size, strip, 0)


def weave(sel, tt, after, begin, size, peers, dirs):
    vmem = pl.BlockSpec(memory_space=pltpu.VMEM)
    return pl.pallas_call(
        functools.partial(weave_kernel, peers, dirs, begin, size),
        in_specs=[vmem, vmem, pl.BlockSpec(memory_space=pl.ANY)],
        out_specs=vmem,
        out_shape=jax.ShapeDtypeStruct((peers * size * NF, ND * NF), jnp.bfloat16),
        compiler_params=params(),
        cost_estimate=cost(0.1),
        name="weave",
    )(sel, tt, after)


def gather(meta, pieces, spots, dirs, x, sem):
    copies = []
    for i, (k, first) in enumerate(spots):
        depth = pieces[i].shape[0]
        start = pl.multiple_of(((meta[0] ^ k) * dirs + first) * NF, NF)
        copies.append(pltpu.make_async_copy(pieces[i], x.at[pl.ds(start, depth), :], sem.at[i]))
        copies[-1].start()
    return copies


def propagate_kernel(peers, share, begin, depth, offset, source, dirs, aliased, spots, meta, act, across, beyond,
                     across_tail, beyond_tail, ae_ref, an_ref, east, north, onehot, *rest):
    rows, _, lon = act.shape
    ready = rest[:len(spots)]
    rest = rest[len(spots) + aliased:]
    even = meta[3 + rows] == 0
    moved_out = rest[0]
    outs = rest[1:peers + 1]
    block, moved, once, be_ref, bn_ref, packed, in_sem, out_sem, x_sem = rest[-9:]
    count = depth // NF
    halves = lon // 128
    lane = lax.broadcasted_iota(jnp.int32, (SUBK, 128), 1)
    first = lane == 0
    last = lane == 127

    def bring(i):
        part = pl.ds(pl.multiple_of(i * NF, NF), NF)
        there = pl.ds(pl.multiple_of(source + i * NF, NF), NF)
        return pltpu.make_async_copy(act.at[:, there, :], block.at[:, part, :], in_sem.at[i])

    def leave(i):
        part = pl.ds(pl.multiple_of(i * NF, NF), NF)
        far = pl.ds(pl.multiple_of(begin + i * NF, NF), NF)
        return pltpu.make_async_copy(moved.at[:, part, :], moved_out.at[:, far, :], out_sem.at[i])

    for i in range(count):
        bring(i).start()
    gathering = gather(meta, ready, spots, dirs, rest[peers + 1], x_sem)
    for n, (own, b_ref) in enumerate(((east, be_ref), (north, bn_ref))):
        for at, one, other in ((0, beyond_tail, across_tail), (rows + 1, across_tail, beyond_tail)):
            tails = [t[0, t.shape[1] - 16:, :].astype(jnp.float32) for t in (one, other)]
            ends = jnp.where(even, tails[0], tails[1])
            b_ref[at:at + 1, :] = courant_scale * (ends[n:n + 1, :] + ends[n + 2:n + 3, :])
        b_ref[1:rows + 1, :] = courant_scale * own[...]

    def advance(center, south, north_of, far, r):
        ae = ae_ref[far, :]
        an = an_ref[far, :]
        right = [pltpu.roll(c, 1, 1) for c in center]
        left = [pltpu.roll(c, 127, 1) for c in center]
        result = []
        for h in range(halves):
            ce = ae + be_ref[r + 1:r + 2, h * 128:(h + 1) * 128]
            cn = an + bn_ref[r + 1:r + 2, h * 128:(h + 1) * 128]
            west = jnp.where(first, right[h - 1] if h else 0.0, right[h])
            east_of = jnp.where(last, left[h + 1] if h < halves - 1 else 0.0, left[h])
            along = jnp.where(ce > 0.0, west, east_of)
            across = jnp.where(cn > 0.0, south[h], north_of[h])
            c = center[h]
            result.append(c - jnp.abs(ce) * (c - along) - jnp.abs(cn) * (c - across))
        return result

    def group(g, carry):
        ks = pl.ds(pl.multiple_of(g * SUBK, SUBK), SUBK)
        far = pl.ds(pl.multiple_of(begin + g * SUBK, SUBK), SUBK)
        edge = pl.ds(pl.multiple_of(offset + g * SUBK, SUBK), SUBK)

        def halved(value):
            return [value[:, h * 128:(h + 1) * 128] for h in range(halves)]

        def load(r):
            if 0 <= r < rows:
                return halved(block[r, ks, :].astype(jnp.float32))
            at = r + 2 if r < 0 else r - rows
            one, other = (beyond, across) if r < 0 else (across, beyond)
            return halved(
                jnp.where(even, one[at, edge, :].astype(jnp.float32), other[at, edge, :].astype(jnp.float32))
            )

        below, here = load(-2), load(-1)
        for r in range(-1, rows + 1):
            above = load(r + 1)
            value = advance(here, below, above, far, r)
            if r == -1:
                value = [jnp.where(meta[1] > 0, v, 0.0) for v in value]
            if r == rows:
                value = [jnp.where(meta[2] > 0, v, 0.0) for v in value]
            for h in range(halves):
                once[r + 1, :, h * 128:(h + 1) * 128] = value[h]
            below, here = here, above
        below, here = halved(once[0]), halved(once[1])
        for r in range(rows):
            above = halved(once[r + 2])
            value = advance(here, below, above, far, r)
            for h in range(halves):
                moved[r, ks, h * 128:(h + 1) * 128] = value[h].astype(jnp.bfloat16)
            below, here = here, above
        return carry

    def piece(i, carry):
        bring(i).wait()
        lax.fori_loop(i * (NF // SUBK), (i + 1) * (NF // SUBK), group, 0)
        leave(i).start()
        return carry

    lax.fori_loop(0, count, piece, 0)

    packed[...] = jnp.zeros_like(packed)
    for r in range(rows):
        window = pl.ds(pl.multiple_of(meta[3 + r], STEP), WINDOW)
        part = jnp.dot(moved[r], onehot[r], preferred_element_type=jnp.float32)
        packed[:, window] += part.astype(jnp.bfloat16)
    me = meta[0]
    for k in range(peers):
        start = pl.multiple_of((me ^ k) * share, 128)
        outs[k][...] = packed[:, pl.ds(start, share)]
    for i in range(count):
        leave(i).wait()
    for copy in gathering:
        copy.wait()


def propagate(meta, held, halos, offset, tails, ae, an, east, north, onehot, moved, x, ready, spots, begin, count, peers):
    rows, _, lon = held.shape
    comps = ae.shape[0]
    share = SEA // peers
    depth = count * NF
    vmem = pl.BlockSpec(memory_space=pltpu.VMEM)
    hbm = pl.BlockSpec(memory_space=pltpu.HBM)
    loose = pl.BlockSpec(memory_space=pl.ANY)
    in_specs = [pl.BlockSpec(memory_space=pltpu.SMEM), loose] + [vmem] * 9 + [loose] * len(ready)
    args = [meta, held, *halos, *tails, ae, an, east, north, onehot, *ready]
    out_specs = [hbm] + [vmem] * peers
    out_shape = [jax.ShapeDtypeStruct((rows, comps, lon), jnp.bfloat16)]
    out_shape += [jax.ShapeDtypeStruct((depth, share), jnp.bfloat16)] * peers
    if ready:
        out_specs.append(vmem)
        out_shape.append(jax.ShapeDtypeStruct((ND * NF, share), jnp.bfloat16))
    aliases = {}
    for buffer, spec, out in ((moved, hbm, 0), (x, vmem, peers + 1)):
        if buffer is not None:
            aliases[len(args)] = out
            in_specs.append(spec)
            args.append(buffer)
    result = pl.pallas_call(
        functools.partial(
            propagate_kernel, peers, share, begin * NF, depth, offset * NF,
            (begin if held.shape[1] == comps else 0) * NF, comps // NF, len(aliases), spots,
        ),
        in_specs=in_specs,
        out_specs=out_specs,
        scratch_shapes=[
            pltpu.VMEM((rows, depth, lon), jnp.bfloat16),
            pltpu.VMEM((rows, depth, lon), jnp.bfloat16),
            pltpu.VMEM((rows + 2, SUBK, lon), jnp.float32),
            pltpu.VMEM((rows + 2, lon), jnp.float32),
            pltpu.VMEM((rows + 2, lon), jnp.float32),
            pltpu.VMEM((depth, SEA), jnp.bfloat16),
            pltpu.SemaphoreType.DMA((count,)),
            pltpu.SemaphoreType.DMA((count,)),
            pltpu.SemaphoreType.DMA((max(len(ready), 1),)),
        ],
        out_shape=out_shape,
        input_output_aliases=aliases,
        compiler_params=params(),
        cost_estimate=cost(2.2 * count),
        name="propagate",
    )(*args)
    return result[0], result[1:peers + 1], result[peers + 1] if ready else None


def collect_kernel(spots, dirs, meta, *rest):
    sem = rest[-1]
    for copy in gather(meta, rest[:len(spots)], spots, dirs, rest[-2], sem):
        copy.wait()


def collect(meta, x, pieces, spots, dirs):
    vmem = pl.BlockSpec(memory_space=pltpu.VMEM)
    return pl.pallas_call(
        functools.partial(collect_kernel, spots, dirs),
        in_specs=[pl.BlockSpec(memory_space=pltpu.SMEM)]
        + [pl.BlockSpec(memory_space=pl.ANY)] * len(pieces)
        + [vmem],
        out_specs=vmem,
        out_shape=jax.ShapeDtypeStruct(x.shape, x.dtype),
        scratch_shapes=[pltpu.SemaphoreType.DMA((len(pieces),))],
        input_output_aliases={1 + len(pieces): 0},
        compiler_params=params(),
        cost_estimate=cost(0.2),
        name="collect",
    )(meta, *pieces, x)


def couple_kernel(peers, dirs, begin, size, spots, meta, w, *rest):
    me = meta[0]
    if spots:
        outs = rest[len(spots) + 1:len(spots) + 1 + peers]
        x, y, sem = rest[-3:]
        for copy in gather(meta, rest[:len(spots)], spots, dirs, x, sem):
            copy.wait()
    else:
        x = rest[0]
        outs = rest[-(peers + 1):-1]
        y = rest[-1]
    coupled = jnp.dot(w[...], x[...], preferred_element_type=jnp.float32)
    for p in range(peers):
        own = x[(p * dirs + begin) * NF:(p * dirs + begin + size) * NF, :].astype(jnp.float32)
        y[p] = (own + own * coupled[p * size * NF:(p + 1) * size * NF]).astype(jnp.bfloat16)
    for k in range(peers):
        outs[k][...] = y[me ^ k]


def couple(meta, w, x, pieces, after, spots, begin, size, peers, dirs):
    share = SEA // peers
    vmem = pl.BlockSpec(memory_space=pltpu.VMEM)
    loose = pl.BlockSpec(memory_space=pl.ANY)
    outs = [jax.ShapeDtypeStruct((size * NF, share), jnp.bfloat16)] * peers
    scratch = [pltpu.VMEM((peers, size * NF, share), jnp.bfloat16)]
    aliases = {}
    if after is None:
        in_specs, args = [loose] * len(pieces) + [vmem], [*pieces, x]
        outs = outs + [jax.ShapeDtypeStruct((ND * NF, share), jnp.bfloat16)]
        scratch.append(pltpu.SemaphoreType.DMA((len(pieces),)))
        aliases = {2 + len(pieces): peers}
    else:
        in_specs, args, spots = [vmem] + [loose] * len(after), [x, *after], ()
    result = pl.pallas_call(
        functools.partial(couple_kernel, peers, dirs, begin, size, spots),
        in_specs=[pl.BlockSpec(memory_space=pltpu.SMEM), vmem] + in_specs,
        out_specs=[vmem] * len(outs),
        out_shape=outs,
        scratch_shapes=scratch,
        input_output_aliases=aliases,
        compiler_params=params(),
        cost_estimate=cost(size),
        name="couple",
    )(meta, w, *args)
    return result[:peers], result[peers] if after is None else x


def finish_kernel(peers, share, begin, group, meta, slot, spread, moved, *rest):
    pieces = rest[:peers]
    out, renewed, old, new, piece_sem, in_sem, out_sem = rest[peers:]
    rows, lon = slot.shape
    depth = renewed.shape[0]
    me = meta[0]
    copies = []
    for k in range(peers):
        start = pl.multiple_of((me ^ k) * share, 128)
        copies.append(pltpu.make_async_copy(pieces[k], renewed.at[:, pl.ds(start, share)], piece_sem.at[k]))
        copies[-1].start()
    far = slice(begin, begin + depth)
    bring, leave = [], []
    for i in range(rows // group):
        part = slice(i * group, (i + 1) * group)
        bring.append(pltpu.make_async_copy(moved.at[part, far, :], old.at[part], in_sem.at[i]))
        leave.append(pltpu.make_async_copy(new.at[part], out.at[part, far, :], out_sem.at[i]))
        bring[-1].start()
    for copy in copies:
        copy.wait()
    for r in range(rows):
        if r % group == 0:
            bring[r // group].wait()
        base = pl.multiple_of(meta[3 + r], STEP)
        value = jnp.dot(renewed[:, pl.ds(base, WINDOW)], spread[r], preferred_element_type=jnp.float32)
        sea = slot[r:r + 1, :] >= 0
        new[r] = jnp.where(sea, value, old[r].astype(jnp.float32)).astype(jnp.bfloat16)
        if r % group == group - 1:
            leave[r // group].start()
    for copy in leave:
        copy.wait()


def finish(meta, slot, spread, moved, pieces, begin, size, peers):
    rows, comps, lon = moved.shape
    share = SEA // peers
    group = 4
    hbm = pl.BlockSpec(memory_space=pltpu.HBM)
    vmem = pl.BlockSpec(memory_space=pltpu.VMEM)
    return pl.pallas_call(
        functools.partial(finish_kernel, peers, share, begin * NF, group),
        in_specs=[pl.BlockSpec(memory_space=pltpu.SMEM), vmem, vmem, hbm]
        + [pl.BlockSpec(memory_space=pl.ANY)] * peers,
        out_specs=hbm,
        out_shape=jax.ShapeDtypeStruct(moved.shape, jnp.bfloat16),
        scratch_shapes=[
            pltpu.VMEM((size * NF, SEA), jnp.bfloat16),
            pltpu.VMEM((rows, size * NF, lon), jnp.bfloat16),
            pltpu.VMEM((rows, size * NF, lon), jnp.bfloat16),
            pltpu.SemaphoreType.DMA((peers,)),
            pltpu.SemaphoreType.DMA((rows // group,)),
            pltpu.SemaphoreType.DMA((rows // group,)),
        ],
        input_output_aliases={3: 0},
        compiler_params=params(),
        cost_estimate=cost(size),
        name="finish",
    )(meta, slot, spread, moved, *pieces)


def swap(array, first):
    count = lax.axis_size("tile")
    pairs = [(i, i + 1) for i in range(first, count - 1, 2)]
    return lax.ppermute(array, "tile", pairs + [(j, i) for i, j in pairs])


def local(action, east_current, north_current, sea_mask, pattern, table):
    rows, comps, lon = action.shape
    peers = lax.axis_size("spec")
    me = lax.axis_index("spec")
    tile = lax.axis_index("tile")
    tiles = lax.axis_size("tile")
    dirs = comps // NF
    parts_out = split_directions(dirs, (3, 3, 3, 3))
    parts_back = split_directions(dirs, (2, 4, 4, 2))

    ahead = parts_out[0] * NF
    parity = (tile % 2).astype(jnp.int32)
    parity = (tile % 2).astype(jnp.int32)
    currents = jnp.stack([east_current, north_current])

    def near_edge(top):
        first = jnp.where(top, rows - 2, 0)
        body = lax.dynamic_slice(action, (first, 0, 0), (2, ahead, lon))
        pair = lax.dynamic_slice(currents, (0, jnp.where(top, rows - 1, 0), 0), (2, 1, lon))[:, 0]
        coarse = lax.reduce_precision(pair, 8, 7)
        tail = jnp.concatenate([coarse, pair - coarse, jnp.zeros((12, lon), jnp.float32)])
        return jnp.concatenate([body, jnp.broadcast_to(tail.astype(jnp.bfloat16), (2, 16, lon))], axis=1)

    def far_edge(top, zero):
        first = jnp.where(top, rows - 2, 0) + zero
        return lax.dynamic_slice(action, (first, ahead, 0), (2, comps - ahead, lon))

    near = swap(near_edge(parity == 0), 0), swap(near_edge(parity == 1), 1)

    components = me * comps + jnp.arange(comps, dtype=jnp.int32)
    direction = (components // NF).astype(jnp.float32)
    frequency = (components % NF).astype(jnp.float32)
    speed = courant_scale * jnp.exp(-2.0 * frequency / (NF - 1))
    theta = 2.0 * jnp.pi * direction / ND
    ae = jnp.broadcast_to((speed * jnp.cos(theta))[:, None], (comps, 128))
    an = jnp.broadcast_to((speed * jnp.sin(theta))[:, None], (comps, 128))

    sea = sea_mask > 0
    before = jnp.dot(
        sea.astype(jnp.bfloat16),
        jnp.triu(jnp.ones((lon, lon), jnp.bfloat16), 1),
        preferred_element_type=jnp.float32,
    )
    totals = jnp.sum(sea.astype(jnp.float32), axis=1)
    starts = jnp.sum(
        jnp.where(jnp.tril(jnp.ones((rows, rows), jnp.bool_), -1), totals[None, :], 0.0), axis=1
    )
    slot = jnp.where(sea, (before + starts[:, None]).astype(jnp.int32), -1)
    bases = jnp.minimum(starts.astype(jnp.int32) // STEP * STEP, SEA - WINDOW)
    meta = jnp.concatenate([
        jnp.stack([me, (tile > 0).astype(jnp.int32), (tile < tiles - 1).astype(jnp.int32)]),
        bases,
        parity.reshape(1),
    ]).astype(jnp.int32)
    slot_t = slot.T

    onehot, token = mark(bases, slot_t)
    far = swap(far_edge(parity == 0, token[0, 0]), 0), swap(far_edge(parity == 1, token[0, 0]), 1)

    moved, x = None, None
    pieces, spots = [], []
    for j, (begin, count) in enumerate(zip(offsets_of(parts_out), parts_out)):
        offset = begin - parts_out[0] if j else 0
        ready = (pieces[j - 2], tuple(spots[j - 2])) if j >= 2 else ([], ())
        moved, packed, x = propagate(
            meta, action if j else action[:, :ahead], far if j else near, offset, near, ae, an,
            east_current, north_current, onehot, moved, x, *ready, begin, count, peers,
        )
        pieces.append([packed[0]] + [
            lax.ppermute(packed[k], "spec", [(i, i ^ k) for i in range(peers)])
            for k in range(1, peers)
        ])
        spots.append([(k, begin) for k in range(peers)])

    spread, sel, tt = setup(bases, slot, pattern, table, packed[0])
    woven = [
        weave(sel, tt, packed[0], begin, size, peers, dirs)
        for begin, size in zip(offsets_of(parts_back), parts_back)
    ]
    x = collect(meta, x, pieces[-2], tuple(spots[-2]), dirs)
    result = moved
    backs = []
    for g, (begin, size) in enumerate(zip(offsets_of(parts_back), parts_back)):
        after = backs[g - 2][1:] if g >= 2 else renewed[:1] if g else None
        renewed, x = couple(
            meta, woven[g], x, pieces[-1], after, tuple(spots[-1]), begin, size, peers, dirs
        )
        back = [renewed[0]] + [
            lax.ppermute(renewed[k], "spec", [(i, i ^ k) for i in range(peers)])
            for k in range(1, peers)
        ]
        backs.append(back)
        result = finish(meta, slot, spread, result, back, begin, size, peers)
    return result


def solution(mesh):
    return jax.shard_map(
        local,
        mesh=mesh,
        in_specs=(
            P("tile", "spec", None),
            P("tile", None),
            P("tile", None),
            P("tile", None),
            P(),
            P(),
        ),
        out_specs=P("tile", "spec", None),
        check_vma=False,
    )
```

```python
import functools

import jax
import jax.numpy as jnp
from jax import lax
from jax.experimental import pallas as pl
from jax.experimental.pallas import tpu as pltpu
from jax.sharding import PartitionSpec as P

NF = 64
ND = 48
SEA = 2048
WINDOW = 512
STEP = 256
SUBK = 16
courant_scale = 0.45
MIB = 1024 * 1024


def split_directions(count, sizes):
    if sum(sizes) == count:
        return sizes
    return (1,) * count


def offsets_of(sizes):
    return [sum(sizes[:i]) for i in range(len(sizes))]


def cost(us):
    return pl.CostEstimate(
        flops=int(us * 1.15e9), bytes_accessed=int(us * 3e6), transcendentals=0
    )


def params(mib=16):
    return pltpu.CompilerParams(vmem_limit_bytes=mib * MIB)


def mark_kernel(rows, ahead, meta, slot_t, pattern, act, onehot, passed, across, beyond, sem):
    even = meta[3 + rows] == 0
    copies = []
    for i, (top, far) in enumerate(((even, across), (jnp.logical_not(even), beyond))):
        first = jnp.where(top, rows - 2, 0)
        copies.append(pltpu.make_async_copy(act.at[pl.ds(first, 2), ahead:, :], far, sem.at[i]))
        copies[-1].start()
    passed[...] = pattern[...]
    lanes = lax.broadcasted_iota(jnp.int32, onehot.shape[1:], 1)
    for r in range(rows):
        onehot[r] = jnp.where(slot_t[:, r:r + 1] - meta[3 + r] == lanes, 1.0, 0.0).astype(jnp.bfloat16)
    for copy in copies:
        copy.wait()


def mark(meta, slot_t, pattern, action, ahead):
    rows, comps, lon = action.shape
    vmem = pl.BlockSpec(memory_space=pltpu.VMEM)
    far = jax.ShapeDtypeStruct((2, comps - ahead, lon), jnp.bfloat16)
    return pl.pallas_call(
        functools.partial(mark_kernel, rows, ahead),
        in_specs=[pl.BlockSpec(memory_space=pltpu.SMEM), vmem, vmem, pl.BlockSpec(memory_space=pl.ANY)],
        out_specs=[vmem] * 4,
        out_shape=[
            jax.ShapeDtypeStruct((rows, lon, WINDOW), jnp.bfloat16),
            jax.ShapeDtypeStruct(pattern.shape, pattern.dtype),
            far,
            far,
        ],
        scratch_shapes=[pltpu.SemaphoreType.DMA((2,))],
        compiler_params=params(),
        cost_estimate=cost(0.2),
        name="mark",
    )(meta, slot_t, pattern, action)


def setup_kernel(rows, meta, slot, pattern, table, after, spread, sel, tt):
    lon = slot.shape[1]
    depths = lax.broadcasted_iota(jnp.int32, (WINDOW, lon), 0)
    for r in range(rows):
        spread[r] = jnp.where(slot[r:r + 1, :] - meta[3 + r] == depths, 1.0, 0.0).astype(jnp.bfloat16)
    columns = [jnp.broadcast_to(pattern[:, j:j + 1], (ND, 128)) for j in range(pattern.shape[1])]
    which = lax.broadcasted_iota(jnp.int32, (ND, 128), 1) // NF
    for t in range(ND * NF // 128):
        target = which + t * (128 // NF)
        hit = columns[0] == target
        for column in columns[1:]:
            hit = hit | (column == target)
        sel[:, t * 128:(t + 1) * 128] = jnp.where(hit, 1.0, 0.0)
    for odd in range(2):
        for t in range(ND // 2):
            pair = jnp.concatenate(
                [table[2 * t + odd].astype(jnp.float32), table[(2 * t + odd + 1) % ND].astype(jnp.float32)],
                axis=1,
            ).astype(jnp.bfloat16)
            tt[odd, :, t * 128:(t + 1) * 128] = pair
            tt[odd, :, ND * NF + t * 128:ND * NF + (t + 1) * 128] = pair


def setup(meta, slot, pattern, table, after):
    rows, lon = slot.shape
    vmem = pl.BlockSpec(memory_space=pltpu.VMEM)
    return pl.pallas_call(
        functools.partial(setup_kernel, rows),
        in_specs=[pl.BlockSpec(memory_space=pltpu.SMEM)] + [vmem] * 3 + [pl.BlockSpec(memory_space=pl.ANY)],
        out_specs=[vmem] * 3,
        out_shape=[
            jax.ShapeDtypeStruct((rows, WINDOW, lon), jnp.bfloat16),
            jax.ShapeDtypeStruct((ND, ND * NF), jnp.float32),
            jax.ShapeDtypeStruct((2, NF, 2 * ND * NF), jnp.bfloat16),
        ],
        compiler_params=params(),
        cost_estimate=cost(0.2),
        name="setup",
    )(meta, slot, pattern, table, after)


def weave_kernel(peers, dirs, begin, size, sel, tt, after, w):
    def strip(i, carry):
        r = i // size * dirs + begin + i % size
        turn = lax.rem(ND - r, ND)
        lanes = pl.ds(pl.multiple_of((turn // 2) * 128, 128), ND * NF)
        keep = jnp.broadcast_to(sel[pl.ds(r, 1), :], (16, ND * NF)).astype(jnp.bfloat16)
        for q in range(NF // 16):
            w[pl.ds(pl.multiple_of(i * NF + q * 16, 16), 16), :] = tt[turn % 2, pl.ds(q * 16, 16), lanes] * keep
        return carry

    lax.fori_loop(0, peers * size, strip, 0)


def weave(sel, tt, after, begin, size, peers, dirs):
    vmem = pl.BlockSpec(memory_space=pltpu.VMEM)
    return pl.pallas_call(
        functools.partial(weave_kernel, peers, dirs, begin, size),
        in_specs=[vmem, vmem, pl.BlockSpec(memory_space=pl.ANY)],
        out_specs=vmem,
        out_shape=jax.ShapeDtypeStruct((peers * size * NF, ND * NF), jnp.bfloat16),
        compiler_params=params(),
        cost_estimate=cost(0.1),
        name="weave",
    )(sel, tt, after)


def gather(meta, pieces, spots, dirs, x, sem):
    copies = []
    for i, (k, first) in enumerate(spots):
        depth = pieces[i].shape[0]
        start = pl.multiple_of(((meta[0] ^ k) * dirs + first) * NF, NF)
        copies.append(pltpu.make_async_copy(pieces[i], x.at[pl.ds(start, depth), :], sem.at[i]))
        copies[-1].start()
    return copies


def propagate_kernel(peers, share, begin, depth, offset, source, dirs, aliased, spots, meta, act, across, beyond,
                     across_tail, beyond_tail, ae_ref, an_ref, east, north, onehot, *rest):
    rows, _, lon = act.shape
    ready = rest[:len(spots)]
    rest = rest[len(spots) + aliased:]
    even = meta[3 + rows] == 0
    moved_out = rest[0]
    outs = rest[1:peers + 1]
    block, moved, once, be_ref, bn_ref, packed, in_sem, out_sem, x_sem = rest[-9:]
    count = depth // NF
    halves = lon // 128
    lane = lax.broadcasted_iota(jnp.int32, (SUBK, 128), 1)
    first = lane == 0
    last = lane == 127

    def bring(i):
        part = pl.ds(pl.multiple_of(i * NF, NF), NF)
        there = pl.ds(pl.multiple_of(source + i * NF, NF), NF)
        return pltpu.make_async_copy(act.at[:, there, :], block.at[:, part, :], in_sem.at[i])

    def leave(i):
        part = pl.ds(pl.multiple_of(i * NF, NF), NF)
        far = pl.ds(pl.multiple_of(begin + i * NF, NF), NF)
        return pltpu.make_async_copy(moved.at[:, part, :], moved_out.at[:, far, :], out_sem.at[i])

    for i in range(count):
        bring(i).start()
    gathering = gather(meta, ready, spots, dirs, rest[peers + 1], x_sem)
    for n, (own, b_ref) in enumerate(((east, be_ref), (north, bn_ref))):
        for at, one, other in ((0, beyond_tail, across_tail), (rows + 1, across_tail, beyond_tail)):
            tails = [t[0, t.shape[1] - 16:, :].astype(jnp.float32) for t in (one, other)]
            ends = jnp.where(even, tails[0], tails[1])
            b_ref[at:at + 1, :] = courant_scale * (ends[n:n + 1, :] + ends[n + 2:n + 3, :])
        b_ref[1:rows + 1, :] = courant_scale * own[...]

    def advance(center, south, north_of, far, r):
        ae = ae_ref[far, :]
        an = an_ref[far, :]
        right = [pltpu.roll(c, 1, 1) for c in center]
        left = [pltpu.roll(c, 127, 1) for c in center]
        result = []
        for h in range(halves):
            ce = ae + be_ref[r + 1:r + 2, h * 128:(h + 1) * 128]
            cn = an + bn_ref[r + 1:r + 2, h * 128:(h + 1) * 128]
            west = jnp.where(first, right[h - 1] if h else 0.0, right[h])
            east_of = jnp.where(last, left[h + 1] if h < halves - 1 else 0.0, left[h])
            along = jnp.where(ce > 0.0, west, east_of)
            across = jnp.where(cn > 0.0, south[h], north_of[h])
            c = center[h]
            result.append(c - jnp.abs(ce) * (c - along) - jnp.abs(cn) * (c - across))
        return result

    def group(g, carry):
        ks = pl.ds(pl.multiple_of(g * SUBK, SUBK), SUBK)
        far = pl.ds(pl.multiple_of(begin + g * SUBK, SUBK), SUBK)
        edge = pl.ds(pl.multiple_of(offset + g * SUBK, SUBK), SUBK)

        def halved(value):
            return [value[:, h * 128:(h + 1) * 128] for h in range(halves)]

        def load(r):
            if 0 <= r < rows:
                return halved(block[r, ks, :].astype(jnp.float32))
            at = r + 2 if r < 0 else r - rows
            one, other = (beyond, across) if r < 0 else (across, beyond)
            return halved(
                jnp.where(even, one[at, edge, :].astype(jnp.float32), other[at, edge, :].astype(jnp.float32))
            )

        below, here = load(-2), load(-1)
        for r in range(-1, rows + 1):
            above = load(r + 1)
            value = advance(here, below, above, far, r)
            if r == -1:
                value = [jnp.where(meta[1] > 0, v, 0.0) for v in value]
            if r == rows:
                value = [jnp.where(meta[2] > 0, v, 0.0) for v in value]
            for h in range(halves):
                once[r + 1, :, h * 128:(h + 1) * 128] = value[h]
            below, here = here, above
        below, here = halved(once[0]), halved(once[1])
        for r in range(rows):
            above = halved(once[r + 2])
            value = advance(here, below, above, far, r)
            for h in range(halves):
                moved[r, ks, h * 128:(h + 1) * 128] = value[h].astype(jnp.bfloat16)
            below, here = here, above
        return carry

    def piece(i, carry):
        bring(i).wait()
        lax.fori_loop(i * (NF // SUBK), (i + 1) * (NF // SUBK), group, 0)
        leave(i).start()
        return carry

    lax.fori_loop(0, count, piece, 0)

    packed[...] = jnp.zeros_like(packed)
    for r in range(rows):
        window = pl.ds(pl.multiple_of(meta[3 + r], STEP), WINDOW)
        part = jnp.dot(moved[r], onehot[r], preferred_element_type=jnp.float32)
        packed[:, window] += part.astype(jnp.bfloat16)
    me = meta[0]
    for k in range(peers):
        start = pl.multiple_of((me ^ k) * share, 128)
        outs[k][...] = packed[:, pl.ds(start, share)]
    for i in range(count):
        leave(i).wait()
    for copy in gathering:
        copy.wait()


def propagate(meta, held, halos, offset, tails, ae, an, east, north, onehot, moved, x, ready, spots, begin, count, peers):
    rows, _, lon = held.shape
    comps = ae.shape[0]
    share = SEA // peers
    depth = count * NF
    vmem = pl.BlockSpec(memory_space=pltpu.VMEM)
    hbm = pl.BlockSpec(memory_space=pltpu.HBM)
    loose = pl.BlockSpec(memory_space=pl.ANY)
    in_specs = [pl.BlockSpec(memory_space=pltpu.SMEM), loose] + [vmem] * 9 + [loose] * len(ready)
    args = [meta, held, *halos, *tails, ae, an, east, north, onehot, *ready]
    out_specs = [hbm] + [vmem] * peers
    out_shape = [jax.ShapeDtypeStruct((rows, comps, lon), jnp.bfloat16)]
    out_shape += [jax.ShapeDtypeStruct((depth, share), jnp.bfloat16)] * peers
    if ready:
        out_specs.append(vmem)
        out_shape.append(jax.ShapeDtypeStruct((ND * NF, share), jnp.bfloat16))
    aliases = {}
    for buffer, spec, out in ((moved, hbm, 0), (x, vmem, peers + 1)):
        if buffer is not None:
            aliases[len(args)] = out
            in_specs.append(spec)
            args.append(buffer)
    result = pl.pallas_call(
        functools.partial(
            propagate_kernel, peers, share, begin * NF, depth, offset * NF,
            (begin if held.shape[1] == comps else 0) * NF, comps // NF, len(aliases), spots,
        ),
        in_specs=in_specs,
        out_specs=out_specs,
        scratch_shapes=[
            pltpu.VMEM((rows, depth, lon), jnp.bfloat16),
            pltpu.VMEM((rows, depth, lon), jnp.bfloat16),
            pltpu.VMEM((rows + 2, SUBK, lon), jnp.float32),
            pltpu.VMEM((rows + 2, lon), jnp.float32),
            pltpu.VMEM((rows + 2, lon), jnp.float32),
            pltpu.VMEM((depth, SEA), jnp.bfloat16),
            pltpu.SemaphoreType.DMA((count,)),
            pltpu.SemaphoreType.DMA((count,)),
            pltpu.SemaphoreType.DMA((max(len(ready), 1),)),
        ],
        out_shape=out_shape,
        input_output_aliases=aliases,
        compiler_params=params(),
        cost_estimate=cost(2.2 * count),
        name="propagate",
    )(*args)
    return result[0], result[1:peers + 1], result[peers + 1] if ready else None


def collect_kernel(spots, dirs, meta, *rest):
    sem = rest[-1]
    for copy in gather(meta, rest[:len(spots)], spots, dirs, rest[-2], sem):
        copy.wait()


def collect(meta, x, pieces, spots, dirs):
    vmem = pl.BlockSpec(memory_space=pltpu.VMEM)
    return pl.pallas_call(
        functools.partial(collect_kernel, spots, dirs),
        in_specs=[pl.BlockSpec(memory_space=pltpu.SMEM)]
        + [pl.BlockSpec(memory_space=pl.ANY)] * len(pieces)
        + [vmem],
        out_specs=vmem,
        out_shape=jax.ShapeDtypeStruct(x.shape, x.dtype),
        scratch_shapes=[pltpu.SemaphoreType.DMA((len(pieces),))],
        input_output_aliases={1 + len(pieces): 0},
        compiler_params=params(),
        cost_estimate=cost(0.2),
        name="collect",
    )(meta, *pieces, x)


def couple_kernel(peers, dirs, begin, size, spots, meta, w, *rest):
    me = meta[0]
    if spots:
        outs = rest[len(spots) + 1:len(spots) + 1 + peers]
        x, y, sem = rest[-3:]
        for copy in gather(meta, rest[:len(spots)], spots, dirs, x, sem):
            copy.wait()
    else:
        x = rest[0]
        outs = rest[-(peers + 1):-1]
        y = rest[-1]
    coupled = jnp.dot(w[...], x[...], preferred_element_type=jnp.float32)
    for p in range(peers):
        own = x[(p * dirs + begin) * NF:(p * dirs + begin + size) * NF, :].astype(jnp.float32)
        y[p] = (own + own * coupled[p * size * NF:(p + 1) * size * NF]).astype(jnp.bfloat16)
    for k in range(peers):
        outs[k][...] = y[me ^ k]


def couple(meta, w, x, pieces, after, spots, begin, size, peers, dirs):
    share = SEA // peers
    vmem = pl.BlockSpec(memory_space=pltpu.VMEM)
    loose = pl.BlockSpec(memory_space=pl.ANY)
    outs = [jax.ShapeDtypeStruct((size * NF, share), jnp.bfloat16)] * peers
    scratch = [pltpu.VMEM((peers, size * NF, share), jnp.bfloat16)]
    aliases = {}
    if after is None:
        in_specs, args = [loose] * len(pieces) + [vmem], [*pieces, x]
        outs = outs + [jax.ShapeDtypeStruct((ND * NF, share), jnp.bfloat16)]
        scratch.append(pltpu.SemaphoreType.DMA((len(pieces),)))
        aliases = {2 + len(pieces): peers}
    else:
        in_specs, args, spots = [vmem] + [loose] * len(after), [x, *after], ()
    result = pl.pallas_call(
        functools.partial(couple_kernel, peers, dirs, begin, size, spots),
        in_specs=[pl.BlockSpec(memory_space=pltpu.SMEM), vmem] + in_specs,
        out_specs=[vmem] * len(outs),
        out_shape=outs,
        scratch_shapes=scratch,
        input_output_aliases=aliases,
        compiler_params=params(),
        cost_estimate=cost(size),
        name="couple",
    )(meta, w, *args)
    return result[:peers], result[peers] if after is None else x


def finish_kernel(peers, share, begin, group, meta, slot, spread, moved, *rest):
    pieces = rest[:peers]
    out, renewed, old, new, piece_sem, in_sem, out_sem = rest[peers:]
    rows, lon = slot.shape
    depth = renewed.shape[0]
    me = meta[0]
    copies = []
    for k in range(peers):
        start = pl.multiple_of((me ^ k) * share, 128)
        copies.append(pltpu.make_async_copy(pieces[k], renewed.at[:, pl.ds(start, share)], piece_sem.at[k]))
        copies[-1].start()
    far = slice(begin, begin + depth)
    bring, leave = [], []
    for i in range(rows // group):
        part = slice(i * group, (i + 1) * group)
        bring.append(pltpu.make_async_copy(moved.at[part, far, :], old.at[part], in_sem.at[i]))
        leave.append(pltpu.make_async_copy(new.at[part], out.at[part, far, :], out_sem.at[i]))
        bring[-1].start()
    for copy in copies:
        copy.wait()
    for r in range(rows):
        if r % group == 0:
            bring[r // group].wait()
        base = pl.multiple_of(meta[3 + r], STEP)
        value = jnp.dot(renewed[:, pl.ds(base, WINDOW)], spread[r], preferred_element_type=jnp.float32)
        sea = slot[r:r + 1, :] >= 0
        new[r] = jnp.where(sea, value, old[r].astype(jnp.float32)).astype(jnp.bfloat16)
        if r % group == group - 1:
            leave[r // group].start()
    for copy in leave:
        copy.wait()


def finish(meta, slot, spread, moved, pieces, begin, size, peers):
    rows, comps, lon = moved.shape
    share = SEA // peers
    group = 4
    hbm = pl.BlockSpec(memory_space=pltpu.HBM)
    vmem = pl.BlockSpec(memory_space=pltpu.VMEM)
    return pl.pallas_call(
        functools.partial(finish_kernel, peers, share, begin * NF, group),
        in_specs=[pl.BlockSpec(memory_space=pltpu.SMEM), vmem, vmem, hbm]
        + [pl.BlockSpec(memory_space=pl.ANY)] * peers,
        out_specs=hbm,
        out_shape=jax.ShapeDtypeStruct(moved.shape, jnp.bfloat16),
        scratch_shapes=[
            pltpu.VMEM((size * NF, SEA), jnp.bfloat16),
            pltpu.VMEM((rows, size * NF, lon), jnp.bfloat16),
            pltpu.VMEM((rows, size * NF, lon), jnp.bfloat16),
            pltpu.SemaphoreType.DMA((peers,)),
            pltpu.SemaphoreType.DMA((rows // group,)),
            pltpu.SemaphoreType.DMA((rows // group,)),
        ],
        input_output_aliases={3: 0},
        compiler_params=params(),
        cost_estimate=cost(size),
        name="finish",
    )(meta, slot, spread, moved, *pieces)


def swap(array, first):
    count = lax.axis_size("tile")
    pairs = [(i, i + 1) for i in range(first, count - 1, 2)]
    return lax.ppermute(array, "tile", pairs + [(j, i) for i, j in pairs])


def local(action, east_current, north_current, sea_mask, pattern, table):
    rows, comps, lon = action.shape
    peers = lax.axis_size("spec")
    me = lax.axis_index("spec")
    tile = lax.axis_index("tile")
    tiles = lax.axis_size("tile")
    dirs = comps // NF
    parts_out = split_directions(dirs, (3, 3, 3, 3))
    parts_back = split_directions(dirs, (2, 4, 4, 2))

    ahead = parts_out[0] * NF
    parity = (tile % 2).astype(jnp.int32)
    parity = (tile % 2).astype(jnp.int32)
    currents = jnp.stack([east_current, north_current])

    def near_edge(top):
        first = jnp.where(top, rows - 2, 0)
        body = lax.dynamic_slice(action, (first, 0, 0), (2, ahead, lon))
        pair = lax.dynamic_slice(currents, (0, jnp.where(top, rows - 1, 0), 0), (2, 1, lon))[:, 0]
        coarse = lax.reduce_precision(pair, 8, 7)
        tail = jnp.concatenate([coarse, pair - coarse, jnp.zeros((12, lon), jnp.float32)])
        return jnp.concatenate([body, jnp.broadcast_to(tail.astype(jnp.bfloat16), (2, 16, lon))], axis=1)

    near = swap(near_edge(parity == 0), 0), swap(near_edge(parity == 1), 1)

    components = me * comps + jnp.arange(comps, dtype=jnp.int32)
    direction = (components // NF).astype(jnp.float32)
    frequency = (components % NF).astype(jnp.float32)
    speed = courant_scale * jnp.exp(-2.0 * frequency / (NF - 1))
    theta = 2.0 * jnp.pi * direction / ND
    ae = jnp.broadcast_to((speed * jnp.cos(theta))[:, None], (comps, 128))
    an = jnp.broadcast_to((speed * jnp.sin(theta))[:, None], (comps, 128))

    sea = sea_mask > 0
    before = jnp.dot(
        sea.astype(jnp.bfloat16),
        jnp.triu(jnp.ones((lon, lon), jnp.bfloat16), 1),
        preferred_element_type=jnp.float32,
    )
    totals = jnp.sum(sea.astype(jnp.float32), axis=1)
    starts = jnp.sum(
        jnp.where(jnp.tril(jnp.ones((rows, rows), jnp.bool_), -1), totals[None, :], 0.0), axis=1
    )
    slot = jnp.where(sea, (before + starts[:, None]).astype(jnp.int32), -1)
    bases = jnp.minimum(starts.astype(jnp.int32) // STEP * STEP, SEA - WINDOW)
    meta = jnp.concatenate([
        jnp.stack([me, (tile > 0).astype(jnp.int32), (tile < tiles - 1).astype(jnp.int32)]),
        bases,
        parity.reshape(1),
    ]).astype(jnp.int32)
    slot_t = slot.T

    onehot, pattern, across, beyond = mark(meta, slot_t, pattern, action, ahead)
    far = swap(across, 0), swap(beyond, 1)

    moved, x = None, None
    pieces, spots = [], []
    for j, (begin, count) in enumerate(zip(offsets_of(parts_out), parts_out)):
        offset = begin - parts_out[0] if j else 0
        ready = (pieces[j - 2], tuple(spots[j - 2])) if j >= 2 else ([], ())
        moved, packed, x = propagate(
            meta, action, far if j else near, offset, near, ae, an,
            east_current, north_current, onehot, moved, x, *ready, begin, count, peers,
        )
        pieces.append([packed[0]] + [
            lax.ppermute(packed[k], "spec", [(i, i ^ k) for i in range(peers)])
            for k in range(1, peers)
        ])
        spots.append([(k, begin) for k in range(peers)])

    spread, sel, tt = setup(meta, slot, pattern, table, packed[0])
    woven = [
        weave(sel, tt, packed[0], begin, size, peers, dirs)
        for begin, size in zip(offsets_of(parts_back), parts_back)
    ]
    x = collect(meta, x, pieces[-2], tuple(spots[-2]), dirs)
    result = moved
    backs = []
    for g, (begin, size) in enumerate(zip(offsets_of(parts_back), parts_back)):
        after = backs[g - 2][1:] if g >= 2 else renewed[:1] if g else None
        renewed, x = couple(
            meta, woven[g], x, pieces[-1], after, tuple(spots[-1]), begin, size, peers, dirs
        )
        back = [renewed[0]] + [
            lax.ppermute(renewed[k], "spec", [(i, i ^ k) for i in range(peers)])
            for k in range(1, peers)
        ]
        backs.append(back)
        result = finish(meta, slot, spread, result, back, begin, size, peers)
    return result


def solution(mesh):
    return jax.shard_map(
        local,
        mesh=mesh,
        in_specs=(
            P("tile", "spec", None),
            P("tile", None),
            P("tile", None),
            P("tile", None),
            P(),
            P(),
        ),
        out_specs=P("tile", "spec", None),
        check_vma=False,
    )
```

```python
import functools

import jax
import jax.numpy as jnp
from jax import lax
from jax.experimental import pallas as pl
from jax.experimental.pallas import tpu as pltpu
from jax.sharding import PartitionSpec as P

NF = 64
ND = 48
SEA = 2048
WINDOW = 512
STEP = 256
SUBK = 16
courant_scale = 0.45
MIB = 1024 * 1024


def split_directions(count, sizes):
    if sum(sizes) == count:
        return sizes
    return (1,) * count


def offsets_of(sizes):
    return [sum(sizes[:i]) for i in range(len(sizes))]


def cost(us):
    return pl.CostEstimate(
        flops=int(us * 1.15e9), bytes_accessed=int(us * 3e6), transcendentals=0
    )


def params(mib=16):
    return pltpu.CompilerParams(vmem_limit_bytes=mib * MIB)


def mark_kernel(rows, meta, slot_t, pattern, ae, an, top, bottom, onehot, passed, ae_out, an_out, across, beyond):
    even = meta[3 + rows] == 0

    @pl.when(even)
    def rising():
        across[...] = top[...]
        beyond[...] = bottom[...]

    @pl.when(jnp.logical_not(even))
    def falling():
        across[...] = bottom[...]
        beyond[...] = top[...]

    passed[...] = pattern[...]
    ae_out[...] = jnp.broadcast_to(ae[...], ae_out.shape)
    an_out[...] = jnp.broadcast_to(an[...], an_out.shape)
    lanes = lax.broadcasted_iota(jnp.int32, onehot.shape[1:], 1)
    for r in range(rows):
        onehot[r] = jnp.where(slot_t[:, r:r + 1] - meta[3 + r] == lanes, 1.0, 0.0).astype(jnp.bfloat16)


def mark(meta, slot_t, pattern, ae, an, top, bottom):
    lon, rows = slot_t.shape
    vmem = pl.BlockSpec(memory_space=pltpu.VMEM)
    return pl.pallas_call(
        functools.partial(mark_kernel, rows),
        in_specs=[pl.BlockSpec(memory_space=pltpu.SMEM)] + [vmem] * 6,
        out_specs=[vmem] * 6,
        out_shape=[
            jax.ShapeDtypeStruct((rows, lon, WINDOW), jnp.bfloat16),
            jax.ShapeDtypeStruct(pattern.shape, pattern.dtype),
            jax.ShapeDtypeStruct(ae.shape, ae.dtype),
            jax.ShapeDtypeStruct(an.shape, an.dtype),
            jax.ShapeDtypeStruct(top.shape, top.dtype),
            jax.ShapeDtypeStruct(top.shape, top.dtype),
        ],
        compiler_params=params(),
        cost_estimate=cost(0.2),
        name="mark",
    )(meta, slot_t, pattern, ae, an, top, bottom)


def setup_kernel(rows, meta, slot, pattern, table, after, spread, sel, tt):
    lon = slot.shape[1]
    depths = lax.broadcasted_iota(jnp.int32, (WINDOW, lon), 0)
    for r in range(rows):
        spread[r] = jnp.where(slot[r:r + 1, :] - meta[3 + r] == depths, 1.0, 0.0).astype(jnp.bfloat16)
    target = lax.broadcasted_iota(jnp.int32, (ND, 128), 1)
    hit = pattern[:, 0:1] == target
    for j in range(1, pattern.shape[1]):
        hit = hit | (pattern[:, j:j + 1] == target)
    chosen = jnp.where(hit, 1.0, 0.0).astype(jnp.bfloat16)
    block = lax.broadcasted_iota(jnp.int32, (128, ND * NF), 1) // NF
    owner = lax.broadcasted_iota(jnp.int32, (128, ND * NF), 0)
    widen = jnp.where(block == owner, 1.0, 0.0).astype(jnp.bfloat16)
    sel[...] = jnp.dot(chosen, widen, preferred_element_type=jnp.float32)
    for odd in range(2):
        for t in range(ND // 2):
            pair = jnp.concatenate(
                [table[2 * t + odd].astype(jnp.float32), table[(2 * t + odd + 1) % ND].astype(jnp.float32)],
                axis=1,
            ).astype(jnp.bfloat16)
            tt[odd, :, t * 128:(t + 1) * 128] = pair
            tt[odd, :, ND * NF + t * 128:ND * NF + (t + 1) * 128] = pair


def setup(meta, slot, pattern, table, after):
    rows, lon = slot.shape
    vmem = pl.BlockSpec(memory_space=pltpu.VMEM)
    return pl.pallas_call(
        functools.partial(setup_kernel, rows),
        in_specs=[pl.BlockSpec(memory_space=pltpu.SMEM)] + [vmem] * 3 + [pl.BlockSpec(memory_space=pl.ANY)],
        out_specs=[vmem] * 3,
        out_shape=[
            jax.ShapeDtypeStruct((rows, WINDOW, lon), jnp.bfloat16),
            jax.ShapeDtypeStruct((ND, ND * NF), jnp.float32),
            jax.ShapeDtypeStruct((2, NF, 2 * ND * NF), jnp.bfloat16),
        ],
        compiler_params=params(),
        cost_estimate=cost(0.2),
        name="setup",
    )(meta, slot, pattern, table, after)


def weave_kernel(peers, dirs, begin, size, sel, tt, after, w):
    def strip(i, carry):
        r = i // size * dirs + begin + i % size
        turn = lax.rem(ND - r, ND)
        lanes = pl.ds(pl.multiple_of((turn // 2) * 128, 128), ND * NF)
        keep = jnp.broadcast_to(sel[pl.ds(r, 1), :], (16, ND * NF)).astype(jnp.bfloat16)
        for q in range(NF // 16):
            w[pl.ds(pl.multiple_of(i * NF + q * 16, 16), 16), :] = tt[turn % 2, pl.ds(q * 16, 16), lanes] * keep
        return carry

    lax.fori_loop(0, peers * size, strip, 0)


def weave(sel, tt, after, begin, size, peers, dirs):
    vmem = pl.BlockSpec(memory_space=pltpu.VMEM)
    return pl.pallas_call(
        functools.partial(weave_kernel, peers, dirs, begin, size),
        in_specs=[vmem, vmem, pl.BlockSpec(memory_space=pl.ANY)],
        out_specs=vmem,
        out_shape=jax.ShapeDtypeStruct((peers * size * NF, ND * NF), jnp.bfloat16),
        compiler_params=params(),
        cost_estimate=cost(0.1),
        name="weave",
    )(sel, tt, after)


def gather(meta, pieces, spots, dirs, x, sem):
    copies = []
    for i, (k, first) in enumerate(spots):
        depth = pieces[i].shape[0]
        start = pl.multiple_of(((meta[0] ^ k) * dirs + first) * NF, NF)
        copies.append(pltpu.make_async_copy(pieces[i], x.at[pl.ds(start, depth), :], sem.at[i]))
        copies[-1].start()
    return copies


def propagate_kernel(peers, share, begin, depth, offset, source, dirs, aliased, spots, meta, act, across, beyond,
                     across_tail, beyond_tail, ae_ref, an_ref, east, north, onehot, *rest):
    rows, _, lon = act.shape
    ready = rest[:len(spots)]
    rest = rest[len(spots) + aliased:]
    even = meta[3 + rows] == 0
    moved_out = rest[0]
    outs = rest[1:peers + 1]
    block, moved, once, be_ref, bn_ref, packed, in_sem, out_sem, x_sem = rest[-9:]
    count = depth // NF
    halves = lon // 128
    lane = lax.broadcasted_iota(jnp.int32, (SUBK, 128), 1)
    first = lane == 0
    last = lane == 127

    def bring(i):
        part = pl.ds(pl.multiple_of(i * NF, NF), NF)
        there = pl.ds(pl.multiple_of(source + i * NF, NF), NF)
        return pltpu.make_async_copy(act.at[:, there, :], block.at[:, part, :], in_sem.at[i])

    def leave(i):
        part = pl.ds(pl.multiple_of(i * NF, NF), NF)
        far = pl.ds(pl.multiple_of(begin + i * NF, NF), NF)
        return pltpu.make_async_copy(moved.at[:, part, :], moved_out.at[:, far, :], out_sem.at[i])

    for i in range(count):
        bring(i).start()
    gathering = gather(meta, ready, spots, dirs, rest[peers + 1], x_sem)
    for n, (own, b_ref) in enumerate(((east, be_ref), (north, bn_ref))):
        for at, one, other in ((0, beyond_tail, across_tail), (rows + 1, across_tail, beyond_tail)):
            tails = [t[0, t.shape[1] - 16:, :].astype(jnp.float32) for t in (one, other)]
            ends = jnp.where(even, tails[0], tails[1])
            b_ref[at:at + 1, :] = courant_scale * (ends[n:n + 1, :] + ends[n + 2:n + 3, :])
        b_ref[1:rows + 1, :] = courant_scale * own[...]

    def advance(center, south, north_of, far, r):
        ae = ae_ref[far, :]
        an = an_ref[far, :]
        right = [pltpu.roll(c, 1, 1) for c in center]
        left = [pltpu.roll(c, 127, 1) for c in center]
        result = []
        for h in range(halves):
            ce = ae + be_ref[r + 1:r + 2, h * 128:(h + 1) * 128]
            cn = an + bn_ref[r + 1:r + 2, h * 128:(h + 1) * 128]
            west = jnp.where(first, right[h - 1] if h else 0.0, right[h])
            east_of = jnp.where(last, left[h + 1] if h < halves - 1 else 0.0, left[h])
            along = jnp.where(ce > 0.0, west, east_of)
            across = jnp.where(cn > 0.0, south[h], north_of[h])
            c = center[h]
            result.append(c - jnp.abs(ce) * (c - along) - jnp.abs(cn) * (c - across))
        return result

    def group(g, carry):
        ks = pl.ds(pl.multiple_of(g * SUBK, SUBK), SUBK)
        far = pl.ds(pl.multiple_of(begin + g * SUBK, SUBK), SUBK)
        edge = pl.ds(pl.multiple_of(offset + g * SUBK, SUBK), SUBK)

        def halved(value):
            return [value[:, h * 128:(h + 1) * 128] for h in range(halves)]

        def load(r):
            if 0 <= r < rows:
                return halved(block[r, ks, :].astype(jnp.float32))
            at = r + 2 if r < 0 else r - rows
            one, other = (beyond, across) if r < 0 else (across, beyond)
            return halved(
                jnp.where(even, one[at, edge, :].astype(jnp.float32), other[at, edge, :].astype(jnp.float32))
            )

        below, here = load(-2), load(-1)
        for r in range(-1, rows + 1):
            above = load(r + 1)
            value = advance(here, below, above, far, r)
            if r == -1:
                value = [jnp.where(meta[1] > 0, v, 0.0) for v in value]
            if r == rows:
                value = [jnp.where(meta[2] > 0, v, 0.0) for v in value]
            for h in range(halves):
                once[r + 1, :, h * 128:(h + 1) * 128] = value[h]
            below, here = here, above
        below, here = halved(once[0]), halved(once[1])
        for r in range(rows):
            above = halved(once[r + 2])
            value = advance(here, below, above, far, r)
            for h in range(halves):
                moved[r, ks, h * 128:(h + 1) * 128] = value[h].astype(jnp.bfloat16)
            below, here = here, above
        return carry

    def piece(i, carry):
        bring(i).wait()
        lax.fori_loop(i * (NF // SUBK), (i + 1) * (NF // SUBK), group, 0)
        leave(i).start()
        return carry

    lax.fori_loop(0, count, piece, 0)

    packed[...] = jnp.zeros_like(packed)
    for r in range(rows):
        window = pl.ds(pl.multiple_of(meta[3 + r], STEP), WINDOW)
        part = jnp.dot(moved[r], onehot[r], preferred_element_type=jnp.float32)
        packed[:, window] += part.astype(jnp.bfloat16)
    me = meta[0]
    for k in range(peers):
        start = pl.multiple_of((me ^ k) * share, 128)
        outs[k][...] = packed[:, pl.ds(start, share)]
    for i in range(count):
        leave(i).wait()
    for copy in gathering:
        copy.wait()


def propagate(meta, held, halos, offset, tails, ae, an, east, north, onehot, moved, x, ready, spots, begin, count, peers):
    rows, _, lon = held.shape
    comps = ae.shape[0]
    share = SEA // peers
    depth = count * NF
    vmem = pl.BlockSpec(memory_space=pltpu.VMEM)
    hbm = pl.BlockSpec(memory_space=pltpu.HBM)
    loose = pl.BlockSpec(memory_space=pl.ANY)
    in_specs = [pl.BlockSpec(memory_space=pltpu.SMEM), loose] + [vmem] * 9 + [loose] * len(ready)
    args = [meta, held, *halos, *tails, ae, an, east, north, onehot, *ready]
    out_specs = [hbm] + [vmem] * peers
    out_shape = [jax.ShapeDtypeStruct((rows, comps, lon), jnp.bfloat16)]
    out_shape += [jax.ShapeDtypeStruct((depth, share), jnp.bfloat16)] * peers
    if ready:
        out_specs.append(vmem)
        out_shape.append(jax.ShapeDtypeStruct((ND * NF, share), jnp.bfloat16))
    aliases = {}
    for buffer, spec, out in ((moved, hbm, 0), (x, vmem, peers + 1)):
        if buffer is not None:
            aliases[len(args)] = out
            in_specs.append(spec)
            args.append(buffer)
    result = pl.pallas_call(
        functools.partial(
            propagate_kernel, peers, share, begin * NF, depth, offset * NF,
            (begin if held.shape[1] == comps else 0) * NF, comps // NF, len(aliases), spots,
        ),
        in_specs=in_specs,
        out_specs=out_specs,
        scratch_shapes=[
            pltpu.VMEM((rows, depth, lon), jnp.bfloat16),
            pltpu.VMEM((rows, depth, lon), jnp.bfloat16),
            pltpu.VMEM((rows + 2, SUBK, lon), jnp.float32),
            pltpu.VMEM((rows + 2, lon), jnp.float32),
            pltpu.VMEM((rows + 2, lon), jnp.float32),
            pltpu.VMEM((depth, SEA), jnp.bfloat16),
            pltpu.SemaphoreType.DMA((count,)),
            pltpu.SemaphoreType.DMA((count,)),
            pltpu.SemaphoreType.DMA((max(len(ready), 1),)),
        ],
        out_shape=out_shape,
        input_output_aliases=aliases,
        compiler_params=params(),
        cost_estimate=cost(2.2 * count),
        name="propagate",
    )(*args)
    return result[0], result[1:peers + 1], result[peers + 1] if ready else None


def collect_kernel(spots, dirs, meta, *rest):
    sem = rest[-1]
    for copy in gather(meta, rest[:len(spots)], spots, dirs, rest[-2], sem):
        copy.wait()


def collect(meta, x, pieces, spots, dirs):
    vmem = pl.BlockSpec(memory_space=pltpu.VMEM)
    return pl.pallas_call(
        functools.partial(collect_kernel, spots, dirs),
        in_specs=[pl.BlockSpec(memory_space=pltpu.SMEM)]
        + [pl.BlockSpec(memory_space=pl.ANY)] * len(pieces)
        + [vmem],
        out_specs=vmem,
        out_shape=jax.ShapeDtypeStruct(x.shape, x.dtype),
        scratch_shapes=[pltpu.SemaphoreType.DMA((len(pieces),))],
        input_output_aliases={1 + len(pieces): 0},
        compiler_params=params(),
        cost_estimate=cost(0.2),
        name="collect",
    )(meta, *pieces, x)


def couple_kernel(peers, dirs, begin, size, spots, meta, w, *rest):
    me = meta[0]
    if spots:
        outs = rest[len(spots) + 1:len(spots) + 1 + peers]
        x, y, sem = rest[-3:]
        for copy in gather(meta, rest[:len(spots)], spots, dirs, x, sem):
            copy.wait()
    else:
        x = rest[0]
        outs = rest[-(peers + 1):-1]
        y = rest[-1]
    coupled = jnp.dot(w[...], x[...], preferred_element_type=jnp.float32)
    for p in range(peers):
        own = x[(p * dirs + begin) * NF:(p * dirs + begin + size) * NF, :].astype(jnp.float32)
        y[p] = (own + own * coupled[p * size * NF:(p + 1) * size * NF]).astype(jnp.bfloat16)
    for k in range(peers):
        outs[k][...] = y[me ^ k]


def couple(meta, w, x, pieces, after, spots, begin, size, peers, dirs):
    share = SEA // peers
    vmem = pl.BlockSpec(memory_space=pltpu.VMEM)
    loose = pl.BlockSpec(memory_space=pl.ANY)
    outs = [jax.ShapeDtypeStruct((size * NF, share), jnp.bfloat16)] * peers
    scratch = [pltpu.VMEM((peers, size * NF, share), jnp.bfloat16)]
    aliases = {}
    if after is None:
        in_specs, args = [loose] * len(pieces) + [vmem], [*pieces, x]
        outs = outs + [jax.ShapeDtypeStruct((ND * NF, share), jnp.bfloat16)]
        scratch.append(pltpu.SemaphoreType.DMA((len(pieces),)))
        aliases = {2 + len(pieces): peers}
    else:
        in_specs, args, spots = [vmem] + [loose] * len(after), [x, *after], ()
    result = pl.pallas_call(
        functools.partial(couple_kernel, peers, dirs, begin, size, spots),
        in_specs=[pl.BlockSpec(memory_space=pltpu.SMEM), vmem] + in_specs,
        out_specs=[vmem] * len(outs),
        out_shape=outs,
        scratch_shapes=scratch,
        input_output_aliases=aliases,
        compiler_params=params(),
        cost_estimate=cost(size),
        name="couple",
    )(meta, w, *args)
    return result[:peers], result[peers] if after is None else x


def finish_kernel(peers, share, begin, group, meta, slot, spread, moved, *rest):
    pieces = rest[:peers]
    out, renewed, old, new, piece_sem, in_sem, out_sem = rest[peers:]
    rows, lon = slot.shape
    depth = renewed.shape[0]
    me = meta[0]
    copies = []
    for k in range(peers):
        start = pl.multiple_of((me ^ k) * share, 128)
        copies.append(pltpu.make_async_copy(pieces[k], renewed.at[:, pl.ds(start, share)], piece_sem.at[k]))
        copies[-1].start()
    far = slice(begin, begin + depth)
    bring, leave = [], []
    for i in range(rows // group):
        part = slice(i * group, (i + 1) * group)
        bring.append(pltpu.make_async_copy(moved.at[part, far, :], old.at[part], in_sem.at[i]))
        leave.append(pltpu.make_async_copy(new.at[part], out.at[part, far, :], out_sem.at[i]))
        bring[-1].start()
    for copy in copies:
        copy.wait()
    for r in range(rows):
        if r % group == 0:
            bring[r // group].wait()
        base = pl.multiple_of(meta[3 + r], STEP)
        value = jnp.dot(renewed[:, pl.ds(base, WINDOW)], spread[r], preferred_element_type=jnp.float32)
        sea = slot[r:r + 1, :] >= 0
        new[r] = jnp.where(sea, value, old[r].astype(jnp.float32)).astype(jnp.bfloat16)
        if r % group == group - 1:
            leave[r // group].start()
    for copy in leave:
        copy.wait()


def finish(meta, slot, spread, moved, pieces, begin, size, peers):
    rows, comps, lon = moved.shape
    share = SEA // peers
    group = 4
    hbm = pl.BlockSpec(memory_space=pltpu.HBM)
    vmem = pl.BlockSpec(memory_space=pltpu.VMEM)
    return pl.pallas_call(
        functools.partial(finish_kernel, peers, share, begin * NF, group),
        in_specs=[pl.BlockSpec(memory_space=pltpu.SMEM), vmem, vmem, hbm]
        + [pl.BlockSpec(memory_space=pl.ANY)] * peers,
        out_specs=hbm,
        out_shape=jax.ShapeDtypeStruct(moved.shape, jnp.bfloat16),
        scratch_shapes=[
            pltpu.VMEM((size * NF, SEA), jnp.bfloat16),
            pltpu.VMEM((rows, size * NF, lon), jnp.bfloat16),
            pltpu.VMEM((rows, size * NF, lon), jnp.bfloat16),
            pltpu.SemaphoreType.DMA((peers,)),
            pltpu.SemaphoreType.DMA((rows // group,)),
            pltpu.SemaphoreType.DMA((rows // group,)),
        ],
        input_output_aliases={3: 0},
        compiler_params=params(),
        cost_estimate=cost(size),
        name="finish",
    )(meta, slot, spread, moved, *pieces)


def swap(array, first):
    count = lax.axis_size("tile")
    pairs = [(i, i + 1) for i in range(first, count - 1, 2)]
    return lax.ppermute(array, "tile", pairs + [(j, i) for i, j in pairs])


def local(action, east_current, north_current, sea_mask, pattern, table):
    rows, comps, lon = action.shape
    peers = lax.axis_size("spec")
    me = lax.axis_index("spec")
    tile = lax.axis_index("tile")
    tiles = lax.axis_size("tile")
    dirs = comps // NF
    parts_out = split_directions(dirs, (3, 3, 3, 3))
    parts_back = split_directions(dirs, (2, 4, 4, 2))

    ahead = parts_out[0] * NF
    parity = (tile % 2).astype(jnp.int32)
    parity = (tile % 2).astype(jnp.int32)
    currents = jnp.stack([east_current, north_current])

    def near_edge(top):
        first = jnp.where(top, rows - 2, 0)
        body = lax.dynamic_slice(action, (first, 0, 0), (2, ahead, lon))
        pair = lax.dynamic_slice(currents, (0, jnp.where(top, rows - 1, 0), 0), (2, 1, lon))[:, 0]
        coarse = lax.reduce_precision(pair, 8, 7)
        tail = jnp.concatenate([coarse, pair - coarse, jnp.zeros((12, lon), jnp.float32)])
        return jnp.concatenate([body, jnp.broadcast_to(tail.astype(jnp.bfloat16), (2, 16, lon))], axis=1)

    near = swap(near_edge(parity == 0), 0), swap(near_edge(parity == 1), 1)

    components = me * comps + jnp.arange(comps, dtype=jnp.int32)
    direction = (components // NF).astype(jnp.float32)
    frequency = (components % NF).astype(jnp.float32)
    speed = courant_scale * jnp.exp(-2.0 * frequency / (NF - 1))
    theta = 2.0 * jnp.pi * direction / ND
    ae = jnp.broadcast_to((speed * jnp.cos(theta))[:, None], (comps, 128))
    an = jnp.broadcast_to((speed * jnp.sin(theta))[:, None], (comps, 128))

    sea = sea_mask > 0
    before = jnp.dot(
        sea.astype(jnp.bfloat16),
        jnp.triu(jnp.ones((lon, lon), jnp.bfloat16), 1),
        preferred_element_type=jnp.float32,
    )
    totals = jnp.sum(sea.astype(jnp.float32), axis=1)
    starts = jnp.sum(
        jnp.where(jnp.tril(jnp.ones((rows, rows), jnp.bool_), -1), totals[None, :], 0.0), axis=1
    )
    slot = jnp.where(sea, (before + starts[:, None]).astype(jnp.int32), -1)
    bases = jnp.minimum(starts.astype(jnp.int32) // STEP * STEP, SEA - WINDOW)
    meta = jnp.concatenate([
        jnp.stack([me, (tile > 0).astype(jnp.int32), (tile < tiles - 1).astype(jnp.int32)]),
        bases,
        parity.reshape(1),
    ]).astype(jnp.int32)
    slot_t = slot.T

    onehot, pattern, ae, an, across, beyond = mark(
        meta, slot_t, pattern, ae, an, action[rows - 2:, ahead:], action[:2, ahead:]
    )
    far = swap(across, 0), swap(beyond, 1)

    moved, x = None, None
    pieces, spots = [], []
    for j, (begin, count) in enumerate(zip(offsets_of(parts_out), parts_out)):
        offset = begin - parts_out[0] if j else 0
        ready = (pieces[j - 2], tuple(spots[j - 2])) if j >= 2 else ([], ())
        moved, packed, x = propagate(
            meta, action, far if j else near, offset, near, ae, an,
            east_current, north_current, onehot, moved, x, *ready, begin, count, peers,
        )
        pieces.append([packed[0]] + [
            lax.ppermute(packed[k], "spec", [(i, i ^ k) for i in range(peers)])
            for k in range(1, peers)
        ])
        spots.append([(k, begin) for k in range(peers)])

    spread, sel, tt = setup(meta, slot, pattern, table, packed[0])
    woven = [
        weave(sel, tt, packed[0], begin, size, peers, dirs)
        for begin, size in zip(offsets_of(parts_back), parts_back)
    ]
    x = collect(meta, x, pieces[-2], tuple(spots[-2]), dirs)
    result = moved
    backs = []
    for g, (begin, size) in enumerate(zip(offsets_of(parts_back), parts_back)):
        after = backs[g - 2][1:] if g >= 2 else renewed[:1] if g else None
        renewed, x = couple(
            meta, woven[g], x, pieces[-1], after, tuple(spots[-1]), begin, size, peers, dirs
        )
        back = [renewed[0]] + [
            lax.ppermute(renewed[k], "spec", [(i, i ^ k) for i in range(peers)])
            for k in range(1, peers)
        ]
        backs.append(back)
        result = finish(meta, slot, spread, result, back, begin, size, peers)
    return result


def solution(mesh):
    return jax.shard_map(
        local,
        mesh=mesh,
        in_specs=(
            P("tile", "spec", None),
            P("tile", None),
            P("tile", None),
            P("tile", None),
            P(),
            P(),
        ),
        out_specs=P("tile", "spec", None),
        check_vma=False,
    )
```

```python
import functools

import jax
import jax.numpy as jnp
from jax import lax
from jax.experimental import pallas as pl
from jax.experimental.pallas import tpu as pltpu
from jax.sharding import PartitionSpec as P

NF = 64
ND = 48
SEA = 2048
WINDOW = 512
STEP = 256
SUBK = 16
courant_scale = 0.45
MIB = 1024 * 1024


def split_directions(count, sizes):
    if sum(sizes) == count:
        return sizes
    return (1,) * count


def offsets_of(sizes):
    return [sum(sizes[:i]) for i in range(len(sizes))]


def cost(us):
    return pl.CostEstimate(
        flops=int(us * 1.15e9), bytes_accessed=int(us * 3e6), transcendentals=0
    )


def params(mib=16):
    return pltpu.CompilerParams(vmem_limit_bytes=mib * MIB)


def mark_kernel(rows, meta, slot_t, ae, an, top, bottom, onehot, ae_out, an_out, across, beyond):
    even = meta[3 + rows] == 0

    @pl.when(even)
    def rising():
        across[...] = top[...]
        beyond[...] = bottom[...]

    @pl.when(jnp.logical_not(even))
    def falling():
        across[...] = bottom[...]
        beyond[...] = top[...]

    ae_out[...] = jnp.broadcast_to(ae[...], ae_out.shape)
    an_out[...] = jnp.broadcast_to(an[...], an_out.shape)
    lanes = lax.broadcasted_iota(jnp.int32, onehot.shape[1:], 1)
    for r in range(rows):
        onehot[r] = jnp.where(slot_t[:, r:r + 1] - meta[3 + r] == lanes, 1.0, 0.0).astype(jnp.bfloat16)


def mark(meta, slot_t, ae, an, top, bottom):
    lon, rows = slot_t.shape
    vmem = pl.BlockSpec(memory_space=pltpu.VMEM)
    return pl.pallas_call(
        functools.partial(mark_kernel, rows),
        in_specs=[pl.BlockSpec(memory_space=pltpu.SMEM)] + [vmem] * 5,
        out_specs=[vmem] * 5,
        out_shape=[
            jax.ShapeDtypeStruct((rows, lon, WINDOW), jnp.bfloat16),
            jax.ShapeDtypeStruct(ae.shape, ae.dtype),
            jax.ShapeDtypeStruct(an.shape, an.dtype),
            jax.ShapeDtypeStruct(top.shape, top.dtype),
            jax.ShapeDtypeStruct(top.shape, top.dtype),
        ],
        compiler_params=params(),
        cost_estimate=cost(4),
        name="mark",
    )(meta, slot_t, ae, an, top, bottom)


def setup_kernel(rows, meta, slot, pattern_t, table, after, spread, sel, tt):
    lon = slot.shape[1]
    depths = lax.broadcasted_iota(jnp.int32, (WINDOW, lon), 0)
    for r in range(rows):
        spread[r] = jnp.where(slot[r:r + 1, :] - meta[3 + r] == depths, 1.0, 0.0).astype(jnp.bfloat16)
    target = lax.broadcasted_iota(jnp.int32, (128, ND), 0)
    hit = pattern_t[0:1, :] == target
    for j in range(1, pattern_t.shape[0]):
        hit = hit | (pattern_t[j:j + 1, :] == target)
    chosen = jnp.where(hit, 1.0, 0.0).astype(jnp.bfloat16)
    block = lax.broadcasted_iota(jnp.int32, (128, ND * NF), 1) // NF
    owner = lax.broadcasted_iota(jnp.int32, (128, ND * NF), 0)
    widen = jnp.where(block == owner, 1.0, 0.0).astype(jnp.bfloat16)
    sel[...] = lax.dot_general(
        chosen, widen, (((0,), (0,)), ((), ())), preferred_element_type=jnp.float32
    )
    for odd in range(2):
        for t in range(ND // 2):
            pair = jnp.concatenate(
                [table[2 * t + odd].astype(jnp.float32), table[(2 * t + odd + 1) % ND].astype(jnp.float32)],
                axis=1,
            ).astype(jnp.bfloat16)
            tt[odd, :, t * 128:(t + 1) * 128] = pair
            tt[odd, :, ND * NF + t * 128:ND * NF + (t + 1) * 128] = pair


def setup(meta, slot, pattern_t, table, after):
    rows, lon = slot.shape
    vmem = pl.BlockSpec(memory_space=pltpu.VMEM)
    return pl.pallas_call(
        functools.partial(setup_kernel, rows),
        in_specs=[pl.BlockSpec(memory_space=pltpu.SMEM)] + [vmem] * 3 + [pl.BlockSpec(memory_space=pl.ANY)],
        out_specs=[vmem] * 3,
        out_shape=[
            jax.ShapeDtypeStruct((rows, WINDOW, lon), jnp.bfloat16),
            jax.ShapeDtypeStruct((ND, ND * NF), jnp.float32),
            jax.ShapeDtypeStruct((2, NF, 2 * ND * NF), jnp.bfloat16),
        ],
        compiler_params=params(),
        cost_estimate=cost(0.2),
        name="setup",
    )(meta, slot, pattern_t, table, after)


def weave_kernel(peers, dirs, begin, size, sel, tt, after, w):
    def strip(i, carry):
        r = i // size * dirs + begin + i % size
        turn = lax.rem(ND - r, ND)
        lanes = pl.ds(pl.multiple_of((turn // 2) * 128, 128), ND * NF)
        keep = jnp.broadcast_to(sel[pl.ds(r, 1), :], (16, ND * NF)).astype(jnp.bfloat16)
        for q in range(NF // 16):
            w[pl.ds(pl.multiple_of(i * NF + q * 16, 16), 16), :] = tt[turn % 2, pl.ds(q * 16, 16), lanes] * keep
        return carry

    lax.fori_loop(0, peers * size, strip, 0)


def weave(sel, tt, after, begin, size, peers, dirs):
    vmem = pl.BlockSpec(memory_space=pltpu.VMEM)
    return pl.pallas_call(
        functools.partial(weave_kernel, peers, dirs, begin, size),
        in_specs=[vmem, vmem, pl.BlockSpec(memory_space=pl.ANY)],
        out_specs=vmem,
        out_shape=jax.ShapeDtypeStruct((peers * size * NF, ND * NF), jnp.bfloat16),
        compiler_params=params(),
        cost_estimate=cost(0.1),
        name="weave",
    )(sel, tt, after)


def gather(meta, pieces, spots, dirs, x, sem):
    copies = []
    for i, (k, first) in enumerate(spots):
        depth = pieces[i].shape[0]
        start = pl.multiple_of(((meta[0] ^ k) * dirs + first) * NF, NF)
        copies.append(pltpu.make_async_copy(pieces[i], x.at[pl.ds(start, depth), :], sem.at[i]))
        copies[-1].start()
    return copies


def propagate_kernel(peers, share, begin, depth, offset, source, dirs, aliased, spots, meta, act, across, beyond,
                     across_tail, beyond_tail, ae_ref, an_ref, east, north, onehot, *rest):
    rows, _, lon = act.shape
    ready = rest[:len(spots)]
    rest = rest[len(spots) + aliased:]
    even = meta[3 + rows] == 0
    moved_out = rest[0]
    outs = rest[1:peers + 1]
    block, moved, once, be_ref, bn_ref, packed, in_sem, out_sem, x_sem = rest[-9:]
    count = depth // NF
    halves = lon // 128
    lane = lax.broadcasted_iota(jnp.int32, (SUBK, 128), 1)
    first = lane == 0
    last = lane == 127

    def bring(i):
        part = pl.ds(pl.multiple_of(i * NF, NF), NF)
        there = pl.ds(pl.multiple_of(source + i * NF, NF), NF)
        return pltpu.make_async_copy(act.at[:, there, :], block.at[:, part, :], in_sem.at[i])

    def leave(i):
        part = pl.ds(pl.multiple_of(i * NF, NF), NF)
        far = pl.ds(pl.multiple_of(begin + i * NF, NF), NF)
        return pltpu.make_async_copy(moved.at[:, part, :], moved_out.at[:, far, :], out_sem.at[i])

    for i in range(count):
        bring(i).start()
    gathering = gather(meta, ready, spots, dirs, rest[peers + 1], x_sem)
    for n, (own, b_ref) in enumerate(((east, be_ref), (north, bn_ref))):
        for at, one, other in ((0, beyond_tail, across_tail), (rows + 1, across_tail, beyond_tail)):
            tails = [t[0, t.shape[1] - 16:, :].astype(jnp.float32) for t in (one, other)]
            ends = jnp.where(even, tails[0], tails[1])
            b_ref[at:at + 1, :] = courant_scale * (ends[n:n + 1, :] + ends[n + 2:n + 3, :])
        b_ref[1:rows + 1, :] = courant_scale * own[...]

    def advance(center, south, north_of, far, r):
        ae = ae_ref[far, :]
        an = an_ref[far, :]
        right = [pltpu.roll(c, 1, 1) for c in center]
        left = [pltpu.roll(c, 127, 1) for c in center]
        result = []
        for h in range(halves):
            ce = ae + be_ref[r + 1:r + 2, h * 128:(h + 1) * 128]
            cn = an + bn_ref[r + 1:r + 2, h * 128:(h + 1) * 128]
            west = jnp.where(first, right[h - 1] if h else 0.0, right[h])
            east_of = jnp.where(last, left[h + 1] if h < halves - 1 else 0.0, left[h])
            along = jnp.where(ce > 0.0, west, east_of)
            across = jnp.where(cn > 0.0, south[h], north_of[h])
            c = center[h]
            result.append(c - jnp.abs(ce) * (c - along) - jnp.abs(cn) * (c - across))
        return result

    def group(g, carry):
        ks = pl.ds(pl.multiple_of(g * SUBK, SUBK), SUBK)
        far = pl.ds(pl.multiple_of(begin + g * SUBK, SUBK), SUBK)
        edge = pl.ds(pl.multiple_of(offset + g * SUBK, SUBK), SUBK)

        def halved(value):
            return [value[:, h * 128:(h + 1) * 128] for h in range(halves)]

        def load(r):
            if 0 <= r < rows:
                return halved(block[r, ks, :].astype(jnp.float32))
            at = r + 2 if r < 0 else r - rows
            one, other = (beyond, across) if r < 0 else (across, beyond)
            return halved(
                jnp.where(even, one[at, edge, :].astype(jnp.float32), other[at, edge, :].astype(jnp.float32))
            )

        below, here = load(-2), load(-1)
        for r in range(-1, rows + 1):
            above = load(r + 1)
            value = advance(here, below, above, far, r)
            if r == -1:
                value = [jnp.where(meta[1] > 0, v, 0.0) for v in value]
            if r == rows:
                value = [jnp.where(meta[2] > 0, v, 0.0) for v in value]
            for h in range(halves):
                once[r + 1, :, h * 128:(h + 1) * 128] = value[h]
            below, here = here, above
        below, here = halved(once[0]), halved(once[1])
        for r in range(rows):
            above = halved(once[r + 2])
            value = advance(here, below, above, far, r)
            for h in range(halves):
                moved[r, ks, h * 128:(h + 1) * 128] = value[h].astype(jnp.bfloat16)
            below, here = here, above
        return carry

    def piece(i, carry):
        bring(i).wait()
        lax.fori_loop(i * (NF // SUBK), (i + 1) * (NF // SUBK), group, 0)
        leave(i).start()
        return carry

    lax.fori_loop(0, count, piece, 0)

    packed[...] = jnp.zeros_like(packed)
    for r in range(rows):
        window = pl.ds(pl.multiple_of(meta[3 + r], STEP), WINDOW)
        part = jnp.dot(moved[r], onehot[r], preferred_element_type=jnp.float32)
        packed[:, window] += part.astype(jnp.bfloat16)
    me = meta[0]
    for k in range(peers):
        start = pl.multiple_of((me ^ k) * share, 128)
        outs[k][...] = packed[:, pl.ds(start, share)]
    for i in range(count):
        leave(i).wait()
    for copy in gathering:
        copy.wait()


def propagate(meta, held, halos, offset, tails, ae, an, east, north, onehot, moved, x, ready, spots, begin, count, peers):
    rows, _, lon = held.shape
    comps = ae.shape[0]
    share = SEA // peers
    depth = count * NF
    vmem = pl.BlockSpec(memory_space=pltpu.VMEM)
    hbm = pl.BlockSpec(memory_space=pltpu.HBM)
    loose = pl.BlockSpec(memory_space=pl.ANY)
    in_specs = [pl.BlockSpec(memory_space=pltpu.SMEM), loose] + [vmem] * 9 + [loose] * len(ready)
    args = [meta, held, *halos, *tails, ae, an, east, north, onehot, *ready]
    out_specs = [hbm] + [vmem] * peers
    out_shape = [jax.ShapeDtypeStruct((rows, comps, lon), jnp.bfloat16)]
    out_shape += [jax.ShapeDtypeStruct((depth, share), jnp.bfloat16)] * peers
    if ready:
        out_specs.append(vmem)
        out_shape.append(jax.ShapeDtypeStruct((ND * NF, share), jnp.bfloat16))
    aliases = {}
    for buffer, spec, out in ((moved, hbm, 0), (x, vmem, peers + 1)):
        if buffer is not None:
            aliases[len(args)] = out
            in_specs.append(spec)
            args.append(buffer)
    result = pl.pallas_call(
        functools.partial(
            propagate_kernel, peers, share, begin * NF, depth, offset * NF,
            (begin if held.shape[1] == comps else 0) * NF, comps // NF, len(aliases), spots,
        ),
        in_specs=in_specs,
        out_specs=out_specs,
        scratch_shapes=[
            pltpu.VMEM((rows, depth, lon), jnp.bfloat16),
            pltpu.VMEM((rows, depth, lon), jnp.bfloat16),
            pltpu.VMEM((rows + 2, SUBK, lon), jnp.float32),
            pltpu.VMEM((rows + 2, lon), jnp.float32),
            pltpu.VMEM((rows + 2, lon), jnp.float32),
            pltpu.VMEM((depth, SEA), jnp.bfloat16),
            pltpu.SemaphoreType.DMA((count,)),
            pltpu.SemaphoreType.DMA((count,)),
            pltpu.SemaphoreType.DMA((max(len(ready), 1),)),
        ],
        out_shape=out_shape,
        input_output_aliases=aliases,
        compiler_params=params(),
        cost_estimate=cost(2.2 * count),
        name="propagate",
    )(*args)
    return result[0], result[1:peers + 1], result[peers + 1] if ready else None


def collect_kernel(spots, dirs, meta, *rest):
    sem = rest[-1]
    for copy in gather(meta, rest[:len(spots)], spots, dirs, rest[-2], sem):
        copy.wait()


def collect(meta, x, pieces, spots, dirs):
    vmem = pl.BlockSpec(memory_space=pltpu.VMEM)
    return pl.pallas_call(
        functools.partial(collect_kernel, spots, dirs),
        in_specs=[pl.BlockSpec(memory_space=pltpu.SMEM)]
        + [pl.BlockSpec(memory_space=pl.ANY)] * len(pieces)
        + [vmem],
        out_specs=vmem,
        out_shape=jax.ShapeDtypeStruct(x.shape, x.dtype),
        scratch_shapes=[pltpu.SemaphoreType.DMA((len(pieces),))],
        input_output_aliases={1 + len(pieces): 0},
        compiler_params=params(),
        cost_estimate=cost(0.2),
        name="collect",
    )(meta, *pieces, x)


def couple_kernel(peers, dirs, begin, size, spots, meta, w, *rest):
    me = meta[0]
    if spots:
        outs = rest[len(spots) + 1:len(spots) + 1 + peers]
        x, y, sem = rest[-3:]
        for copy in gather(meta, rest[:len(spots)], spots, dirs, x, sem):
            copy.wait()
    else:
        x = rest[0]
        outs = rest[-(peers + 1):-1]
        y = rest[-1]
    coupled = jnp.dot(w[...], x[...], preferred_element_type=jnp.float32)
    for p in range(peers):
        own = x[(p * dirs + begin) * NF:(p * dirs + begin + size) * NF, :].astype(jnp.float32)
        y[p] = (own + own * coupled[p * size * NF:(p + 1) * size * NF]).astype(jnp.bfloat16)
    for k in range(peers):
        outs[k][...] = y[me ^ k]


def couple(meta, w, x, pieces, after, spots, begin, size, peers, dirs):
    share = SEA // peers
    vmem = pl.BlockSpec(memory_space=pltpu.VMEM)
    loose = pl.BlockSpec(memory_space=pl.ANY)
    outs = [jax.ShapeDtypeStruct((size * NF, share), jnp.bfloat16)] * peers
    scratch = [pltpu.VMEM((peers, size * NF, share), jnp.bfloat16)]
    aliases = {}
    if after is None:
        in_specs, args = [loose] * len(pieces) + [vmem], [*pieces, x]
        outs = outs + [jax.ShapeDtypeStruct((ND * NF, share), jnp.bfloat16)]
        scratch.append(pltpu.SemaphoreType.DMA((len(pieces),)))
        aliases = {2 + len(pieces): peers}
    else:
        in_specs, args, spots = [vmem] + [loose] * len(after), [x, *after], ()
    result = pl.pallas_call(
        functools.partial(couple_kernel, peers, dirs, begin, size, spots),
        in_specs=[pl.BlockSpec(memory_space=pltpu.SMEM), vmem] + in_specs,
        out_specs=[vmem] * len(outs),
        out_shape=outs,
        scratch_shapes=scratch,
        input_output_aliases=aliases,
        compiler_params=params(),
        cost_estimate=cost(size),
        name="couple",
    )(meta, w, *args)
    return result[:peers], result[peers] if after is None else x


def finish_kernel(peers, share, begin, group, meta, slot, spread, moved, *rest):
    pieces = rest[:peers]
    out, renewed, old, new, piece_sem, in_sem, out_sem = rest[peers:]
    rows, lon = slot.shape
    depth = renewed.shape[0]
    me = meta[0]
    copies = []
    for k in range(peers):
        start = pl.multiple_of((me ^ k) * share, 128)
        copies.append(pltpu.make_async_copy(pieces[k], renewed.at[:, pl.ds(start, share)], piece_sem.at[k]))
        copies[-1].start()
    far = slice(begin, begin + depth)
    bring, leave = [], []
    for i in range(rows // group):
        part = slice(i * group, (i + 1) * group)
        bring.append(pltpu.make_async_copy(moved.at[part, far, :], old.at[part], in_sem.at[i]))
        leave.append(pltpu.make_async_copy(new.at[part], out.at[part, far, :], out_sem.at[i]))
        bring[-1].start()
    for copy in copies:
        copy.wait()
    for r in range(rows):
        if r % group == 0:
            bring[r // group].wait()
        base = pl.multiple_of(meta[3 + r], STEP)
        value = jnp.dot(renewed[:, pl.ds(base, WINDOW)], spread[r], preferred_element_type=jnp.float32)
        sea = slot[r:r + 1, :] >= 0
        new[r] = jnp.where(sea, value, old[r].astype(jnp.float32)).astype(jnp.bfloat16)
        if r % group == group - 1:
            leave[r // group].start()
    for copy in leave:
        copy.wait()


def finish(meta, slot, spread, moved, pieces, begin, size, peers):
    rows, comps, lon = moved.shape
    share = SEA // peers
    group = 4
    hbm = pl.BlockSpec(memory_space=pltpu.HBM)
    vmem = pl.BlockSpec(memory_space=pltpu.VMEM)
    return pl.pallas_call(
        functools.partial(finish_kernel, peers, share, begin * NF, group),
        in_specs=[pl.BlockSpec(memory_space=pltpu.SMEM), vmem, vmem, hbm]
        + [pl.BlockSpec(memory_space=pl.ANY)] * peers,
        out_specs=hbm,
        out_shape=jax.ShapeDtypeStruct(moved.shape, jnp.bfloat16),
        scratch_shapes=[
            pltpu.VMEM((size * NF, SEA), jnp.bfloat16),
            pltpu.VMEM((rows, size * NF, lon), jnp.bfloat16),
            pltpu.VMEM((rows, size * NF, lon), jnp.bfloat16),
            pltpu.SemaphoreType.DMA((peers,)),
            pltpu.SemaphoreType.DMA((rows // group,)),
            pltpu.SemaphoreType.DMA((rows // group,)),
        ],
        input_output_aliases={3: 0},
        compiler_params=params(),
        cost_estimate=cost(size),
        name="finish",
    )(meta, slot, spread, moved, *pieces)


def swap(array, first):
    count = lax.axis_size("tile")
    pairs = [(i, i + 1) for i in range(first, count - 1, 2)]
    return lax.ppermute(array, "tile", pairs + [(j, i) for i, j in pairs])


def local(action, east_current, north_current, sea_mask, pattern, table):
    rows, comps, lon = action.shape
    peers = lax.axis_size("spec")
    me = lax.axis_index("spec")
    tile = lax.axis_index("tile")
    tiles = lax.axis_size("tile")
    dirs = comps // NF
    parts_out = split_directions(dirs, (4, 4, 4))
    parts_back = split_directions(dirs, (3, 6, 3))

    ahead = parts_out[0] * NF
    parity = (tile % 2).astype(jnp.int32)
    parity = (tile % 2).astype(jnp.int32)
    currents = jnp.stack([east_current, north_current])

    def near_edge(top):
        first = jnp.where(top, rows - 2, 0)
        body = lax.dynamic_slice(action, (first, 0, 0), (2, ahead, lon))
        pair = lax.dynamic_slice(currents, (0, jnp.where(top, rows - 1, 0), 0), (2, 1, lon))[:, 0]
        coarse = lax.reduce_precision(pair, 8, 7)
        tail = jnp.concatenate([coarse, pair - coarse, jnp.zeros((12, lon), jnp.float32)])
        return jnp.concatenate([body, jnp.broadcast_to(tail.astype(jnp.bfloat16), (2, 16, lon))], axis=1)

    near = swap(near_edge(parity == 0), 0), swap(near_edge(parity == 1), 1)

    components = me * comps + jnp.arange(comps, dtype=jnp.int32)
    direction = (components // NF).astype(jnp.float32)
    frequency = (components % NF).astype(jnp.float32)
    speed = courant_scale * jnp.exp(-2.0 * frequency / (NF - 1))
    theta = 2.0 * jnp.pi * direction / ND
    ae = jnp.broadcast_to((speed * jnp.cos(theta))[:, None], (comps, 128))
    an = jnp.broadcast_to((speed * jnp.sin(theta))[:, None], (comps, 128))

    sea = sea_mask > 0
    before = jnp.dot(
        sea.astype(jnp.bfloat16),
        jnp.triu(jnp.ones((lon, lon), jnp.bfloat16), 1),
        preferred_element_type=jnp.float32,
    )
    totals = jnp.sum(sea.astype(jnp.float32), axis=1)
    starts = jnp.sum(
        jnp.where(jnp.tril(jnp.ones((rows, rows), jnp.bool_), -1), totals[None, :], 0.0), axis=1
    )
    slot = jnp.where(sea, (before + starts[:, None]).astype(jnp.int32), -1)
    bases = jnp.minimum(starts.astype(jnp.int32) // STEP * STEP, SEA - WINDOW)
    meta = jnp.concatenate([
        jnp.stack([me, (tile > 0).astype(jnp.int32), (tile < tiles - 1).astype(jnp.int32)]),
        bases,
        parity.reshape(1),
    ]).astype(jnp.int32)
    slot_t = slot.T

    onehot, ae, an, across, beyond = mark(
        meta, slot_t, ae, an, action[rows - 2:, ahead:], action[:2, ahead:]
    )
    far = swap(across, 0), swap(beyond, 1)

    moved, x = None, None
    pieces, spots = [], []
    for j, (begin, count) in enumerate(zip(offsets_of(parts_out), parts_out)):
        offset = begin - parts_out[0] if j else 0
        ready = (pieces[j - 2], tuple(spots[j - 2])) if j >= 2 else ([], ())
        moved, packed, x = propagate(
            meta, action, far if j else near, offset, near, ae, an,
            east_current, north_current, onehot, moved, x, *ready, begin, count, peers,
        )
        pieces.append([packed[0]] + [
            lax.ppermute(packed[k], "spec", [(i, i ^ k) for i in range(peers)])
            for k in range(1, peers)
        ])
        spots.append([(k, begin) for k in range(peers)])

    spread, sel, tt = setup(meta, slot, pattern.T, table, packed[0])
    woven = [
        weave(sel, tt, packed[0], begin, size, peers, dirs)
        for begin, size in zip(offsets_of(parts_back), parts_back)
    ]
    x = collect(meta, x, pieces[-2], tuple(spots[-2]), dirs)
    result = moved
    backs = []
    for g, (begin, size) in enumerate(zip(offsets_of(parts_back), parts_back)):
        after = backs[g - 2][1:] if g >= 2 else renewed[:1] if g else None
        renewed, x = couple(
            meta, woven[g], x, pieces[-1], after, tuple(spots[-1]), begin, size, peers, dirs
        )
        back = [renewed[0]] + [
            lax.ppermute(renewed[k], "spec", [(i, i ^ k) for i in range(peers)])
            for k in range(1, peers)
        ]
        backs.append(back)
        result = finish(meta, slot, spread, result, back, begin, size, peers)
    return result


def solution(mesh):
    return jax.shard_map(
        local,
        mesh=mesh,
        in_specs=(
            P("tile", "spec", None),
            P("tile", None),
            P("tile", None),
            P("tile", None),
            P(),
            P(),
        ),
        out_specs=P("tile", "spec", None),
        check_vma=False,
    )
```

```python
import functools

import jax
import jax.numpy as jnp
from jax import lax
from jax.experimental import pallas as pl
from jax.experimental.pallas import tpu as pltpu
from jax.sharding import PartitionSpec as P

NF = 64
ND = 48
SEA = 2048
WINDOW = 512
STEP = 256
SUBK = 16
courant_scale = 0.45
MIB = 1024 * 1024


def split_directions(count, sizes):
    if sum(sizes) == count:
        return sizes
    return (1,) * count


def offsets_of(sizes):
    return [sum(sizes[:i]) for i in range(len(sizes))]


def cost(us):
    return pl.CostEstimate(
        flops=int(us * 1.15e9), bytes_accessed=int(us * 3e6), transcendentals=0
    )


def params(mib=16):
    return pltpu.CompilerParams(vmem_limit_bytes=mib * MIB)


def mark_kernel(rows, meta, slot_t, ae, an, top, bottom, onehot, ae_out, an_out, across, beyond):
    even = meta[3 + rows] == 0

    @pl.when(even)
    def rising():
        across[...] = top[...]
        beyond[...] = bottom[...]

    @pl.when(jnp.logical_not(even))
    def falling():
        across[...] = bottom[...]
        beyond[...] = top[...]

    ae_out[...] = jnp.broadcast_to(ae[...], ae_out.shape)
    an_out[...] = jnp.broadcast_to(an[...], an_out.shape)
    lanes = lax.broadcasted_iota(jnp.int32, onehot.shape[1:], 1)
    for r in range(rows):
        onehot[r] = jnp.where(slot_t[:, r:r + 1] - meta[3 + r] == lanes, 1.0, 0.0).astype(jnp.bfloat16)


def mark(meta, slot_t, ae, an, top, bottom):
    lon, rows = slot_t.shape
    vmem = pl.BlockSpec(memory_space=pltpu.VMEM)
    return pl.pallas_call(
        functools.partial(mark_kernel, rows),
        in_specs=[pl.BlockSpec(memory_space=pltpu.SMEM)] + [vmem] * 5,
        out_specs=[vmem] * 5,
        out_shape=[
            jax.ShapeDtypeStruct((rows, lon, WINDOW), jnp.bfloat16),
            jax.ShapeDtypeStruct(ae.shape, ae.dtype),
            jax.ShapeDtypeStruct(an.shape, an.dtype),
            jax.ShapeDtypeStruct(top.shape, top.dtype),
            jax.ShapeDtypeStruct(top.shape, top.dtype),
        ],
        compiler_params=params(),
        cost_estimate=cost(4),
        name="mark",
    )(meta, slot_t, ae, an, top, bottom)


def setup_kernel(rows, meta, slot, pattern_t, table, after, spread, sel, tt):
    lon = slot.shape[1]
    depths = lax.broadcasted_iota(jnp.int32, (WINDOW, lon), 0)
    for r in range(rows):
        spread[r] = jnp.where(slot[r:r + 1, :] - meta[3 + r] == depths, 1.0, 0.0).astype(jnp.bfloat16)
    target = lax.broadcasted_iota(jnp.int32, (128, ND), 0)
    hit = pattern_t[0:1, :] == target
    for j in range(1, pattern_t.shape[0]):
        hit = hit | (pattern_t[j:j + 1, :] == target)
    chosen = jnp.where(hit, 1.0, 0.0).astype(jnp.bfloat16)
    block = lax.broadcasted_iota(jnp.int32, (128, ND * NF), 1) // NF
    owner = lax.broadcasted_iota(jnp.int32, (128, ND * NF), 0)
    widen = jnp.where(block == owner, 1.0, 0.0).astype(jnp.bfloat16)
    sel[...] = lax.dot_general(
        chosen, widen, (((0,), (0,)), ((), ())), preferred_element_type=jnp.float32
    )
    for odd in range(2):
        for t in range(ND // 2):
            pair = jnp.concatenate(
                [table[2 * t + odd].astype(jnp.float32), table[(2 * t + odd + 1) % ND].astype(jnp.float32)],
                axis=1,
            ).astype(jnp.bfloat16)
            tt[odd, :, t * 128:(t + 1) * 128] = pair
            tt[odd, :, ND * NF + t * 128:ND * NF + (t + 1) * 128] = pair


def setup(meta, slot, pattern_t, table, after):
    rows, lon = slot.shape
    vmem = pl.BlockSpec(memory_space=pltpu.VMEM)
    return pl.pallas_call(
        functools.partial(setup_kernel, rows),
        in_specs=[pl.BlockSpec(memory_space=pltpu.SMEM)] + [vmem] * 3 + [pl.BlockSpec(memory_space=pl.ANY)],
        out_specs=[vmem] * 3,
        out_shape=[
            jax.ShapeDtypeStruct((rows, WINDOW, lon), jnp.bfloat16),
            jax.ShapeDtypeStruct((ND, ND * NF), jnp.float32),
            jax.ShapeDtypeStruct((2, NF, 2 * ND * NF), jnp.bfloat16),
        ],
        compiler_params=params(),
        cost_estimate=cost(0.2),
        name="setup",
    )(meta, slot, pattern_t, table, after)


def weave_kernel(peers, dirs, begin, size, sel, tt, after, w):
    def strip(i, carry):
        r = i // size * dirs + begin + i % size
        turn = lax.rem(ND - r, ND)
        lanes = pl.ds(pl.multiple_of((turn // 2) * 128, 128), ND * NF)
        keep = jnp.broadcast_to(sel[pl.ds(r, 1), :], (16, ND * NF)).astype(jnp.bfloat16)
        for q in range(NF // 16):
            w[pl.ds(pl.multiple_of(i * NF + q * 16, 16), 16), :] = tt[turn % 2, pl.ds(q * 16, 16), lanes] * keep
        return carry

    lax.fori_loop(0, peers * size, strip, 0)


def weave(sel, tt, after, begin, size, peers, dirs):
    vmem = pl.BlockSpec(memory_space=pltpu.VMEM)
    return pl.pallas_call(
        functools.partial(weave_kernel, peers, dirs, begin, size),
        in_specs=[vmem, vmem, pl.BlockSpec(memory_space=pl.ANY)],
        out_specs=vmem,
        out_shape=jax.ShapeDtypeStruct((peers * size * NF, ND * NF), jnp.bfloat16),
        compiler_params=params(),
        cost_estimate=cost(0.1),
        name="weave",
    )(sel, tt, after)


def gather(meta, pieces, spots, dirs, x, sem):
    copies = []
    for i, (k, first) in enumerate(spots):
        depth = pieces[i].shape[0]
        start = pl.multiple_of(((meta[0] ^ k) * dirs + first) * NF, NF)
        copies.append(pltpu.make_async_copy(pieces[i], x.at[pl.ds(start, depth), :], sem.at[i]))
        copies[-1].start()
    return copies


def propagate_kernel(peers, share, begin, depth, offset, source, dirs, aliased, spots, meta, act, across, beyond,
                     across_tail, beyond_tail, ae_ref, an_ref, east, north, onehot, *rest):
    rows, _, lon = act.shape
    ready = rest[:len(spots)]
    rest = rest[len(spots) + aliased:]
    even = meta[3 + rows] == 0
    moved_out = rest[0]
    outs = rest[1:peers + 1]
    block, moved, once, be_ref, bn_ref, packed, in_sem, out_sem, x_sem = rest[-9:]
    count = depth // NF
    halves = lon // 128
    lane = lax.broadcasted_iota(jnp.int32, (SUBK, 128), 1)
    first = lane == 0
    last = lane == 127

    def bring(i):
        part = pl.ds(pl.multiple_of(i * NF, NF), NF)
        there = pl.ds(pl.multiple_of(source + i * NF, NF), NF)
        return pltpu.make_async_copy(act.at[:, there, :], block.at[:, part, :], in_sem.at[i])

    def leave(i):
        part = pl.ds(pl.multiple_of(i * NF, NF), NF)
        far = pl.ds(pl.multiple_of(begin + i * NF, NF), NF)
        return pltpu.make_async_copy(moved.at[:, part, :], moved_out.at[:, far, :], out_sem.at[i])

    for i in range(count):
        bring(i).start()
    gathering = gather(meta, ready, spots, dirs, rest[peers + 1], x_sem)
    for n, (own, b_ref) in enumerate(((east, be_ref), (north, bn_ref))):
        for at, one, other in ((0, beyond_tail, across_tail), (rows + 1, across_tail, beyond_tail)):
            tails = [t[0, t.shape[1] - 16:, :].astype(jnp.float32) for t in (one, other)]
            ends = jnp.where(even, tails[0], tails[1])
            b_ref[at:at + 1, :] = courant_scale * (ends[n:n + 1, :] + ends[n + 2:n + 3, :])
        b_ref[1:rows + 1, :] = courant_scale * own[...]

    def advance(center, south, north_of, far, r):
        ae = ae_ref[far, :]
        an = an_ref[far, :]
        right = [pltpu.roll(c, 1, 1) for c in center]
        left = [pltpu.roll(c, 127, 1) for c in center]
        result = []
        for h in range(halves):
            ce = ae + be_ref[r + 1:r + 2, h * 128:(h + 1) * 128]
            cn = an + bn_ref[r + 1:r + 2, h * 128:(h + 1) * 128]
            west = jnp.where(first, right[h - 1] if h else 0.0, right[h])
            east_of = jnp.where(last, left[h + 1] if h < halves - 1 else 0.0, left[h])
            along = jnp.where(ce > 0.0, west, east_of)
            across = jnp.where(cn > 0.0, south[h], north_of[h])
            c = center[h]
            result.append(c - jnp.abs(ce) * (c - along) - jnp.abs(cn) * (c - across))
        return result

    def group(g, carry):
        ks = pl.ds(pl.multiple_of(g * SUBK, SUBK), SUBK)
        far = pl.ds(pl.multiple_of(begin + g * SUBK, SUBK), SUBK)
        edge = pl.ds(pl.multiple_of(offset + g * SUBK, SUBK), SUBK)

        def halved(value):
            return [value[:, h * 128:(h + 1) * 128] for h in range(halves)]

        def load(r):
            if 0 <= r < rows:
                return halved(block[r, ks, :].astype(jnp.float32))
            at = r + 2 if r < 0 else r - rows
            one, other = (beyond, across) if r < 0 else (across, beyond)
            return halved(
                jnp.where(even, one[at, edge, :].astype(jnp.float32), other[at, edge, :].astype(jnp.float32))
            )

        below, here = load(-2), load(-1)
        for r in range(-1, rows + 1):
            above = load(r + 1)
            value = advance(here, below, above, far, r)
            if r == -1:
                value = [jnp.where(meta[1] > 0, v, 0.0) for v in value]
            if r == rows:
                value = [jnp.where(meta[2] > 0, v, 0.0) for v in value]
            for h in range(halves):
                once[r + 1, :, h * 128:(h + 1) * 128] = value[h]
            below, here = here, above
        below, here = halved(once[0]), halved(once[1])
        for r in range(rows):
            above = halved(once[r + 2])
            value = advance(here, below, above, far, r)
            for h in range(halves):
                moved[r, ks, h * 128:(h + 1) * 128] = value[h].astype(jnp.bfloat16)
            below, here = here, above
        return carry

    def piece(i, carry):
        bring(i).wait()
        lax.fori_loop(i * (NF // SUBK), (i + 1) * (NF // SUBK), group, 0)
        leave(i).start()
        return carry

    lax.fori_loop(0, count, piece, 0)

    packed[...] = jnp.zeros_like(packed)
    for r in range(rows):
        window = pl.ds(pl.multiple_of(meta[3 + r], STEP), WINDOW)
        part = jnp.dot(moved[r], onehot[r], preferred_element_type=jnp.float32)
        packed[:, window] += part.astype(jnp.bfloat16)
    me = meta[0]
    for k in range(peers):
        start = pl.multiple_of((me ^ k) * share, 128)
        outs[k][...] = packed[:, pl.ds(start, share)]
    for i in range(count):
        leave(i).wait()
    for copy in gathering:
        copy.wait()


def propagate(meta, held, halos, offset, tails, ae, an, east, north, onehot, moved, x, ready, spots, begin, count, peers):
    rows, _, lon = held.shape
    comps = ae.shape[0]
    share = SEA // peers
    depth = count * NF
    vmem = pl.BlockSpec(memory_space=pltpu.VMEM)
    hbm = pl.BlockSpec(memory_space=pltpu.HBM)
    loose = pl.BlockSpec(memory_space=pl.ANY)
    in_specs = [pl.BlockSpec(memory_space=pltpu.SMEM), loose] + [vmem] * 9 + [loose] * len(ready)
    args = [meta, held, *halos, *tails, ae, an, east, north, onehot, *ready]
    out_specs = [hbm] + [vmem] * peers
    out_shape = [jax.ShapeDtypeStruct((rows, comps, lon), jnp.bfloat16)]
    out_shape += [jax.ShapeDtypeStruct((depth, share), jnp.bfloat16)] * peers
    if ready:
        out_specs.append(vmem)
        out_shape.append(jax.ShapeDtypeStruct((ND * NF, share), jnp.bfloat16))
    aliases = {}
    for buffer, spec, out in ((moved, hbm, 0), (x, vmem, peers + 1)):
        if buffer is not None:
            aliases[len(args)] = out
            in_specs.append(spec)
            args.append(buffer)
    result = pl.pallas_call(
        functools.partial(
            propagate_kernel, peers, share, begin * NF, depth, offset * NF,
            (begin if held.shape[1] == comps else 0) * NF, comps // NF, len(aliases), spots,
        ),
        in_specs=in_specs,
        out_specs=out_specs,
        scratch_shapes=[
            pltpu.VMEM((rows, depth, lon), jnp.bfloat16),
            pltpu.VMEM((rows, depth, lon), jnp.bfloat16),
            pltpu.VMEM((rows + 2, SUBK, lon), jnp.float32),
            pltpu.VMEM((rows + 2, lon), jnp.float32),
            pltpu.VMEM((rows + 2, lon), jnp.float32),
            pltpu.VMEM((depth, SEA), jnp.bfloat16),
            pltpu.SemaphoreType.DMA((count,)),
            pltpu.SemaphoreType.DMA((count,)),
            pltpu.SemaphoreType.DMA((max(len(ready), 1),)),
        ],
        out_shape=out_shape,
        input_output_aliases=aliases,
        compiler_params=params(),
        cost_estimate=cost(2.2 * count),
        name="propagate",
    )(*args)
    return result[0], result[1:peers + 1], result[peers + 1] if ready else None


def collect_kernel(spots, dirs, meta, *rest):
    sem = rest[-1]
    for copy in gather(meta, rest[:len(spots)], spots, dirs, rest[-2], sem):
        copy.wait()


def collect(meta, x, pieces, spots, dirs, after=()):
    vmem = pl.BlockSpec(memory_space=pltpu.VMEM)
    return pl.pallas_call(
        functools.partial(collect_kernel, spots, dirs),
        in_specs=[pl.BlockSpec(memory_space=pltpu.SMEM)]
        + [pl.BlockSpec(memory_space=pl.ANY)] * (len(pieces) + len(after))
        + [vmem],
        out_specs=vmem,
        out_shape=jax.ShapeDtypeStruct(x.shape, x.dtype),
        scratch_shapes=[pltpu.SemaphoreType.DMA((len(pieces),))],
        input_output_aliases={1 + len(pieces) + len(after): 0},
        compiler_params=params(),
        cost_estimate=cost(0.2),
        name="collect",
    )(meta, *pieces, *after, x)


def couple_kernel(peers, dirs, begin, size, spots, meta, w, *rest):
    me = meta[0]
    if spots:
        outs = rest[len(spots) + 1:len(spots) + 1 + peers]
        x, y, sem = rest[-3:]
        for copy in gather(meta, rest[:len(spots)], spots, dirs, x, sem):
            copy.wait()
    else:
        x = rest[0]
        outs = rest[-(peers + 1):-1]
        y = rest[-1]
    coupled = jnp.dot(w[...], x[...], preferred_element_type=jnp.float32)
    for p in range(peers):
        own = x[(p * dirs + begin) * NF:(p * dirs + begin + size) * NF, :].astype(jnp.float32)
        y[p] = (own + own * coupled[p * size * NF:(p + 1) * size * NF]).astype(jnp.bfloat16)
    for k in range(peers):
        outs[k][...] = y[me ^ k]


def couple(meta, w, x, pieces, after, spots, begin, size, peers, dirs):
    share = SEA // peers
    vmem = pl.BlockSpec(memory_space=pltpu.VMEM)
    loose = pl.BlockSpec(memory_space=pl.ANY)
    outs = [jax.ShapeDtypeStruct((size * NF, share), jnp.bfloat16)] * peers
    scratch = [pltpu.VMEM((peers, size * NF, share), jnp.bfloat16)]
    aliases = {}
    if after is None:
        in_specs, args = [loose] * len(pieces) + [vmem], [*pieces, x]
        outs = outs + [jax.ShapeDtypeStruct((ND * NF, share), jnp.bfloat16)]
        scratch.append(pltpu.SemaphoreType.DMA((len(pieces),)))
        aliases = {2 + len(pieces): peers}
    else:
        in_specs, args, spots = [vmem] + [loose] * len(after), [x, *after], ()
    result = pl.pallas_call(
        functools.partial(couple_kernel, peers, dirs, begin, size, spots),
        in_specs=[pl.BlockSpec(memory_space=pltpu.SMEM), vmem] + in_specs,
        out_specs=[vmem] * len(outs),
        out_shape=outs,
        scratch_shapes=scratch,
        input_output_aliases=aliases,
        compiler_params=params(),
        cost_estimate=cost(size),
        name="couple",
    )(meta, w, *args)
    return result[:peers], result[peers] if after is None else x


def columns_of(meta, k, first, depth, dirs):
    return pl.ds(pl.multiple_of(((meta[0] ^ k) * dirs + first) * NF, 128), depth)


def begin_kernel(dirs, spots, meta, w, *rest):
    total = rest[-1]
    for i, (k, first) in enumerate(spots):
        piece = rest[i]
        part = jnp.dot(
            w[:, columns_of(meta, k, first, piece.shape[0], dirs)], piece[...],
            preferred_element_type=jnp.float32,
        )
        if i:
            total[...] += part
        else:
            total[...] = part


def begin_couple(meta, w, pieces, spots, dirs):
    vmem = pl.BlockSpec(memory_space=pltpu.VMEM)
    return pl.pallas_call(
        functools.partial(begin_kernel, dirs, spots),
        in_specs=[pl.BlockSpec(memory_space=pltpu.SMEM)] + [vmem] * (1 + len(pieces)),
        out_specs=vmem,
        out_shape=jax.ShapeDtypeStruct((w.shape[0], pieces[0].shape[1]), jnp.float32),
        compiler_params=params(),
        cost_estimate=cost(0.2),
        name="begin_couple",
    )(meta, w, *pieces)


def end_kernel(peers, dirs, size, spots, meta, w, partial, *rest):
    owns, pieces, outs, total = rest[:peers], rest[peers:2 * peers], rest[2 * peers:-1], rest[-1]
    coupled = partial[...]
    for i, (k, first) in enumerate(spots):
        coupled += jnp.dot(
            w[:, columns_of(meta, k, first, pieces[i].shape[0], dirs)], pieces[i][...],
            preferred_element_type=jnp.float32,
        )
    for p in range(peers):
        total[p] = coupled[p * size * NF:(p + 1) * size * NF]
    for k in range(peers):
        own = owns[k][:size * NF, :].astype(jnp.float32)
        outs[k][...] = (own + own * total[meta[0] ^ k]).astype(jnp.bfloat16)


def end_couple(meta, w, partial, owns, pieces, spots, size, peers, dirs):
    vmem = pl.BlockSpec(memory_space=pltpu.VMEM)
    share = SEA // peers
    return pl.pallas_call(
        functools.partial(end_kernel, peers, dirs, size, spots),
        in_specs=[pl.BlockSpec(memory_space=pltpu.SMEM)] + [vmem] * (2 + 2 * peers),
        out_specs=[vmem] * peers,
        out_shape=[jax.ShapeDtypeStruct((size * NF, share), jnp.bfloat16)] * peers,
        scratch_shapes=[pltpu.VMEM((peers, size * NF, share), jnp.float32)],
        compiler_params=params(),
        cost_estimate=cost(2),
        name="end_couple",
    )(meta, w, partial, *owns, *pieces)


def finish_kernel(peers, share, begin, group, meta, slot, spread, moved, *rest):
    pieces = rest[:peers]
    out, renewed, old, new, piece_sem, in_sem, out_sem = rest[peers:]
    rows, lon = slot.shape
    depth = renewed.shape[0]
    me = meta[0]
    copies = []
    for k in range(peers):
        start = pl.multiple_of((me ^ k) * share, 128)
        copies.append(pltpu.make_async_copy(pieces[k], renewed.at[:, pl.ds(start, share)], piece_sem.at[k]))
        copies[-1].start()
    far = slice(begin, begin + depth)
    bring, leave = [], []
    for i in range(rows // group):
        part = slice(i * group, (i + 1) * group)
        bring.append(pltpu.make_async_copy(moved.at[part, far, :], old.at[part], in_sem.at[i]))
        leave.append(pltpu.make_async_copy(new.at[part], out.at[part, far, :], out_sem.at[i]))
        bring[-1].start()
    for copy in copies:
        copy.wait()
    for r in range(rows):
        if r % group == 0:
            bring[r // group].wait()
        base = pl.multiple_of(meta[3 + r], STEP)
        value = jnp.dot(renewed[:, pl.ds(base, WINDOW)], spread[r], preferred_element_type=jnp.float32)
        sea = slot[r:r + 1, :] >= 0
        new[r] = jnp.where(sea, value, old[r].astype(jnp.float32)).astype(jnp.bfloat16)
        if r % group == group - 1:
            leave[r // group].start()
    for copy in leave:
        copy.wait()


def finish(meta, slot, spread, moved, pieces, begin, size, peers):
    rows, comps, lon = moved.shape
    share = SEA // peers
    group = 4
    hbm = pl.BlockSpec(memory_space=pltpu.HBM)
    vmem = pl.BlockSpec(memory_space=pltpu.VMEM)
    return pl.pallas_call(
        functools.partial(finish_kernel, peers, share, begin * NF, group),
        in_specs=[pl.BlockSpec(memory_space=pltpu.SMEM), vmem, vmem, hbm]
        + [pl.BlockSpec(memory_space=pl.ANY)] * peers,
        out_specs=hbm,
        out_shape=jax.ShapeDtypeStruct(moved.shape, jnp.bfloat16),
        scratch_shapes=[
            pltpu.VMEM((size * NF, SEA), jnp.bfloat16),
            pltpu.VMEM((rows, size * NF, lon), jnp.bfloat16),
            pltpu.VMEM((rows, size * NF, lon), jnp.bfloat16),
            pltpu.SemaphoreType.DMA((peers,)),
            pltpu.SemaphoreType.DMA((rows // group,)),
            pltpu.SemaphoreType.DMA((rows // group,)),
        ],
        input_output_aliases={3: 0},
        compiler_params=params(),
        cost_estimate=cost(size),
        name="finish",
    )(meta, slot, spread, moved, *pieces)


def swap(array, first):
    count = lax.axis_size("tile")
    pairs = [(i, i + 1) for i in range(first, count - 1, 2)]
    return lax.ppermute(array, "tile", pairs + [(j, i) for i, j in pairs])


def local(action, east_current, north_current, sea_mask, pattern, table):
    rows, comps, lon = action.shape
    peers = lax.axis_size("spec")
    me = lax.axis_index("spec")
    tile = lax.axis_index("tile")
    tiles = lax.axis_size("tile")
    dirs = comps // NF
    parts_out = split_directions(dirs, (4, 4, 4))
    parts_back = split_directions(dirs, (3, 6, 3))

    ahead = parts_out[0] * NF
    parity = (tile % 2).astype(jnp.int32)
    parity = (tile % 2).astype(jnp.int32)
    currents = jnp.stack([east_current, north_current])

    def near_edge(top):
        first = jnp.where(top, rows - 2, 0)
        body = lax.dynamic_slice(action, (first, 0, 0), (2, ahead, lon))
        pair = lax.dynamic_slice(currents, (0, jnp.where(top, rows - 1, 0), 0), (2, 1, lon))[:, 0]
        coarse = lax.reduce_precision(pair, 8, 7)
        tail = jnp.concatenate([coarse, pair - coarse, jnp.zeros((12, lon), jnp.float32)])
        return jnp.concatenate([body, jnp.broadcast_to(tail.astype(jnp.bfloat16), (2, 16, lon))], axis=1)

    near = swap(near_edge(parity == 0), 0), swap(near_edge(parity == 1), 1)

    components = me * comps + jnp.arange(comps, dtype=jnp.int32)
    direction = (components // NF).astype(jnp.float32)
    frequency = (components % NF).astype(jnp.float32)
    speed = courant_scale * jnp.exp(-2.0 * frequency / (NF - 1))
    theta = 2.0 * jnp.pi * direction / ND
    ae = jnp.broadcast_to((speed * jnp.cos(theta))[:, None], (comps, 128))
    an = jnp.broadcast_to((speed * jnp.sin(theta))[:, None], (comps, 128))

    sea = sea_mask > 0
    before = jnp.dot(
        sea.astype(jnp.bfloat16),
        jnp.triu(jnp.ones((lon, lon), jnp.bfloat16), 1),
        preferred_element_type=jnp.float32,
    )
    totals = jnp.sum(sea.astype(jnp.float32), axis=1)
    starts = jnp.sum(
        jnp.where(jnp.tril(jnp.ones((rows, rows), jnp.bool_), -1), totals[None, :], 0.0), axis=1
    )
    slot = jnp.where(sea, (before + starts[:, None]).astype(jnp.int32), -1)
    bases = jnp.minimum(starts.astype(jnp.int32) // STEP * STEP, SEA - WINDOW)
    meta = jnp.concatenate([
        jnp.stack([me, (tile > 0).astype(jnp.int32), (tile < tiles - 1).astype(jnp.int32)]),
        bases,
        parity.reshape(1),
    ]).astype(jnp.int32)
    slot_t = slot.T

    onehot, ae, an, across, beyond = mark(
        meta, slot_t, ae, an, action[rows - 2:, ahead:], action[:2, ahead:]
    )
    far = swap(across, 0), swap(beyond, 1)

    moved, x = None, None
    pieces, spots = [], []
    for j, (begin, count) in enumerate(zip(offsets_of(parts_out), parts_out)):
        offset = begin - parts_out[0] if j else 0
        ready = (pieces[j - 2], tuple(spots[j - 2])) if j >= 2 else ([], ())
        moved, packed, x = propagate(
            meta, action, far if j else near, offset, near, ae, an,
            east_current, north_current, onehot, moved, x, *ready, begin, count, peers,
        )
        pieces.append([packed[0]] + [
            lax.ppermute(packed[k], "spec", [(i, i ^ k) for i in range(peers)])
            for k in range(1, peers)
        ])
        spots.append([(k, begin) for k in range(peers)])

    spread, sel, tt = setup(meta, slot, pattern.T, table, packed[0])
    woven = [
        weave(sel, tt, packed[0], begin, size, peers, dirs)
        for begin, size in zip(offsets_of(parts_back), parts_back)
    ]
    x = collect(meta, x, pieces[-2], tuple(spots[-2]), dirs)
    early = comps % 128 == 0 and parts_back[0] <= parts_out[0]
    early = early and all(size * NF % 128 == 0 for size in parts_out)
    if early:
        ahead_pieces = [piece for part in pieces[:-1] for piece in part]
        ahead_spots = tuple(spot for part in spots[:-1] for spot in part)
        partial = begin_couple(meta, woven[0], ahead_pieces, ahead_spots, dirs)
    result = moved
    backs = []
    for g, (begin, size) in enumerate(zip(offsets_of(parts_back), parts_back)):
        after = backs[g - 2][1:] if g >= 2 else renewed[:1] if g else None
        if early and g == 0:
            renewed = end_couple(
                meta, woven[0], partial, pieces[0], pieces[-1], tuple(spots[-1]), size, peers, dirs
            )
            x = collect(meta, x, pieces[-1], tuple(spots[-1]), dirs, tuple(renewed[:1]))
        else:
            renewed, x = couple(
                meta, woven[g], x, pieces[-1], after, tuple(spots[-1]), begin, size, peers, dirs
            )
        back = [renewed[0]] + [
            lax.ppermute(renewed[k], "spec", [(i, i ^ k) for i in range(peers)])
            for k in range(1, peers)
        ]
        backs.append(back)
        result = finish(meta, slot, spread, result, back, begin, size, peers)
    return result


def solution(mesh):
    return jax.shard_map(
        local,
        mesh=mesh,
        in_specs=(
            P("tile", "spec", None),
            P("tile", None),
            P("tile", None),
            P("tile", None),
            P(),
            P(),
        ),
        out_specs=P("tile", "spec", None),
        check_vma=False,
    )
```

```python
import functools

import jax
import jax.numpy as jnp
from jax import lax
from jax.experimental import pallas as pl
from jax.experimental.pallas import tpu as pltpu
from jax.sharding import PartitionSpec as P

NF = 64
ND = 48
SEA = 2048
WINDOW = 512
STEP = 256
SUBK = 32
courant_scale = 0.45
MIB = 1024 * 1024


def split_directions(count, sizes):
    if sum(sizes) == count:
        return sizes
    return (1,) * count


def offsets_of(sizes):
    return [sum(sizes[:i]) for i in range(len(sizes))]


def cost(us):
    return pl.CostEstimate(
        flops=int(us * 1.15e9), bytes_accessed=int(us * 3e6), transcendentals=0
    )


def params(mib=16):
    return pltpu.CompilerParams(vmem_limit_bytes=mib * MIB)


def mark_kernel(rows, meta, slot_t, ae, an, top, bottom, onehot, ae_out, an_out, across, beyond):
    even = meta[3 + rows] == 0

    @pl.when(even)
    def rising():
        across[...] = top[...]
        beyond[...] = bottom[...]

    @pl.when(jnp.logical_not(even))
    def falling():
        across[...] = bottom[...]
        beyond[...] = top[...]

    ae_out[...] = jnp.broadcast_to(ae[...], ae_out.shape)
    an_out[...] = jnp.broadcast_to(an[...], an_out.shape)
    lanes = lax.broadcasted_iota(jnp.int32, onehot.shape[1:], 1)
    for r in range(rows):
        onehot[r] = jnp.where(slot_t[:, r:r + 1] - meta[3 + r] == lanes, 1.0, 0.0).astype(jnp.bfloat16)


def mark(meta, slot_t, ae, an, top, bottom):
    lon, rows = slot_t.shape
    vmem = pl.BlockSpec(memory_space=pltpu.VMEM)
    return pl.pallas_call(
        functools.partial(mark_kernel, rows),
        in_specs=[pl.BlockSpec(memory_space=pltpu.SMEM)] + [vmem] * 5,
        out_specs=[vmem] * 5,
        out_shape=[
            jax.ShapeDtypeStruct((rows, lon, WINDOW), jnp.bfloat16),
            jax.ShapeDtypeStruct(ae.shape, ae.dtype),
            jax.ShapeDtypeStruct(an.shape, an.dtype),
            jax.ShapeDtypeStruct(top.shape, top.dtype),
            jax.ShapeDtypeStruct(top.shape, top.dtype),
        ],
        compiler_params=params(),
        cost_estimate=cost(4),
        name="mark",
    )(meta, slot_t, ae, an, top, bottom)


def setup_kernel(rows, meta, slot, pattern_t, table, after, spread, sel, tt):
    lon = slot.shape[1]
    depths = lax.broadcasted_iota(jnp.int32, (WINDOW, lon), 0)
    for r in range(rows):
        spread[r] = jnp.where(slot[r:r + 1, :] - meta[3 + r] == depths, 1.0, 0.0).astype(jnp.bfloat16)
    target = lax.broadcasted_iota(jnp.int32, (128, ND), 0)
    hit = pattern_t[0:1, :] == target
    for j in range(1, pattern_t.shape[0]):
        hit = hit | (pattern_t[j:j + 1, :] == target)
    chosen = jnp.where(hit, 1.0, 0.0).astype(jnp.bfloat16)
    block = lax.broadcasted_iota(jnp.int32, (128, ND * NF), 1) // NF
    owner = lax.broadcasted_iota(jnp.int32, (128, ND * NF), 0)
    widen = jnp.where(block == owner, 1.0, 0.0).astype(jnp.bfloat16)
    sel[...] = lax.dot_general(
        chosen, widen, (((0,), (0,)), ((), ())), preferred_element_type=jnp.float32
    )
    for odd in range(2):
        for t in range(ND // 2):
            pair = jnp.concatenate(
                [table[2 * t + odd].astype(jnp.float32), table[(2 * t + odd + 1) % ND].astype(jnp.float32)],
                axis=1,
            ).astype(jnp.bfloat16)
            tt[odd, :, t * 128:(t + 1) * 128] = pair
            tt[odd, :, ND * NF + t * 128:ND * NF + (t + 1) * 128] = pair


def setup(meta, slot, pattern_t, table, after):
    rows, lon = slot.shape
    vmem = pl.BlockSpec(memory_space=pltpu.VMEM)
    return pl.pallas_call(
        functools.partial(setup_kernel, rows),
        in_specs=[pl.BlockSpec(memory_space=pltpu.SMEM)] + [vmem] * 3 + [pl.BlockSpec(memory_space=pl.ANY)],
        out_specs=[vmem] * 3,
        out_shape=[
            jax.ShapeDtypeStruct((rows, WINDOW, lon), jnp.bfloat16),
            jax.ShapeDtypeStruct((ND, ND * NF), jnp.float32),
            jax.ShapeDtypeStruct((2, NF, 2 * ND * NF), jnp.bfloat16),
        ],
        compiler_params=params(),
        cost_estimate=cost(0.2),
        name="setup",
    )(meta, slot, pattern_t, table, after)


def weave_kernel(peers, dirs, begin, size, sel, tt, after, w):
    def strip(i, carry):
        r = i // size * dirs + begin + i % size
        turn = lax.rem(ND - r, ND)
        lanes = pl.ds(pl.multiple_of((turn // 2) * 128, 128), ND * NF)
        keep = jnp.broadcast_to(sel[pl.ds(r, 1), :], (16, ND * NF)).astype(jnp.bfloat16)
        for q in range(NF // 16):
            w[pl.ds(pl.multiple_of(i * NF + q * 16, 16), 16), :] = tt[turn % 2, pl.ds(q * 16, 16), lanes] * keep
        return carry

    lax.fori_loop(0, peers * size, strip, 0)


def weave(sel, tt, after, begin, size, peers, dirs):
    vmem = pl.BlockSpec(memory_space=pltpu.VMEM)
    return pl.pallas_call(
        functools.partial(weave_kernel, peers, dirs, begin, size),
        in_specs=[vmem, vmem, pl.BlockSpec(memory_space=pl.ANY)],
        out_specs=vmem,
        out_shape=jax.ShapeDtypeStruct((peers * size * NF, ND * NF), jnp.bfloat16),
        compiler_params=params(),
        cost_estimate=cost(0.1),
        name="weave",
    )(sel, tt, after)


def gather(meta, pieces, spots, dirs, x, sem):
    copies = []
    for i, (k, first) in enumerate(spots):
        depth = pieces[i].shape[0]
        start = pl.multiple_of(((meta[0] ^ k) * dirs + first) * NF, NF)
        copies.append(pltpu.make_async_copy(pieces[i], x.at[pl.ds(start, depth), :], sem.at[i]))
        copies[-1].start()
    return copies


def propagate_kernel(peers, share, begin, depth, offset, source, dirs, aliased, spots, meta, act, across, beyond,
                     across_tail, beyond_tail, ae_ref, an_ref, east, north, onehot, *rest):
    rows, _, lon = act.shape
    ready = rest[:len(spots)]
    rest = rest[len(spots) + aliased:]
    even = meta[3 + rows] == 0
    moved_out = rest[0]
    outs = rest[1:peers + 1]
    block, moved, once, be_ref, bn_ref, packed, in_sem, out_sem, x_sem = rest[-9:]
    count = depth // NF
    halves = lon // 128
    lane = lax.broadcasted_iota(jnp.int32, (SUBK, 128), 1)
    first = lane == 0
    last = lane == 127

    def bring(i):
        part = pl.ds(pl.multiple_of(i * NF, NF), NF)
        there = pl.ds(pl.multiple_of(source + i * NF, NF), NF)
        return pltpu.make_async_copy(act.at[:, there, :], block.at[:, part, :], in_sem.at[i])

    def leave(i):
        part = pl.ds(pl.multiple_of(i * NF, NF), NF)
        far = pl.ds(pl.multiple_of(begin + i * NF, NF), NF)
        return pltpu.make_async_copy(moved.at[:, part, :], moved_out.at[:, far, :], out_sem.at[i])

    for i in range(count):
        bring(i).start()
    gathering = gather(meta, ready, spots, dirs, rest[peers + 1], x_sem)
    for n, (own, b_ref) in enumerate(((east, be_ref), (north, bn_ref))):
        for at, one, other in ((0, beyond_tail, across_tail), (rows + 1, across_tail, beyond_tail)):
            tails = [t[0, t.shape[1] - 16:, :].astype(jnp.float32) for t in (one, other)]
            ends = jnp.where(even, tails[0], tails[1])
            b_ref[at:at + 1, :] = courant_scale * (ends[n:n + 1, :] + ends[n + 2:n + 3, :])
        b_ref[1:rows + 1, :] = courant_scale * own[...]

    def advance(center, south, north_of, far, r):
        ae = ae_ref[far, :]
        an = an_ref[far, :]
        right = [pltpu.roll(c, 1, 1) for c in center]
        left = [pltpu.roll(c, 127, 1) for c in center]
        result = []
        for h in range(halves):
            ce = ae + be_ref[r + 1:r + 2, h * 128:(h + 1) * 128]
            cn = an + bn_ref[r + 1:r + 2, h * 128:(h + 1) * 128]
            west = jnp.where(first, right[h - 1] if h else 0.0, right[h])
            east_of = jnp.where(last, left[h + 1] if h < halves - 1 else 0.0, left[h])
            along = jnp.where(ce > 0.0, west, east_of)
            across = jnp.where(cn > 0.0, south[h], north_of[h])
            c = center[h]
            result.append(c - jnp.abs(ce) * (c - along) - jnp.abs(cn) * (c - across))
        return result

    def group(g, carry):
        ks = pl.ds(pl.multiple_of(g * SUBK, SUBK), SUBK)
        far = pl.ds(pl.multiple_of(begin + g * SUBK, SUBK), SUBK)
        edge = pl.ds(pl.multiple_of(offset + g * SUBK, SUBK), SUBK)

        def halved(value):
            return [value[:, h * 128:(h + 1) * 128] for h in range(halves)]

        def load(r):
            if 0 <= r < rows:
                return halved(block[r, ks, :].astype(jnp.float32))
            at = r + 2 if r < 0 else r - rows
            one, other = (beyond, across) if r < 0 else (across, beyond)
            return halved(
                jnp.where(even, one[at, edge, :].astype(jnp.float32), other[at, edge, :].astype(jnp.float32))
            )

        below, here = load(-2), load(-1)
        for r in range(-1, rows + 1):
            above = load(r + 1)
            value = advance(here, below, above, far, r)
            if r == -1:
                value = [jnp.where(meta[1] > 0, v, 0.0) for v in value]
            if r == rows:
                value = [jnp.where(meta[2] > 0, v, 0.0) for v in value]
            for h in range(halves):
                once[r + 1, :, h * 128:(h + 1) * 128] = value[h]
            below, here = here, above
        below, here = halved(once[0]), halved(once[1])
        for r in range(rows):
            above = halved(once[r + 2])
            value = advance(here, below, above, far, r)
            for h in range(halves):
                moved[r, ks, h * 128:(h + 1) * 128] = value[h].astype(jnp.bfloat16)
            below, here = here, above
        return carry

    def piece(i, carry):
        bring(i).wait()
        lax.fori_loop(i * (NF // SUBK), (i + 1) * (NF // SUBK), group, 0)
        leave(i).start()
        return carry

    lax.fori_loop(0, count, piece, 0)

    packed[...] = jnp.zeros_like(packed)
    for r in range(rows):
        window = pl.ds(pl.multiple_of(meta[3 + r], STEP), WINDOW)
        part = jnp.dot(moved[r], onehot[r], preferred_element_type=jnp.float32)
        packed[:, window] += part.astype(jnp.bfloat16)
    me = meta[0]
    for k in range(peers):
        start = pl.multiple_of((me ^ k) * share, 128)
        outs[k][...] = packed[:, pl.ds(start, share)]
    for i in range(count):
        leave(i).wait()
    for copy in gathering:
        copy.wait()


def propagate(meta, held, halos, offset, tails, ae, an, east, north, onehot, moved, x, ready, spots, begin, count, peers):
    rows, _, lon = held.shape
    comps = ae.shape[0]
    share = SEA // peers
    depth = count * NF
    vmem = pl.BlockSpec(memory_space=pltpu.VMEM)
    hbm = pl.BlockSpec(memory_space=pltpu.HBM)
    loose = pl.BlockSpec(memory_space=pl.ANY)
    in_specs = [pl.BlockSpec(memory_space=pltpu.SMEM), loose] + [vmem] * 9 + [loose] * len(ready)
    args = [meta, held, *halos, *tails, ae, an, east, north, onehot, *ready]
    out_specs = [hbm] + [vmem] * peers
    out_shape = [jax.ShapeDtypeStruct((rows, comps, lon), jnp.bfloat16)]
    out_shape += [jax.ShapeDtypeStruct((depth, share), jnp.bfloat16)] * peers
    if ready:
        out_specs.append(vmem)
        out_shape.append(jax.ShapeDtypeStruct((ND * NF, share), jnp.bfloat16))
    aliases = {}
    for buffer, spec, out in ((moved, hbm, 0), (x, vmem, peers + 1)):
        if buffer is not None:
            aliases[len(args)] = out
            in_specs.append(spec)
            args.append(buffer)
    result = pl.pallas_call(
        functools.partial(
            propagate_kernel, peers, share, begin * NF, depth, offset * NF,
            (begin if held.shape[1] == comps else 0) * NF, comps // NF, len(aliases), spots,
        ),
        in_specs=in_specs,
        out_specs=out_specs,
        scratch_shapes=[
            pltpu.VMEM((rows, depth, lon), jnp.bfloat16),
            pltpu.VMEM((rows, depth, lon), jnp.bfloat16),
            pltpu.VMEM((rows + 2, SUBK, lon), jnp.float32),
            pltpu.VMEM((rows + 2, lon), jnp.float32),
            pltpu.VMEM((rows + 2, lon), jnp.float32),
            pltpu.VMEM((depth, SEA), jnp.bfloat16),
            pltpu.SemaphoreType.DMA((count,)),
            pltpu.SemaphoreType.DMA((count,)),
            pltpu.SemaphoreType.DMA((max(len(ready), 1),)),
        ],
        out_shape=out_shape,
        input_output_aliases=aliases,
        compiler_params=params(),
        cost_estimate=cost(2.2 * count),
        name="propagate",
    )(*args)
    return result[0], result[1:peers + 1], result[peers + 1] if ready else None


def collect_kernel(spots, dirs, meta, *rest):
    sem = rest[-1]
    for copy in gather(meta, rest[:len(spots)], spots, dirs, rest[-2], sem):
        copy.wait()


def collect(meta, x, pieces, spots, dirs, after=()):
    vmem = pl.BlockSpec(memory_space=pltpu.VMEM)
    return pl.pallas_call(
        functools.partial(collect_kernel, spots, dirs),
        in_specs=[pl.BlockSpec(memory_space=pltpu.SMEM)]
        + [pl.BlockSpec(memory_space=pl.ANY)] * (len(pieces) + len(after))
        + [vmem],
        out_specs=vmem,
        out_shape=jax.ShapeDtypeStruct(x.shape, x.dtype),
        scratch_shapes=[pltpu.SemaphoreType.DMA((len(pieces),))],
        input_output_aliases={1 + len(pieces) + len(after): 0},
        compiler_params=params(),
        cost_estimate=cost(0.2),
        name="collect",
    )(meta, *pieces, *after, x)


def couple_kernel(peers, dirs, begin, size, spots, meta, w, *rest):
    me = meta[0]
    if spots:
        outs = rest[len(spots) + 1:len(spots) + 1 + peers]
        x, y, sem = rest[-3:]
        for copy in gather(meta, rest[:len(spots)], spots, dirs, x, sem):
            copy.wait()
    else:
        x = rest[0]
        outs = rest[-(peers + 1):-1]
        y = rest[-1]
    coupled = jnp.dot(w[...], x[...], preferred_element_type=jnp.float32)
    for p in range(peers):
        own = x[(p * dirs + begin) * NF:(p * dirs + begin + size) * NF, :].astype(jnp.float32)
        y[p] = (own + own * coupled[p * size * NF:(p + 1) * size * NF]).astype(jnp.bfloat16)
    for k in range(peers):
        outs[k][...] = y[me ^ k]


def couple(meta, w, x, pieces, after, spots, begin, size, peers, dirs):
    share = SEA // peers
    vmem = pl.BlockSpec(memory_space=pltpu.VMEM)
    loose = pl.BlockSpec(memory_space=pl.ANY)
    outs = [jax.ShapeDtypeStruct((size * NF, share), jnp.bfloat16)] * peers
    scratch = [pltpu.VMEM((peers, size * NF, share), jnp.bfloat16)]
    aliases = {}
    if after is None:
        in_specs, args = [loose] * len(pieces) + [vmem], [*pieces, x]
        outs = outs + [jax.ShapeDtypeStruct((ND * NF, share), jnp.bfloat16)]
        scratch.append(pltpu.SemaphoreType.DMA((len(pieces),)))
        aliases = {2 + len(pieces): peers}
    else:
        in_specs, args, spots = [vmem] + [loose] * len(after), [x, *after], ()
    result = pl.pallas_call(
        functools.partial(couple_kernel, peers, dirs, begin, size, spots),
        in_specs=[pl.BlockSpec(memory_space=pltpu.SMEM), vmem] + in_specs,
        out_specs=[vmem] * len(outs),
        out_shape=outs,
        scratch_shapes=scratch,
        input_output_aliases=aliases,
        compiler_params=params(),
        cost_estimate=cost(size),
        name="couple",
    )(meta, w, *args)
    return result[:peers], result[peers] if after is None else x


def columns_of(meta, k, first, depth, dirs):
    return pl.ds(pl.multiple_of(((meta[0] ^ k) * dirs + first) * NF, 128), depth)


def begin_kernel(dirs, spots, meta, w, *rest):
    total = rest[-1]
    for i, (k, first) in enumerate(spots):
        piece = rest[i]
        part = jnp.dot(
            w[:, columns_of(meta, k, first, piece.shape[0], dirs)], piece[...],
            preferred_element_type=jnp.float32,
        )
        if i:
            total[...] += part
        else:
            total[...] = part


def begin_couple(meta, w, pieces, spots, dirs):
    vmem = pl.BlockSpec(memory_space=pltpu.VMEM)
    return pl.pallas_call(
        functools.partial(begin_kernel, dirs, spots),
        in_specs=[pl.BlockSpec(memory_space=pltpu.SMEM)] + [vmem] * (1 + len(pieces)),
        out_specs=vmem,
        out_shape=jax.ShapeDtypeStruct((w.shape[0], pieces[0].shape[1]), jnp.float32),
        compiler_params=params(),
        cost_estimate=cost(0.2),
        name="begin_couple",
    )(meta, w, *pieces)


def end_kernel(peers, dirs, size, spots, meta, w, partial, *rest):
    owns, pieces, outs, total = rest[:peers], rest[peers:2 * peers], rest[2 * peers:-1], rest[-1]
    coupled = partial[...]
    for i, (k, first) in enumerate(spots):
        coupled += jnp.dot(
            w[:, columns_of(meta, k, first, pieces[i].shape[0], dirs)], pieces[i][...],
            preferred_element_type=jnp.float32,
        )
    for p in range(peers):
        total[p] = coupled[p * size * NF:(p + 1) * size * NF]
    for k in range(peers):
        own = owns[k][:size * NF, :].astype(jnp.float32)
        outs[k][...] = (own + own * total[meta[0] ^ k]).astype(jnp.bfloat16)


def end_couple(meta, w, partial, owns, pieces, spots, size, peers, dirs):
    vmem = pl.BlockSpec(memory_space=pltpu.VMEM)
    share = SEA // peers
    return pl.pallas_call(
        functools.partial(end_kernel, peers, dirs, size, spots),
        in_specs=[pl.BlockSpec(memory_space=pltpu.SMEM)] + [vmem] * (2 + 2 * peers),
        out_specs=[vmem] * peers,
        out_shape=[jax.ShapeDtypeStruct((size * NF, share), jnp.bfloat16)] * peers,
        scratch_shapes=[pltpu.VMEM((peers, size * NF, share), jnp.float32)],
        compiler_params=params(),
        cost_estimate=cost(2),
        name="end_couple",
    )(meta, w, partial, *owns, *pieces)


def finish_kernel(peers, share, begin, group, meta, slot, spread, moved, *rest):
    pieces = rest[:peers]
    out, renewed, old, new, piece_sem, in_sem, out_sem = rest[peers:]
    rows, lon = slot.shape
    depth = renewed.shape[0]
    me = meta[0]
    copies = []
    for k in range(peers):
        start = pl.multiple_of((me ^ k) * share, 128)
        copies.append(pltpu.make_async_copy(pieces[k], renewed.at[:, pl.ds(start, share)], piece_sem.at[k]))
        copies[-1].start()
    far = slice(begin, begin + depth)
    bring, leave = [], []
    for i in range(rows // group):
        part = slice(i * group, (i + 1) * group)
        bring.append(pltpu.make_async_copy(moved.at[part, far, :], old.at[part], in_sem.at[i]))
        leave.append(pltpu.make_async_copy(new.at[part], out.at[part, far, :], out_sem.at[i]))
        bring[-1].start()
    for copy in copies:
        copy.wait()
    for r in range(rows):
        if r % group == 0:
            bring[r // group].wait()
        base = pl.multiple_of(meta[3 + r], STEP)
        value = jnp.dot(renewed[:, pl.ds(base, WINDOW)], spread[r], preferred_element_type=jnp.float32)
        sea = slot[r:r + 1, :] >= 0
        new[r] = jnp.where(sea, value, old[r].astype(jnp.float32)).astype(jnp.bfloat16)
        if r % group == group - 1:
            leave[r // group].start()
    for copy in leave:
        copy.wait()


def finish(meta, slot, spread, moved, pieces, begin, size, peers):
    rows, comps, lon = moved.shape
    share = SEA // peers
    group = 4
    hbm = pl.BlockSpec(memory_space=pltpu.HBM)
    vmem = pl.BlockSpec(memory_space=pltpu.VMEM)
    return pl.pallas_call(
        functools.partial(finish_kernel, peers, share, begin * NF, group),
        in_specs=[pl.BlockSpec(memory_space=pltpu.SMEM), vmem, vmem, hbm]
        + [pl.BlockSpec(memory_space=pl.ANY)] * peers,
        out_specs=hbm,
        out_shape=jax.ShapeDtypeStruct(moved.shape, jnp.bfloat16),
        scratch_shapes=[
            pltpu.VMEM((size * NF, SEA), jnp.bfloat16),
            pltpu.VMEM((rows, size * NF, lon), jnp.bfloat16),
            pltpu.VMEM((rows, size * NF, lon), jnp.bfloat16),
            pltpu.SemaphoreType.DMA((peers,)),
            pltpu.SemaphoreType.DMA((rows // group,)),
            pltpu.SemaphoreType.DMA((rows // group,)),
        ],
        input_output_aliases={3: 0},
        compiler_params=params(),
        cost_estimate=cost(size),
        name="finish",
    )(meta, slot, spread, moved, *pieces)


def swap(array, first):
    count = lax.axis_size("tile")
    pairs = [(i, i + 1) for i in range(first, count - 1, 2)]
    return lax.ppermute(array, "tile", pairs + [(j, i) for i, j in pairs])


def local(action, east_current, north_current, sea_mask, pattern, table):
    rows, comps, lon = action.shape
    peers = lax.axis_size("spec")
    me = lax.axis_index("spec")
    tile = lax.axis_index("tile")
    tiles = lax.axis_size("tile")
    dirs = comps // NF
    parts_out = split_directions(dirs, (4, 4, 4))
    parts_back = split_directions(dirs, (3, 6, 3))

    ahead = parts_out[0] * NF
    parity = (tile % 2).astype(jnp.int32)
    parity = (tile % 2).astype(jnp.int32)
    currents = jnp.stack([east_current, north_current])

    def near_edge(top):
        first = jnp.where(top, rows - 2, 0)
        body = lax.dynamic_slice(action, (first, 0, 0), (2, ahead, lon))
        pair = lax.dynamic_slice(currents, (0, jnp.where(top, rows - 1, 0), 0), (2, 1, lon))[:, 0]
        coarse = lax.reduce_precision(pair, 8, 7)
        tail = jnp.concatenate([coarse, pair - coarse, jnp.zeros((12, lon), jnp.float32)])
        return jnp.concatenate([body, jnp.broadcast_to(tail.astype(jnp.bfloat16), (2, 16, lon))], axis=1)

    near = swap(near_edge(parity == 0), 0), swap(near_edge(parity == 1), 1)

    components = me * comps + jnp.arange(comps, dtype=jnp.int32)
    direction = (components // NF).astype(jnp.float32)
    frequency = (components % NF).astype(jnp.float32)
    speed = courant_scale * jnp.exp(-2.0 * frequency / (NF - 1))
    theta = 2.0 * jnp.pi * direction / ND
    ae = jnp.broadcast_to((speed * jnp.cos(theta))[:, None], (comps, 128))
    an = jnp.broadcast_to((speed * jnp.sin(theta))[:, None], (comps, 128))

    sea = sea_mask > 0
    before = jnp.dot(
        sea.astype(jnp.bfloat16),
        jnp.triu(jnp.ones((lon, lon), jnp.bfloat16), 1),
        preferred_element_type=jnp.float32,
    )
    totals = jnp.sum(sea.astype(jnp.float32), axis=1)
    starts = jnp.sum(
        jnp.where(jnp.tril(jnp.ones((rows, rows), jnp.bool_), -1), totals[None, :], 0.0), axis=1
    )
    slot = jnp.where(sea, (before + starts[:, None]).astype(jnp.int32), -1)
    bases = jnp.minimum(starts.astype(jnp.int32) // STEP * STEP, SEA - WINDOW)
    meta = jnp.concatenate([
        jnp.stack([me, (tile > 0).astype(jnp.int32), (tile < tiles - 1).astype(jnp.int32)]),
        bases,
        parity.reshape(1),
    ]).astype(jnp.int32)
    slot_t = slot.T

    onehot, ae, an, across, beyond = mark(
        meta, slot_t, ae, an, action[rows - 2:, ahead:], action[:2, ahead:]
    )
    far = swap(across, 0), swap(beyond, 1)

    moved, x = None, None
    pieces, spots = [], []
    for j, (begin, count) in enumerate(zip(offsets_of(parts_out), parts_out)):
        offset = begin - parts_out[0] if j else 0
        ready = (pieces[j - 2], tuple(spots[j - 2])) if j >= 2 else ([], ())
        moved, packed, x = propagate(
            meta, action, far if j else near, offset, near, ae, an,
            east_current, north_current, onehot, moved, x, *ready, begin, count, peers,
        )
        pieces.append([packed[0]] + [
            lax.ppermute(packed[k], "spec", [(i, i ^ k) for i in range(peers)])
            for k in range(1, peers)
        ])
        spots.append([(k, begin) for k in range(peers)])

    spread, sel, tt = setup(meta, slot, pattern.T, table, packed[0])
    woven = [
        weave(sel, tt, packed[0], begin, size, peers, dirs)
        for begin, size in zip(offsets_of(parts_back), parts_back)
    ]
    x = collect(meta, x, pieces[-2], tuple(spots[-2]), dirs)
    early = comps % 128 == 0 and parts_back[0] <= parts_out[0]
    early = early and all(size * NF % 128 == 0 for size in parts_out)
    if early:
        ahead_pieces = [piece for part in pieces[:-1] for piece in part]
        ahead_spots = tuple(spot for part in spots[:-1] for spot in part)
        partial = begin_couple(meta, woven[0], ahead_pieces, ahead_spots, dirs)
    result = moved
    backs = []
    for g, (begin, size) in enumerate(zip(offsets_of(parts_back), parts_back)):
        after = backs[g - 2][1:] if g >= 2 else renewed[:1] if g else None
        if early and g == 0:
            renewed = end_couple(
                meta, woven[0], partial, pieces[0], pieces[-1], tuple(spots[-1]), size, peers, dirs
            )
            x = collect(meta, x, pieces[-1], tuple(spots[-1]), dirs, tuple(renewed[:1]))
        else:
            renewed, x = couple(
                meta, woven[g], x, pieces[-1], after, tuple(spots[-1]), begin, size, peers, dirs
            )
        back = [renewed[0]] + [
            lax.ppermute(renewed[k], "spec", [(i, i ^ k) for i in range(peers)])
            for k in range(1, peers)
        ]
        backs.append(back)
        result = finish(meta, slot, spread, result, back, begin, size, peers)
    return result


def solution(mesh):
    return jax.shard_map(
        local,
        mesh=mesh,
        in_specs=(
            P("tile", "spec", None),
            P("tile", None),
            P("tile", None),
            P("tile", None),
            P(),
            P(),
        ),
        out_specs=P("tile", "spec", None),
        check_vma=False,
    )
```

```python
import functools

import jax
import jax.numpy as jnp
from jax import lax
from jax.experimental import pallas as pl
from jax.experimental.pallas import tpu as pltpu
from jax.sharding import PartitionSpec as P

NF = 64
ND = 48
SEA = 2048
WINDOW = 512
STEP = 256
SUBK = 16
courant_scale = 0.45
MIB = 1024 * 1024


def split_directions(count, sizes):
    if sum(sizes) == count:
        return sizes
    return (1,) * count


def offsets_of(sizes):
    return [sum(sizes[:i]) for i in range(len(sizes))]


def cost(us):
    return pl.CostEstimate(
        flops=int(us * 1.15e9), bytes_accessed=int(us * 3e6), transcendentals=0
    )


def params(mib=16):
    return pltpu.CompilerParams(vmem_limit_bytes=mib * MIB)


def mark_kernel(rows, meta, slot_t, ae, an, top, bottom, onehot, ae_out, an_out, across, beyond):
    even = meta[3 + rows] == 0

    @pl.when(even)
    def rising():
        across[...] = top[...]
        beyond[...] = bottom[...]

    @pl.when(jnp.logical_not(even))
    def falling():
        across[...] = bottom[...]
        beyond[...] = top[...]

    ae_out[...] = jnp.broadcast_to(ae[...], ae_out.shape)
    an_out[...] = jnp.broadcast_to(an[...], an_out.shape)
    lanes = lax.broadcasted_iota(jnp.int32, onehot.shape[1:], 1)
    for r in range(rows):
        onehot[r] = jnp.where(slot_t[:, r:r + 1] - meta[3 + r] == lanes, 1.0, 0.0).astype(jnp.bfloat16)


def mark(meta, slot_t, ae, an, top, bottom):
    lon, rows = slot_t.shape
    vmem = pl.BlockSpec(memory_space=pltpu.VMEM)
    return pl.pallas_call(
        functools.partial(mark_kernel, rows),
        in_specs=[pl.BlockSpec(memory_space=pltpu.SMEM)] + [vmem] * 5,
        out_specs=[vmem] * 5,
        out_shape=[
            jax.ShapeDtypeStruct((rows, lon, WINDOW), jnp.bfloat16),
            jax.ShapeDtypeStruct(ae.shape, ae.dtype),
            jax.ShapeDtypeStruct(an.shape, an.dtype),
            jax.ShapeDtypeStruct(top.shape, top.dtype),
            jax.ShapeDtypeStruct(top.shape, top.dtype),
        ],
        compiler_params=params(),
        cost_estimate=cost(4),
        name="mark",
    )(meta, slot_t, ae, an, top, bottom)


def setup_kernel(rows, meta, slot, pattern_t, table, after, spread, sel, tt):
    lon = slot.shape[1]
    depths = lax.broadcasted_iota(jnp.int32, (WINDOW, lon), 0)
    for r in range(rows):
        spread[r] = jnp.where(slot[r:r + 1, :] - meta[3 + r] == depths, 1.0, 0.0).astype(jnp.bfloat16)
    target = lax.broadcasted_iota(jnp.int32, (128, ND), 0)
    hit = pattern_t[0:1, :] == target
    for j in range(1, pattern_t.shape[0]):
        hit = hit | (pattern_t[j:j + 1, :] == target)
    chosen = jnp.where(hit, 1.0, 0.0).astype(jnp.bfloat16)
    block = lax.broadcasted_iota(jnp.int32, (128, ND * NF), 1) // NF
    owner = lax.broadcasted_iota(jnp.int32, (128, ND * NF), 0)
    widen = jnp.where(block == owner, 1.0, 0.0).astype(jnp.bfloat16)
    sel[...] = lax.dot_general(
        chosen, widen, (((0,), (0,)), ((), ())), preferred_element_type=jnp.float32
    )
    for odd in range(2):
        for t in range(ND // 2):
            pair = jnp.concatenate(
                [table[2 * t + odd].astype(jnp.float32), table[(2 * t + odd + 1) % ND].astype(jnp.float32)],
                axis=1,
            ).astype(jnp.bfloat16)
            tt[odd, :, t * 128:(t + 1) * 128] = pair
            tt[odd, :, ND * NF + t * 128:ND * NF + (t + 1) * 128] = pair


def setup(meta, slot, pattern_t, table, after):
    rows, lon = slot.shape
    vmem = pl.BlockSpec(memory_space=pltpu.VMEM)
    return pl.pallas_call(
        functools.partial(setup_kernel, rows),
        in_specs=[pl.BlockSpec(memory_space=pltpu.SMEM)] + [vmem] * 3 + [pl.BlockSpec(memory_space=pl.ANY)],
        out_specs=[vmem] * 3,
        out_shape=[
            jax.ShapeDtypeStruct((rows, WINDOW, lon), jnp.bfloat16),
            jax.ShapeDtypeStruct((ND, ND * NF), jnp.float32),
            jax.ShapeDtypeStruct((2, NF, 2 * ND * NF), jnp.bfloat16),
        ],
        compiler_params=params(),
        cost_estimate=cost(0.2),
        name="setup",
    )(meta, slot, pattern_t, table, after)


def weave_kernel(peers, dirs, begin, size, sel, tt, after, w):
    def strip(i, carry):
        r = i // size * dirs + begin + i % size
        turn = lax.rem(ND - r, ND)
        lanes = pl.ds(pl.multiple_of((turn // 2) * 128, 128), ND * NF)
        keep = jnp.broadcast_to(sel[pl.ds(r, 1), :], (16, ND * NF)).astype(jnp.bfloat16)
        for q in range(NF // 16):
            w[pl.ds(pl.multiple_of(i * NF + q * 16, 16), 16), :] = tt[turn % 2, pl.ds(q * 16, 16), lanes] * keep
        return carry

    lax.fori_loop(0, peers * size, strip, 0)


def weave(sel, tt, after, begin, size, peers, dirs):
    vmem = pl.BlockSpec(memory_space=pltpu.VMEM)
    return pl.pallas_call(
        functools.partial(weave_kernel, peers, dirs, begin, size),
        in_specs=[vmem, vmem, pl.BlockSpec(memory_space=pl.ANY)],
        out_specs=vmem,
        out_shape=jax.ShapeDtypeStruct((peers * size * NF, ND * NF), jnp.bfloat16),
        compiler_params=params(),
        cost_estimate=cost(0.1),
        name="weave",
    )(sel, tt, after)


def gather(meta, pieces, spots, dirs, x, sem):
    copies = []
    for i, (k, first) in enumerate(spots):
        depth = pieces[i].shape[0]
        start = pl.multiple_of(((meta[0] ^ k) * dirs + first) * NF, NF)
        copies.append(pltpu.make_async_copy(pieces[i], x.at[pl.ds(start, depth), :], sem.at[i]))
        copies[-1].start()
    return copies


def propagate_kernel(peers, share, begin, depth, offset, source, dirs, aliased, spots, meta, act, across, beyond,
                     across_tail, beyond_tail, ae_ref, an_ref, east, north, onehot, *rest):
    rows, _, lon = act.shape
    ready = rest[:len(spots)]
    rest = rest[len(spots) + aliased:]
    even = meta[3 + rows] == 0
    moved_out = rest[0]
    outs = rest[1:peers + 1]
    block, moved, once, be_ref, bn_ref, packed, in_sem, out_sem, x_sem = rest[-9:]
    count = depth // NF
    halves = lon // 128
    lane = lax.broadcasted_iota(jnp.int32, (SUBK, 128), 1)
    first = lane == 0
    last = lane == 127

    def bring(i):
        part = pl.ds(pl.multiple_of(i * NF, NF), NF)
        there = pl.ds(pl.multiple_of(source + i * NF, NF), NF)
        return pltpu.make_async_copy(act.at[:, there, :], block.at[:, part, :], in_sem.at[i])

    def leave(i):
        part = pl.ds(pl.multiple_of(i * NF, NF), NF)
        far = pl.ds(pl.multiple_of(begin + i * NF, NF), NF)
        return pltpu.make_async_copy(moved.at[:, part, :], moved_out.at[:, far, :], out_sem.at[i])

    for i in range(count):
        bring(i).start()
    gathering = gather(meta, ready, spots, dirs, rest[peers + 1], x_sem)
    for n, (own, b_ref) in enumerate(((east, be_ref), (north, bn_ref))):
        for at, one, other in ((0, beyond_tail, across_tail), (rows + 1, across_tail, beyond_tail)):
            tails = [t[0, t.shape[1] - 16:, :].astype(jnp.float32) for t in (one, other)]
            ends = jnp.where(even, tails[0], tails[1])
            b_ref[at:at + 1, :] = courant_scale * (ends[n:n + 1, :] + ends[n + 2:n + 3, :])
        b_ref[1:rows + 1, :] = courant_scale * own[...]

    def advance(center, south, north_of, far, r):
        ae = ae_ref[far, :]
        an = an_ref[far, :]
        right = [pltpu.roll(c, 1, 1) for c in center]
        left = [pltpu.roll(c, 127, 1) for c in center]
        result = []
        for h in range(halves):
            ce = ae + be_ref[r + 1:r + 2, h * 128:(h + 1) * 128]
            cn = an + bn_ref[r + 1:r + 2, h * 128:(h + 1) * 128]
            west = jnp.where(first, right[h - 1] if h else 0.0, right[h])
            east_of = jnp.where(last, left[h + 1] if h < halves - 1 else 0.0, left[h])
            along = jnp.where(ce > 0.0, west, east_of)
            across = jnp.where(cn > 0.0, south[h], north_of[h])
            c = center[h]
            result.append(c - jnp.abs(ce) * (c - along) - jnp.abs(cn) * (c - across))
        return result

    def group(g, carry):
        ks = pl.ds(pl.multiple_of(g * SUBK, SUBK), SUBK)
        far = pl.ds(pl.multiple_of(begin + g * SUBK, SUBK), SUBK)
        edge = pl.ds(pl.multiple_of(offset + g * SUBK, SUBK), SUBK)

        def halved(value):
            return [value[:, h * 128:(h + 1) * 128] for h in range(halves)]

        def load(r):
            if 0 <= r < rows:
                return halved(block[r, ks, :].astype(jnp.float32))
            at = r + 2 if r < 0 else r - rows
            one, other = (beyond, across) if r < 0 else (across, beyond)
            return halved(
                jnp.where(even, one[at, edge, :].astype(jnp.float32), other[at, edge, :].astype(jnp.float32))
            )

        below, here = load(-2), load(-1)
        for r in range(-1, rows + 1):
            above = load(r + 1)
            value = advance(here, below, above, far, r)
            if r == -1:
                value = [jnp.where(meta[1] > 0, v, 0.0) for v in value]
            if r == rows:
                value = [jnp.where(meta[2] > 0, v, 0.0) for v in value]
            for h in range(halves):
                once[r + 1, :, h * 128:(h + 1) * 128] = value[h]
            below, here = here, above
        below, here = halved(once[0]), halved(once[1])
        for r in range(rows):
            above = halved(once[r + 2])
            value = advance(here, below, above, far, r)
            for h in range(halves):
                moved[r, ks, h * 128:(h + 1) * 128] = value[h].astype(jnp.bfloat16)
            below, here = here, above
        return carry

    def piece(i, carry):
        bring(i).wait()
        lax.fori_loop(i * (NF // SUBK), (i + 1) * (NF // SUBK), group, 0)
        leave(i).start()
        return carry

    lax.fori_loop(0, count, piece, 0)

    packed[...] = jnp.zeros_like(packed)
    for r in range(rows):
        window = pl.ds(pl.multiple_of(meta[3 + r], STEP), WINDOW)
        part = jnp.dot(moved[r], onehot[r], preferred_element_type=jnp.float32)
        packed[:, window] += part.astype(jnp.bfloat16)
    me = meta[0]
    for k in range(peers):
        start = pl.multiple_of((me ^ k) * share, 128)
        outs[k][...] = packed[:, pl.ds(start, share)]
    for i in range(count):
        leave(i).wait()
    for copy in gathering:
        copy.wait()


def propagate(meta, held, halos, offset, tails, ae, an, east, north, onehot, moved, x, ready, spots, begin, count, peers):
    rows, _, lon = held.shape
    comps = ae.shape[0]
    share = SEA // peers
    depth = count * NF
    vmem = pl.BlockSpec(memory_space=pltpu.VMEM)
    hbm = pl.BlockSpec(memory_space=pltpu.HBM)
    loose = pl.BlockSpec(memory_space=pl.ANY)
    in_specs = [pl.BlockSpec(memory_space=pltpu.SMEM), loose] + [vmem] * 9 + [loose] * len(ready)
    args = [meta, held, *halos, *tails, ae, an, east, north, onehot, *ready]
    out_specs = [hbm] + [vmem] * peers
    out_shape = [jax.ShapeDtypeStruct((rows, comps, lon), jnp.bfloat16)]
    out_shape += [jax.ShapeDtypeStruct((depth, share), jnp.bfloat16)] * peers
    if ready:
        out_specs.append(vmem)
        out_shape.append(jax.ShapeDtypeStruct((ND * NF, share), jnp.bfloat16))
    aliases = {}
    for buffer, spec, out in ((moved, hbm, 0), (x, vmem, peers + 1)):
        if buffer is not None:
            aliases[len(args)] = out
            in_specs.append(spec)
            args.append(buffer)
    result = pl.pallas_call(
        functools.partial(
            propagate_kernel, peers, share, begin * NF, depth, offset * NF,
            (begin if held.shape[1] == comps else 0) * NF, comps // NF, len(aliases), spots,
        ),
        in_specs=in_specs,
        out_specs=out_specs,
        scratch_shapes=[
            pltpu.VMEM((rows, depth, lon), jnp.bfloat16),
            pltpu.VMEM((rows, depth, lon), jnp.bfloat16),
            pltpu.VMEM((rows + 2, SUBK, lon), jnp.float32),
            pltpu.VMEM((rows + 2, lon), jnp.float32),
            pltpu.VMEM((rows + 2, lon), jnp.float32),
            pltpu.VMEM((depth, SEA), jnp.bfloat16),
            pltpu.SemaphoreType.DMA((count,)),
            pltpu.SemaphoreType.DMA((count,)),
            pltpu.SemaphoreType.DMA((max(len(ready), 1),)),
        ],
        out_shape=out_shape,
        input_output_aliases=aliases,
        compiler_params=params(),
        cost_estimate=cost(2.2 * count),
        name="propagate",
    )(*args)
    return result[0], result[1:peers + 1], result[peers + 1] if ready else None


def collect_kernel(spots, dirs, meta, *rest):
    sem = rest[-1]
    for copy in gather(meta, rest[:len(spots)], spots, dirs, rest[-2], sem):
        copy.wait()


def collect(meta, x, pieces, spots, dirs, after=()):
    vmem = pl.BlockSpec(memory_space=pltpu.VMEM)
    return pl.pallas_call(
        functools.partial(collect_kernel, spots, dirs),
        in_specs=[pl.BlockSpec(memory_space=pltpu.SMEM)]
        + [pl.BlockSpec(memory_space=pl.ANY)] * (len(pieces) + len(after))
        + [vmem],
        out_specs=vmem,
        out_shape=jax.ShapeDtypeStruct(x.shape, x.dtype),
        scratch_shapes=[pltpu.SemaphoreType.DMA((len(pieces),))],
        input_output_aliases={1 + len(pieces) + len(after): 0},
        compiler_params=params(),
        cost_estimate=cost(0.2),
        name="collect",
    )(meta, *pieces, *after, x)


def couple_kernel(peers, dirs, begin, size, spots, meta, w, *rest):
    me = meta[0]
    if spots:
        outs = rest[len(spots) + 1:len(spots) + 1 + peers]
        x, y, sem = rest[-3:]
        for copy in gather(meta, rest[:len(spots)], spots, dirs, x, sem):
            copy.wait()
    else:
        x = rest[0]
        outs = rest[-(peers + 1):-1]
        y = rest[-1]
    coupled = jnp.dot(w[...], x[...], preferred_element_type=jnp.float32)
    for p in range(peers):
        own = x[(p * dirs + begin) * NF:(p * dirs + begin + size) * NF, :].astype(jnp.float32)
        y[p] = (own + own * coupled[p * size * NF:(p + 1) * size * NF]).astype(jnp.bfloat16)
    for k in range(peers):
        outs[k][...] = y[me ^ k]


def couple(meta, w, x, pieces, after, spots, begin, size, peers, dirs):
    share = SEA // peers
    vmem = pl.BlockSpec(memory_space=pltpu.VMEM)
    loose = pl.BlockSpec(memory_space=pl.ANY)
    outs = [jax.ShapeDtypeStruct((size * NF, share), jnp.bfloat16)] * peers
    scratch = [pltpu.VMEM((peers, size * NF, share), jnp.bfloat16)]
    aliases = {}
    if after is None:
        in_specs, args = [loose] * len(pieces) + [vmem], [*pieces, x]
        outs = outs + [jax.ShapeDtypeStruct((ND * NF, share), jnp.bfloat16)]
        scratch.append(pltpu.SemaphoreType.DMA((len(pieces),)))
        aliases = {2 + len(pieces): peers}
    else:
        in_specs, args, spots = [vmem] + [loose] * len(after), [x, *after], ()
    result = pl.pallas_call(
        functools.partial(couple_kernel, peers, dirs, begin, size, spots),
        in_specs=[pl.BlockSpec(memory_space=pltpu.SMEM), vmem] + in_specs,
        out_specs=[vmem] * len(outs),
        out_shape=outs,
        scratch_shapes=scratch,
        input_output_aliases=aliases,
        compiler_params=params(),
        cost_estimate=cost(size),
        name="couple",
    )(meta, w, *args)
    return result[:peers], result[peers] if after is None else x


def columns_of(meta, k, first, depth, dirs):
    return pl.ds(pl.multiple_of(((meta[0] ^ k) * dirs + first) * NF, 128), depth)


def begin_kernel(dirs, spots, meta, w, *rest):
    total = rest[-1]
    for i, (k, first) in enumerate(spots):
        piece = rest[i]
        part = jnp.dot(
            w[:, columns_of(meta, k, first, piece.shape[0], dirs)], piece[...],
            preferred_element_type=jnp.float32,
        )
        if i:
            total[...] += part
        else:
            total[...] = part


def begin_couple(meta, w, pieces, spots, dirs):
    vmem = pl.BlockSpec(memory_space=pltpu.VMEM)
    return pl.pallas_call(
        functools.partial(begin_kernel, dirs, spots),
        in_specs=[pl.BlockSpec(memory_space=pltpu.SMEM)] + [vmem] * (1 + len(pieces)),
        out_specs=vmem,
        out_shape=jax.ShapeDtypeStruct((w.shape[0], pieces[0].shape[1]), jnp.float32),
        compiler_params=params(),
        cost_estimate=cost(0.2),
        name="begin_couple",
    )(meta, w, *pieces)


def end_kernel(peers, dirs, size, spots, meta, w, partial, *rest):
    owns, pieces, outs, total = rest[:peers], rest[peers:2 * peers], rest[2 * peers:-1], rest[-1]
    coupled = partial[...]
    for i, (k, first) in enumerate(spots):
        coupled += jnp.dot(
            w[:, columns_of(meta, k, first, pieces[i].shape[0], dirs)], pieces[i][...],
            preferred_element_type=jnp.float32,
        )
    for p in range(peers):
        total[p] = coupled[p * size * NF:(p + 1) * size * NF]
    for k in range(peers):
        own = owns[k][:size * NF, :].astype(jnp.float32)
        outs[k][...] = (own + own * total[meta[0] ^ k]).astype(jnp.bfloat16)


def end_couple(meta, w, partial, owns, pieces, spots, size, peers, dirs):
    vmem = pl.BlockSpec(memory_space=pltpu.VMEM)
    share = SEA // peers
    return pl.pallas_call(
        functools.partial(end_kernel, peers, dirs, size, spots),
        in_specs=[pl.BlockSpec(memory_space=pltpu.SMEM)] + [vmem] * (2 + 2 * peers),
        out_specs=[vmem] * peers,
        out_shape=[jax.ShapeDtypeStruct((size * NF, share), jnp.bfloat16)] * peers,
        scratch_shapes=[pltpu.VMEM((peers, size * NF, share), jnp.float32)],
        compiler_params=params(),
        cost_estimate=cost(2),
        name="end_couple",
    )(meta, w, partial, *owns, *pieces)


def finish_kernel(peers, share, begin, group, meta, slot, spread, moved, *rest):
    pieces = rest[:peers]
    out, renewed, old, new, piece_sem, in_sem, out_sem = rest[peers:]
    rows, lon = slot.shape
    depth = renewed.shape[0]
    me = meta[0]
    copies = []
    for k in range(peers):
        start = pl.multiple_of((me ^ k) * share, 128)
        copies.append(pltpu.make_async_copy(pieces[k], renewed.at[:, pl.ds(start, share)], piece_sem.at[k]))
        copies[-1].start()
    far = slice(begin, begin + depth)
    bring, leave = [], []
    for i in range(rows // group):
        part = slice(i * group, (i + 1) * group)
        bring.append(pltpu.make_async_copy(moved.at[part, far, :], old.at[part], in_sem.at[i]))
        leave.append(pltpu.make_async_copy(new.at[part], out.at[part, far, :], out_sem.at[i]))
        bring[-1].start()
    for copy in copies:
        copy.wait()
    for r in range(rows):
        if r % group == 0:
            bring[r // group].wait()
        base = pl.multiple_of(meta[3 + r], STEP)
        value = jnp.dot(renewed[:, pl.ds(base, WINDOW)], spread[r], preferred_element_type=jnp.float32)
        sea = slot[r:r + 1, :] >= 0
        new[r] = jnp.where(sea, value, old[r].astype(jnp.float32)).astype(jnp.bfloat16)
        if r % group == group - 1:
            leave[r // group].start()
    for copy in leave:
        copy.wait()


def finish(meta, slot, spread, moved, pieces, begin, size, peers):
    rows, comps, lon = moved.shape
    share = SEA // peers
    group = 4
    hbm = pl.BlockSpec(memory_space=pltpu.HBM)
    vmem = pl.BlockSpec(memory_space=pltpu.VMEM)
    return pl.pallas_call(
        functools.partial(finish_kernel, peers, share, begin * NF, group),
        in_specs=[pl.BlockSpec(memory_space=pltpu.SMEM), vmem, vmem, hbm]
        + [pl.BlockSpec(memory_space=pl.ANY)] * peers,
        out_specs=hbm,
        out_shape=jax.ShapeDtypeStruct(moved.shape, jnp.bfloat16),
        scratch_shapes=[
            pltpu.VMEM((size * NF, SEA), jnp.bfloat16),
            pltpu.VMEM((rows, size * NF, lon), jnp.bfloat16),
            pltpu.VMEM((rows, size * NF, lon), jnp.bfloat16),
            pltpu.SemaphoreType.DMA((peers,)),
            pltpu.SemaphoreType.DMA((rows // group,)),
            pltpu.SemaphoreType.DMA((rows // group,)),
        ],
        input_output_aliases={3: 0},
        compiler_params=params(),
        cost_estimate=cost(size),
        name="finish",
    )(meta, slot, spread, moved, *pieces)


def swap(array, first):
    count = lax.axis_size("tile")
    pairs = [(i, i + 1) for i in range(first, count - 1, 2)]
    return lax.ppermute(array, "tile", pairs + [(j, i) for i, j in pairs])


def local(action, east_current, north_current, sea_mask, pattern, table):
    rows, comps, lon = action.shape
    peers = lax.axis_size("spec")
    me = lax.axis_index("spec")
    tile = lax.axis_index("tile")
    tiles = lax.axis_size("tile")
    dirs = comps // NF
    parts_out = split_directions(dirs, (4, 4, 4))
    parts_back = split_directions(dirs, (4, 6, 2))

    ahead = parts_out[0] * NF
    parity = (tile % 2).astype(jnp.int32)
    parity = (tile % 2).astype(jnp.int32)
    currents = jnp.stack([east_current, north_current])

    def near_edge(top):
        first = jnp.where(top, rows - 2, 0)
        body = lax.dynamic_slice(action, (first, 0, 0), (2, ahead, lon))
        pair = lax.dynamic_slice(currents, (0, jnp.where(top, rows - 1, 0), 0), (2, 1, lon))[:, 0]
        coarse = lax.reduce_precision(pair, 8, 7)
        tail = jnp.concatenate([coarse, pair - coarse, jnp.zeros((12, lon), jnp.float32)])
        return jnp.concatenate([body, jnp.broadcast_to(tail.astype(jnp.bfloat16), (2, 16, lon))], axis=1)

    near = swap(near_edge(parity == 0), 0), swap(near_edge(parity == 1), 1)

    components = me * comps + jnp.arange(comps, dtype=jnp.int32)
    direction = (components // NF).astype(jnp.float32)
    frequency = (components % NF).astype(jnp.float32)
    speed = courant_scale * jnp.exp(-2.0 * frequency / (NF - 1))
    theta = 2.0 * jnp.pi * direction / ND
    ae = jnp.broadcast_to((speed * jnp.cos(theta))[:, None], (comps, 128))
    an = jnp.broadcast_to((speed * jnp.sin(theta))[:, None], (comps, 128))

    sea = sea_mask > 0
    before = jnp.dot(
        sea.astype(jnp.bfloat16),
        jnp.triu(jnp.ones((lon, lon), jnp.bfloat16), 1),
        preferred_element_type=jnp.float32,
    )
    totals = jnp.sum(sea.astype(jnp.float32), axis=1)
    starts = jnp.sum(
        jnp.where(jnp.tril(jnp.ones((rows, rows), jnp.bool_), -1), totals[None, :], 0.0), axis=1
    )
    slot = jnp.where(sea, (before + starts[:, None]).astype(jnp.int32), -1)
    bases = jnp.minimum(starts.astype(jnp.int32) // STEP * STEP, SEA - WINDOW)
    meta = jnp.concatenate([
        jnp.stack([me, (tile > 0).astype(jnp.int32), (tile < tiles - 1).astype(jnp.int32)]),
        bases,
        parity.reshape(1),
    ]).astype(jnp.int32)
    slot_t = slot.T

    onehot, ae, an, across, beyond = mark(
        meta, slot_t, ae, an, action[rows - 2:, ahead:], action[:2, ahead:]
    )
    far = swap(across, 0), swap(beyond, 1)

    moved, x = None, None
    pieces, spots = [], []
    for j, (begin, count) in enumerate(zip(offsets_of(parts_out), parts_out)):
        offset = begin - parts_out[0] if j else 0
        ready = (pieces[j - 2], tuple(spots[j - 2])) if j >= 2 else ([], ())
        moved, packed, x = propagate(
            meta, action, far if j else near, offset, near, ae, an,
            east_current, north_current, onehot, moved, x, *ready, begin, count, peers,
        )
        pieces.append([packed[0]] + [
            lax.ppermute(packed[k], "spec", [(i, i ^ k) for i in range(peers)])
            for k in range(1, peers)
        ])
        spots.append([(k, begin) for k in range(peers)])

    spread, sel, tt = setup(meta, slot, pattern.T, table, packed[0])
    woven = [
        weave(sel, tt, packed[0], begin, size, peers, dirs)
        for begin, size in zip(offsets_of(parts_back), parts_back)
    ]
    x = collect(meta, x, pieces[-2], tuple(spots[-2]), dirs)
    early = comps % 128 == 0 and parts_back[0] <= parts_out[0]
    early = early and all(size * NF % 128 == 0 for size in parts_out)
    if early:
        ahead_pieces = [piece for part in pieces[:-1] for piece in part]
        ahead_spots = tuple(spot for part in spots[:-1] for spot in part)
        partial = begin_couple(meta, woven[0], ahead_pieces, ahead_spots, dirs)
    result = moved
    backs = []
    for g, (begin, size) in enumerate(zip(offsets_of(parts_back), parts_back)):
        after = backs[g - 2][1:] if g >= 2 else renewed[:1] if g else None
        if early and g == 0:
            renewed = end_couple(
                meta, woven[0], partial, pieces[0], pieces[-1], tuple(spots[-1]), size, peers, dirs
            )
            x = collect(meta, x, pieces[-1], tuple(spots[-1]), dirs, tuple(renewed[:1]))
        else:
            renewed, x = couple(
                meta, woven[g], x, pieces[-1], after, tuple(spots[-1]), begin, size, peers, dirs
            )
        back = [renewed[0]] + [
            lax.ppermute(renewed[k], "spec", [(i, i ^ k) for i in range(peers)])
            for k in range(1, peers)
        ]
        backs.append(back)
        result = finish(meta, slot, spread, result, back, begin, size, peers)
    return result


def solution(mesh):
    return jax.shard_map(
        local,
        mesh=mesh,
        in_specs=(
            P("tile", "spec", None),
            P("tile", None),
            P("tile", None),
            P("tile", None),
            P(),
            P(),
        ),
        out_specs=P("tile", "spec", None),
        check_vma=False,
    )
```
